128 devices in a mesh: gx: 16 (over y, z), gy: 8 (over x, core).
Axes of the slice: x: 4, y: 4, z: 4, core: 2. Of those that a mesh axis runs over, the one named last changes fastest.
Arguments:
- raw: bfloat16 [8, 128, 1024], P('gy', None, 'gx'), may hold values from -6 to 6
- section_order: int32 [8], replicated, may hold values from 0 to 7, each once
- margins: int32 [16, 8], replicated, may hold values from 1 to 4, as said below
- w_in: bfloat16 [28, 9], replicated, may hold values from -2 to 2
- b_in: float32 [28], replicated, may hold values from -3 to 3
- w_a: bfloat16 [27, 28, 28], replicated, may hold values from -0.21875 to 0.21875
- b_a: float32 [28], replicated, may hold values from -3 to 3
- w_d: bfloat16 [9, 36, 28], replicated, may hold values from -0.375 to 0.375
- b_d: float32 [36], replicated, may hold values from -3 to 3
- w_u: bfloat16 [28, 36], replicated, may hold values from -1 to 1
- w_o: bfloat16 [3, 28], replicated, may hold values from -1 to 1
- b_o: float32 [3], replicated, may hold values from -3 to 3
Outputs:
- affinities: float32 [3, 8, 128, 1024], P(None, None, 'gx', 'gy')
The draws below stay inside these ranges and needn't reach their ends.
Inputs may be any that keep to these rules, and one draw needn't show every extreme that they name: `section_order`: each section is named once. margins of the groups; one group has margin 4 in every draw.
All inputs are finite; a program needn't handle non-finite values.
Results may differ from the reference program's by a relative error of at most 0.0065.
Values may be sent and summed in bfloat16 or wider, within the bound.
A program may use at most 128 MiB of HBM per device.

```python
import jax
import jax.numpy as jnp
from jax import lax

C0 = 28
C1 = 36
Z = 8
CY = 8
CX = 128
MARGIN = 4
Y = 128
X = 1024
N_GX = 16
N_GY = 8


def draw_margins(key, part):
    key = jax.random.fold_in(key, 5)
    first_key, second_key = jax.random.split(key)
    values = jax.random.randint(first_key, (N_GX * N_GY,), 1, MARGIN + 1)
    where_full = jax.random.randint(second_key, (), 0, N_GX * N_GY)
    values = values.at[where_full].set(MARGIN)
    return values.reshape(N_GX, N_GY).astype(jnp.int32)


def levels(stream_key, dims, pieces, smallest, top_value):
    loudness = 1.0
    for dim, shards_of in pieces:
        draws = jax.random.uniform(jax.random.fold_in(jax.random.fold_in(stream_key, 6), dim), (shards_of,), jnp.float32, smallest / len(pieces), top_value / len(pieces))
        loudness = loudness * jnp.repeat(jnp.exp(draws), dims[dim] // shards_of).reshape((-1,) + (1,) * (len(dims) - 1 - dim))
    return loudness


def bell_draw(own_key, extent, spread, bound, cuts=(), kind=jnp.bfloat16):
    values = jax.random.normal(own_key, extent, jnp.float32) * spread
    if len(cuts) > 0:
        values = levels(own_key, extent, cuts, -0.22, 0.18) * values
    return jnp.clip(values, min=-bound, max=bound).astype(kind)


def setup_inputs(seed: int = 0) -> dict:
    splits = jax.random.split(jax.random.key(seed), 13)
    return {
        "raw": bell_draw(splits[0], (Z, Y, X), 1.0, 6.0, ((0, 8), (2, 16))),
        "section_order": jax.random.permutation(splits[1], Z).astype(jnp.int32),
        "margins": draw_margins(jax.random.fold_in(splits[12], 71), 0),
        "w_in": bell_draw(splits[3], (C0, 9), 9 ** -0.5, 2.0),
        "b_in": bell_draw(splits[4], (C0,), 0.5, 3.0, (), jnp.float32),
        "w_a": bell_draw(splits[5], (27, C0, C0), (27 * C0) ** -0.5, 0.21875),
        "b_a": bell_draw(splits[6], (C0,), 0.5, 3.0, (), jnp.float32),
        "w_d": bell_draw(splits[7], (9, C1, C0), (9 * C0) ** -0.5, 0.375),
        "b_d": bell_draw(splits[8], (C1,), 0.5, 3.0, (), jnp.float32),
        "w_u": bell_draw(splits[9], (C0, C1), C1 ** -0.5, 1.0),
        "w_o": bell_draw(splits[10], (3, C0), C0 ** -0.5, 1.0),
        "b_o": bell_draw(splits[11], (3,), 1.0, 3.0, (), jnp.float32),
    }


def segment_one(padded, w_in, b_in):
    depth, tall, wide = padded.shape
    taps = jnp.stack([padded[:, dy:dy + tall - 2, dx:dx + wide - 2] for dy in range(3) for dx in range(3)])
    total = jnp.einsum("ok,kzyx->ozyx", w_in, taps, preferred_element_type=jnp.float32)
    return jax.nn.relu(total + b_in[:, None, None, None]).astype(jnp.bfloat16)


def network(hidden, w_a, b_a, w_d, b_d, w_u, w_o, b_o):
    chans, depth, tall, wide = hidden.shape
    padded = jnp.pad(hidden, ((0, 0), (1, 1), (1, 1), (1, 1)))
    stacked = jnp.concatenate([padded[:, :, dy:dy + tall, dx:dx + wide] for dy in range(3) for dx in range(3)], axis=0)
    w_planes = jnp.transpose(w_a.reshape(3, 9, chans, chans), (0, 2, 1, 3)).reshape(3, chans, 9 * chans)
    total = jnp.zeros((chans, depth, tall, wide), jnp.float32)
    for dz in range(3):
        total = total + jnp.einsum("ok,kzyx->ozyx", w_planes[dz], stacked[:, dz:dz + depth], preferred_element_type=jnp.float32)
    fine = (hidden.astype(jnp.float32) + jax.nn.relu(total + b_a[:, None, None, None])).astype(jnp.bfloat16)
    pooled = fine.astype(jnp.float32).reshape(chans, depth, tall // 2, 2, wide // 2, 2).mean(axis=(3, 5)).astype(jnp.bfloat16)
    coarse_pad = jnp.pad(pooled, ((0, 0), (0, 0), (1, 1), (1, 1)))
    half_y, half_x = tall // 2, wide // 2
    coarse_cols = jnp.concatenate([coarse_pad[:, :, dy:dy + half_y, dx:dx + half_x] for dy in range(3) for dx in range(3)], axis=0)
    w_coarse = jnp.transpose(w_d, (1, 0, 2)).reshape(w_d.shape[1], 9 * chans)
    coarse = jnp.einsum("ok,kzyx->ozyx", w_coarse, coarse_cols, preferred_element_type=jnp.float32)
    coarse = jax.nn.relu(coarse + b_d[:, None, None, None]).astype(jnp.bfloat16)
    lifted = jnp.einsum("oc,czyx->ozyx", w_u, coarse, preferred_element_type=jnp.float32)
    lifted = jnp.repeat(jnp.repeat(lifted, 2, axis=2), 2, axis=3)
    summed = fine.astype(jnp.float32) + lifted
    logits = jnp.einsum("oc,czyx->ozyx", w_o.astype(jnp.float32), summed, precision=lax.Precision.HIGHEST)
    return jax.nn.sigmoid(logits + b_o[:, None, None, None])


def ramp_weight(offset, core, margin):
    beyond = jnp.maximum(jnp.maximum(-offset, offset - core + 1), 0).astype(jnp.float32)
    return jnp.clip(1.0 - beyond / (margin + 1.0), 0.0, 1.0)


def reference(raw, section_order, margins, w_in, b_in, w_a, b_a, w_d, b_d, w_u, w_o, b_o):
    volume = jnp.zeros(raw.shape, jnp.bfloat16).at[section_order].set(raw)
    first = segment_one(jnp.pad(volume, ((0, 0), (1, 1), (1, 1))), w_in, b_in)
    first_pad = jnp.pad(first, ((0, 0), (0, 0), (MARGIN, MARGIN), (MARGIN, MARGIN)))
    ext_y = CY + 2 * MARGIN
    ext_x = CX + 2 * MARGIN
    start = jnp.zeros((4, Z, Y + 2 * MARGIN, X + 2 * MARGIN), jnp.float32)
    zero = jnp.int32(0)

    def one_group(index, accum):
        row = (index // N_GY).astype(jnp.int32)
        col = (index % N_GY).astype(jnp.int32)
        y_start = (row * CY).astype(jnp.int32)
        x_start = (col * CX).astype(jnp.int32)
        hidden = lax.dynamic_slice(first_pad, (zero, zero, y_start, x_start), (C0, Z, ext_y, ext_x))
        output = network(hidden, w_a, b_a, w_d, b_d, w_u, w_o, b_o)
        margin = margins[row, col].astype(jnp.float32)
        weight_y = ramp_weight(jnp.arange(ext_y, dtype=jnp.int32) - MARGIN, CY, margin)
        weight_x = ramp_weight(jnp.arange(ext_x, dtype=jnp.int32) - MARGIN, CX, margin)
        weight = weight_y[:, None] * weight_x[None, :]
        piece = jnp.concatenate([output * weight, jnp.broadcast_to(weight, (1, Z, ext_y, ext_x))], axis=0)
        here = lax.dynamic_slice(accum, (zero, zero, y_start, x_start), (4, Z, ext_y, ext_x))
        return lax.dynamic_update_slice(accum, here + piece, (zero, zero, y_start, x_start))

    accum = lax.fori_loop(0, N_GX * N_GY, one_group, start)
    inner = accum[:, :, MARGIN:MARGIN + Y, MARGIN:MARGIN + X]
    return inner[:3] / inner[3:4]
```

```python
import functools

import jax
import jax.numpy as jnp
from jax import lax
from jax.experimental import pallas as pl
from jax.experimental.pallas import tpu as pltpu
from jax.sharding import PartitionSpec as P

MESH = pl.DeviceIdType.MESH
F32 = jnp.float32
BF16 = jnp.bfloat16
BIG = -1e30

LEFT_AT = 96
RIGHT_AT = 32 - 127


def iota(shape, dim):
    return lax.broadcasted_iota(jnp.int32, shape, dim)


def within(x, low, high):
    return (x >= low) & (x <= high)


def dot(a, b):
    return jnp.dot(a, b, preferred_element_type=F32)


def neighbours(gi):
    odd = lax.rem(gi, 2)
    column = lax.div(gi, 2)
    beside = lax.rem(column + 7 + 2 * odd, 8)
    return odd, column, beside


def exchange_kernel(raw_ref, got_ref, send_ref, send_sem, recv_sem):
    gi = lax.axis_index("gx")
    gj = lax.axis_index("gy")
    odd, column, beside = neighbours(gi)
    barrier = pltpu.get_barrier_semaphore()

    def greet(n, carry):
        strip = lax.rem(2 * gj + 15 + lax.rem(n, 4), 16)
        slab = lax.div(n, 4)

        @pl.when((strip != gi) | (slab != gj))
        def _():
            pl.semaphore_signal(barrier, inc=1, device_id=(strip, slab), device_id_type=MESH)

        return carry

    lax.fori_loop(0, 32, greet, 0)

    row = iota((256, 128), 0)
    rows = (iota((256, 128), 1) == 8 * (row // 16) - 4 + row % 16).astype(F32).astype(BF16)
    lane = iota((64, 256), 1)
    tile = lane % 128
    even_main = jnp.where(tile < 64, tile, jnp.where(within(tile, 96, 100), tile - LEFT_AT, -1))
    odd_main = jnp.where(tile >= 64, tile - 64, jnp.where(within(tile, 28, 32), tile + 31, -1))
    even_side = jnp.where(tile < 4, tile, jnp.where(within(tile, 33, 36), tile - 33, -1))
    odd_side = jnp.where(tile >= 124, tile - 64, jnp.where(within(tile, 92, 95), tile - 32, -1))
    ends = (gi == 0) | (gi == 15)
    main = jnp.where(odd == 1, odd_main, even_main)
    side = jnp.where(ends, -1, jnp.where(odd == 1, odd_side, even_side))
    cols = (iota((64, 256), 0) == jnp.where(lane < 128, main, side)).astype(F32).astype(BF16)
    picked = dot(rows, raw_ref[0]).astype(BF16)
    message = dot(picked, cols).astype(BF16)
    send_ref[0:16] = message[:, 0:128].reshape(16, 16, 128)
    send_ref[16:32] = message[:, 128:256].reshape(16, 16, 128)

    at_home = (gj == column) | (gj == beside)

    @pl.when(at_home)
    def _():
        pl.semaphore_wait(barrier, 31)

    @pl.when(jnp.logical_not(at_home))
    def _():
        pl.semaphore_wait(barrier, 32)

    def send(n, carry):
        target = lax.rem(gi + n, 16)
        for kind in range(2):
            where_to = column if kind == 0 else beside
            slot = odd if kind == 0 else 3 - odd
            source = send_ref.at[target + 16 * kind]
            place = got_ref.at[slot, gj]
            here = (target == gi) & (where_to == gj)

            @pl.when(here)
            def _():
                pltpu.make_async_copy(source, place, recv_sem).start()

            @pl.when(jnp.logical_not(here))
            def _():
                pltpu.make_async_remote_copy(
                    src_ref=source,
                    dst_ref=place,
                    send_sem=send_sem,
                    recv_sem=recv_sem,
                    device_id=(target, where_to),
                    device_id_type=MESH,
                ).start()

        return carry

    lax.fori_loop(0, 16, send, 0)
    pltpu.make_async_copy(got_ref, got_ref, recv_sem).wait()

    @pl.when(at_home)
    def _():
        pltpu.make_async_copy(send_ref.at[0:31], send_ref.at[0:31], send_sem).wait()

    @pl.when(jnp.logical_not(at_home))
    def _():
        pltpu.make_async_copy(send_ref, send_ref, send_sem).wait()


def exchange(raw):
    return pl.pallas_call(
        exchange_kernel,
        out_shape=jax.ShapeDtypeStruct((4, 8, 16, 128), BF16),
        in_specs=[pl.BlockSpec(memory_space=pltpu.VMEM)],
        out_specs=pl.BlockSpec(memory_space=pl.ANY),
        scratch_shapes=[
            pltpu.VMEM((32, 16, 128), BF16),
            pltpu.SemaphoreType.DMA,
            pltpu.SemaphoreType.DMA,
        ],
        compiler_params=pltpu.CompilerParams(collective_id=0, has_side_effects=True),
    )(raw)


def as_column(row, size):
    shape = (size, row.shape[1])
    return jnp.sum(jnp.where(iota(shape, 0) == iota(shape, 1), row, 0.0), axis=1, keepdims=True)


def split(x):
    high = x.astype(BF16)
    return high, (x - high.astype(F32)).astype(BF16)


def fine_lane(coarse):
    return jnp.where(
        coarse <= 64,
        2 * coarse,
        jnp.where(
            within(coarse, 95, 97),
            2 * coarse + 32,
            jnp.where(within(coarse, 80, 82), 2 * coarse - 3, jnp.where(coarse == 127, 254, -9)),
        ),
    )


def tiled_taps(pad_ref, first, taps, rows, pitch=32):
    tiles = []
    for start in range(0, taps, 128 // pitch):
        tile = None
        for q in range(min(128 // pitch, taps - start)):
            part = pad_ref[first + start + q, 0:rows].astype(F32)
            part = part if q == 0 else pltpu.roll(part, q * pitch, 1)
            tile = part if tile is None else tile + part
        tiles.append(tile)
    return jnp.concatenate(tiles, axis=1)


def network_kernel(
    place,
    order_ref,
    margins_ref,
    b_o_ref,
    got_ref,
    w_in_ref,
    b_in_ref,
    w_a_ref,
    b_a_ref,
    w_d_ref,
    b_d_ref,
    w_u_ref,
    w_o_ref,
    out_ref,
    pad_ref,
    conv_in_ref,
    conv_a_ref,
    conv_d_ref,
    pool_ref,
    spread_ref,
    h_ref,
    a_ref,
    cut_ref,
    d_ref,
    e_ref,
):
    gi, gj = place()

    pad_ref[...] = jnp.zeros_like(pad_ref)
    pad_ref[0:27, 0:28, 0:28] = w_a_ref[...]
    for dz in range(3):
        taps = tiled_taps(pad_ref, 9 * dz, 9, 32)
        lane = iota((32, 384), 1)
        later = pltpu.roll(taps, 96, 1)
        at = 32 * dz
        conv_a_ref[at : at + 32] = jnp.where(lane < 288, later, 0.0).astype(BF16)
        conv_a_ref[96 + at : 128 + at] = taps.astype(BF16)
        conv_a_ref[192 + at : 224 + at] = later.astype(BF16)
        conv_a_ref[288 + at : 320 + at] = jnp.where(lane >= 96, taps, 0.0).astype(BF16)
    pad_ref[0:9, 0:36, 0:28] = w_d_ref[...]
    taps = tiled_taps(pad_ref, 0, 9, 48)
    conv_d_ref[0] = taps.astype(BF16)
    conv_d_ref[1] = pltpu.roll(taps, 384 - 96, 1).astype(BF16)
    bias_a = as_column(b_a_ref[...], 32)
    bias_d = as_column(b_d_ref[...], 48)

    w_in = w_in_ref[...].astype(F32)
    w_in = jnp.concatenate([w_in, jnp.zeros((4, 9), F32)], axis=0)
    lane = iota((32, 128), 1)
    base = jnp.zeros((32, 128), F32)
    for dy in range(3):
        for dx in range(3):
            tap = dy * 3 + dx
            base = base + jnp.where(lane == 16 * dx + dy, w_in[:, tap : tap + 1], 0.0)
    bias = as_column(b_in_ref[...], 32)
    rest = bias
    extra = jnp.where(lane == 51, BIG, 0.0)
    for n in range(3):
        part = rest.astype(BF16).astype(F32)
        extra = extra + jnp.where(lane == 48 + n, part, 0.0)
        rest = rest - part
    for y in range(14):
        taps = extra + (base if y == 0 else pltpu.roll(base, y, 1))
        if y < 3:
            taps = taps + jnp.where(lane == 52, BIG, 0.0)
        if y >= 11:
            taps = taps + jnp.where(lane == 53, BIG, 0.0)
        conv_in_ref[32 * y : 32 * y + 32] = taps.astype(BF16)

    fine = iota((256, 128), 0)
    first = fine_lane(iota((256, 128), 1))
    pool_ref[...] = jnp.where((fine == first) | (fine == first + 1), 0.25, 0.0).astype(BF16)
    fine = iota((128, 256), 1)
    first = fine_lane(iota((128, 256), 0))
    spread = jnp.where((fine == first) | (fine == first + 1), 1.0, 0.0).astype(BF16)
    spread_ref[0:128] = spread
    spread_ref[128:256] = spread

    w_o = w_o_ref[...].astype(F32)
    w_o_rows = jnp.concatenate([jnp.broadcast_to(w_o[o : o + 1], (8, 28)) for o in range(3)], axis=0)
    pad_ref[0] = jnp.zeros((48, 128), BF16)
    pad_ref[0, 0:28, 0:36] = w_u_ref[...]
    w_u = pad_ref[0, 0:32].astype(F32)
    w_u_wide = jnp.concatenate([w_u, jnp.zeros_like(w_u)], axis=1)
    w_u_tiled = w_u_wide
    for n in range(1, 4):
        w_u_tiled = w_u_tiled + pltpu.roll(w_u_wide, 48 * n, 1)
    w_o_pad = jnp.concatenate([w_o_rows, jnp.zeros((24, 4), F32)], axis=1)
    w_q = dot(w_o_pad.astype(BF16), w_u_tiled.astype(BF16))
    y_of = iota((24, 256), 0) % 8
    w_q = jnp.where(iota((24, 256), 1) // 48 == y_of // 2, w_q, 0.0)[:, 0:192]
    w_q_high, w_q_low = split(w_q)
    w_q = jnp.concatenate([w_q_high.astype(F32), w_q_low.astype(F32)], axis=0).astype(BF16)
    w_o_tiled = jnp.concatenate([w_o_pad] * 8, axis=1)
    w_o_diag = jnp.where(iota((24, 256), 1) // 32 == y_of, w_o_tiled, 0.0).astype(BF16)
    row = iota((24, 1), 0)
    bias_o = jnp.where(row < 8, b_o_ref[0], jnp.where(row < 16, b_o_ref[1], b_o_ref[2]))

    def margin(step_y, step_x):
        y, x = gi + step_y, gj + step_x
        inside = (y >= 0) & (y < 16) & (x >= 0) & (x < 8)
        value = margins_ref[jnp.clip(y, 0, 15), jnp.clip(x, 0, 7)]
        return value.astype(F32), jnp.where(inside, 1.0, 0.0)

    def ramp(distance, width):
        return jnp.clip(1.0 - distance / (width + 1.0), 0.0, 1.0)

    y = iota((8, 128), 0)
    lane = iota((8, 128), 1)
    upper = y < 4
    off_y = jnp.where(upper, y + 1, 8 - y).astype(F32)
    leftward = lane >= 64
    from_left = lane - LEFT_AT
    from_right = lane - RIGHT_AT
    is_left = within(from_left, 0, 3)
    is_right = within(from_right, 124, 127)
    off_x = jnp.where(is_left, from_left + 1, jnp.where(is_right, 128 - from_right, 99)).astype(F32)

    def by_place(pairs):
        m = jnp.where(leftward, pairs[0][0], pairs[1][0])
        there = jnp.where(leftward, pairs[0][1], pairs[1][1])
        return m, there

    m_up, in_up = margin(-1, 0)
    m_down, in_down = margin(1, 0)
    weight_y = ramp(off_y, jnp.where(upper, m_up, m_down)) * jnp.where(upper, in_up, in_down)
    m, there = by_place((margin(0, -1), margin(0, 1)))
    weight_x = ramp(off_x, m) * there
    m_top, there_top = by_place((margin(-1, -1), margin(-1, 1)))
    m_low, there_low = by_place((margin(1, -1), margin(1, 1)))
    m = jnp.where(upper, m_top, m_low)
    weight_xy = ramp(off_y, m) * ramp(off_x, m) * jnp.where(upper, there_top, there_low)

    def fold(core, beyond):
        left = jnp.where(lane < 4, pltpu.roll(beyond, 128 - LEFT_AT, 1), 0.0)
        right = jnp.where(lane >= 124, pltpu.roll(beyond, 95, 1), 0.0)
        return core + left + right

    scale = 1.0 / fold(1.0 + weight_y, weight_x + weight_xy)

    column = iota((16, 256), 1)
    kind = iota((16, 256), 0)
    outside = (
        (column == 128 + 100)
        | (column == 128 + 28)
        | (within(column, 252, 255) & (gj == 0))
        | (within(column, 128, 131) & (gj == 7))
    )
    flags = jnp.where(kind < 3, 1.0, 0.0)
    flags = jnp.where((kind == 3) & outside, 1.0, flags)
    flags = jnp.where((kind == 4) & (gi == 0), 1.0, flags)
    flags = jnp.where((kind == 5) & (gi == 15), 1.0, flags)
    tile = iota((16, 128), 1)

    def first_level(z, carry):
        slab = jnp.int32(0)
        for k in range(8):
            slab = slab + jnp.where(order_ref[k] == z, k, 0)
        near, far, before, after = [got_ref[n, slab].astype(F32) for n in range(4)]
        core = jnp.where(tile < 64, near, far)
        low = jnp.where(within(tile, 28, 32), far, after)
        high = jnp.where(within(tile, 96, 100), near, before)
        raw = jnp.concatenate([core, jnp.where(tile < 64, low, high)], axis=1)
        taps = jnp.concatenate([pltpu.roll(raw, 1, 1), raw, pltpu.roll(raw, 255, 1), flags], axis=0)
        h = jnp.maximum(dot(conv_in_ref[:, 0:64], taps.astype(BF16)), 0.0)
        h_ref[z, :, 32:64] = h.astype(BF16).reshape(14, 32, 256)
        h_ref[z, :, 0:32] = pltpu.roll(h, 1, 1).astype(BF16).reshape(14, 32, 256)
        h_ref[z, :, 64:96] = pltpu.roll(h, 255, 1).astype(BF16).reshape(14, 32, 256)
        return carry

    lax.fori_loop(0, 8, first_level, 0)

    def residual(pair, top, count):
        parts = []

        def finish(z):
            total = parts[z][:, 1]
            if z > 0:
                total = total + parts[z - 1][:, 0]
            if z < 7:
                total = total + parts[z + 1][:, 2]
            total = jnp.maximum(total + bias_a, 0.0)
            for n in range(count):
                which = top // 96 + n
                step = (1, 0, 1, 0)[which]
                centre = h_ref[z, 2 * pair + 1 + step, 32:64].astype(F32)
                value = (centre + total[n]).astype(BF16)
                if which in (1, 2):
                    a_ref[z, 2 * pair + step] = value
                else:
                    cut_ref[z, which // 3] = value

        for z in range(8):
            rows = h_ref[z, pl.ds(2 * pair, 4)].reshape(384, 256)
            product = dot(conv_a_ref[top : top + 96 * count], rows)
            parts.append(product.reshape(count, 3, 32, 256))
            if z > 0:
                finish(z - 1)
        finish(7)

    def plain(n, carry):
        residual(n + 2 * lax.div(n, 2), 96, 2)
        return carry

    lax.fori_loop(0, 4, plain, 0)
    residual(2, 0, 3)
    residual(3, 96, 3)

    def pooling(z, carry):
        a = a_ref[z].reshape(6, 2, 32, 256)
        even = jnp.concatenate([a[:, 0].reshape(192, 256), a_ref[z, 4], cut_ref[z, 1]], axis=0)
        late = jnp.concatenate([a[:, 1].reshape(192, 256), cut_ref[z, 0], a_ref[z, 7]], axis=0)
        d = (dot(even, pool_ref[...]) + dot(late, pool_ref[...])).reshape(8, 32, 128)
        pair, half = z // 2, z % 2
        for dx in range(3):
            moved = d if dx == 1 else pltpu.roll(d, 1 if dx == 0 else 127, 2)
            moved = moved.astype(BF16)
            blocks = jnp.concatenate(
                [moved[0:2], moved[6:7], moved[0:6], moved[7:8], moved[4:6]], axis=0
            )
            d_ref[pair, :, 32 * dx : 32 * dx + 32, 128 * half : 128 * half + 128] = blocks
        return carry

    for z in range(8):
        pooling(z, 0)

    def coarse(pair, carry):
        for n, (start, count, late) in enumerate(
            [(3, 3, 0), (4, 3, 0), (5, 3, 0), (6, 3, 0), (0, 3, 0), (1, 2, 0), (9, 2, 1), (9, 3, 0)]
        ):
            rows = d_ref[pair, start : start + count].reshape(96 * count, 256)
            e = dot(conv_d_ref[late, :, 0 : 96 * count], rows)
            e = jnp.maximum(e + bias_d, 0.0).astype(BF16)
            e_ref[pair, n // 4, 48 * (n % 4) : 48 * (n % 4) + 48] = e
        return carry

    lax.fori_loop(0, 4, coarse, 0)

    def head(pair, carry):
        lifted = []
        for kind in range(2):
            q = dot(w_q, e_ref[pair, kind])
            lifted.append(q[0:24] + q[24:48])
        q = jnp.concatenate(lifted, axis=0)
        high = q.astype(BF16).astype(F32)
        low = q - high
        for half in range(2):
            z = 2 * pair + half
            at = slice(128 * half, 128 * half + 128)
            both = jnp.concatenate([high[:, at], low[:, at]], axis=1).astype(BF16)
            up = dot(both, spread_ref[...])
            own = a_ref[z, 2:10].reshape(256, 256)
            other = jnp.concatenate(
                [
                    a_ref[z, 2:5].reshape(96, 256),
                    cut_ref[z].reshape(64, 256),
                    a_ref[z, 7:10].reshape(96, 256),
                ],
                axis=0,
            )
            own = jax.nn.sigmoid(dot(w_o_diag, own) + up[0:24] + bias_o)
            other = jax.nn.sigmoid(dot(w_o_diag, other) + up[24:48] + bias_o)
            for o in range(3):
                s, t = own[8 * o : 8 * o + 8], other[8 * o : 8 * o + 8]
                core = s[:, 0:128] + t[:, 0:128] * weight_y
                beyond = s[:, 128:256] * weight_x + t[:, 128:256] * weight_xy
                out_ref[o, z] = fold(core, beyond) * scale
        return carry

    lax.fori_loop(0, 4, head, 0)


def network(place, order, margins, b_o, got, w_in, b_in, w_a, b_a, w_d, b_d, w_u, w_o, **options):
    smem = pl.BlockSpec(memory_space=pltpu.SMEM)
    vmem = pl.BlockSpec(memory_space=pltpu.VMEM)
    return pl.pallas_call(
        functools.partial(network_kernel, place),
        out_shape=jax.ShapeDtypeStruct((3, 8, 8, 128), F32),
        in_specs=[smem] * 3 + [vmem] * 9,
        out_specs=vmem,
        scratch_shapes=[
            pltpu.VMEM((27, 48, 128), BF16),
            pltpu.VMEM((448, 128), BF16),
            pltpu.VMEM((384, 384), BF16),
            pltpu.VMEM((2, 48, 384), BF16),
            pltpu.VMEM((256, 128), BF16),
            pltpu.VMEM((256, 256), BF16),
            pltpu.VMEM((8, 14, 96, 256), BF16),
            pltpu.VMEM((8, 12, 32, 256), BF16),
            pltpu.VMEM((8, 2, 32, 256), BF16),
            pltpu.VMEM((4, 12, 96, 256), BF16),
            pltpu.VMEM((4, 2, 192, 256), BF16),
        ],
        compiler_params=pltpu.CompilerParams(vmem_limit_bytes=48 * 1024 * 1024),
        **options,
    )(order, margins, b_o, got, w_in, b_in[None], w_a, b_a[None], w_d, b_d[None], w_u, w_o)


def whereabouts():
    return lax.axis_index("gx"), lax.axis_index("gy")


def per_device(raw, section_order, margins, w_in, b_in, w_a, b_a, w_d, b_d, w_u, w_o, b_o):
    got = exchange(raw)
    return network(
        whereabouts, section_order, margins, b_o, got, w_in, b_in, w_a, b_a, w_d, b_d, w_u, w_o
    )


def solution(mesh):
    placed = (P("gy", None, "gx"), P(), P(), P(), P(), P(), P(), P(), P(), P(), P(), P())
    return jax.shard_map(
        per_device, mesh=mesh, in_specs=placed, out_specs=P(None, None, "gx", "gy"), check_vma=False
    )
```

```python
import functools

import jax
import jax.numpy as jnp
import ml_dtypes
import numpy as np
from jax import lax
from jax.experimental import pallas as pl
from jax.experimental.pallas import tpu as pltpu
from jax.sharding import PartitionSpec as P

MESH = pl.DeviceIdType.MESH
F32 = jnp.float32
BF16 = jnp.bfloat16
BIG = -1e30


def iota(shape, dim):
    return lax.broadcasted_iota(jnp.int32, shape, dim)


def within(x, low, high):
    return (x >= low) & (x <= high)


def dot(a, b):
    return jnp.dot(a, b, preferred_element_type=F32)


def neighbours(gi):
    odd = lax.rem(gi, 2)
    column = lax.div(gi, 2)
    beside = lax.rem(column + 7 + 2 * odd, 8)
    return odd, column, beside


def exchange_kernel(raw_ref, got_ref, send_ref, send_sem, recv_sem):
    gi = lax.axis_index("gx")
    gj = lax.axis_index("gy")
    odd, column, beside = neighbours(gi)
    barrier = pltpu.get_barrier_semaphore()

    def greet(n, carry):
        strip = lax.rem(2 * gj + 15 + lax.rem(n, 4), 16)
        slab = lax.div(n, 4)

        @pl.when((strip != gi) | (slab != gj))
        def _():
            pl.semaphore_signal(barrier, inc=1, device_id=(strip, slab), device_id_type=MESH)

        return carry

    lax.fori_loop(0, 32, greet, 0)

    row = iota((256, 128), 0)
    rows = (iota((256, 128), 1) == 8 * (row // 16) - 4 + row % 16).astype(F32).astype(BF16)
    lane = iota((64, 256), 1)
    tile = lane % 128
    even_main = jnp.where(tile < 64, tile, jnp.where(tile >= 122, tile - 122, -1))
    odd_main = jnp.where(tile >= 64, tile - 64, jnp.where(tile < 6, tile + 58, -1))
    even_side = jnp.where(within(tile, 6, 9), tile - 6, -1)
    odd_side = jnp.where(within(tile, 118, 121), tile - 58, -1)
    ends = (gi == 0) | (gi == 15)
    main = jnp.where(odd == 1, odd_main, even_main)
    side = jnp.where(ends, -1, jnp.where(odd == 1, odd_side, even_side))
    cols = (iota((64, 256), 0) == jnp.where(lane < 128, main, side)).astype(F32).astype(BF16)
    picked = lax.dot_general(
        rows, raw_ref[0], (((1,), (1,)), ((), ())), preferred_element_type=F32
    ).astype(BF16)
    message = dot(picked, cols).astype(BF16)
    send_ref[0:16] = message[:, 0:128].reshape(16, 16, 128)
    send_ref[16:32] = message[:, 128:256].reshape(16, 16, 128)

    at_home = (gj == column) | (gj == beside)

    @pl.when(at_home)
    def _():
        pl.semaphore_wait(barrier, 31)

    @pl.when(jnp.logical_not(at_home))
    def _():
        pl.semaphore_wait(barrier, 32)

    def send(n, carry):
        target = lax.rem(gi + n, 16)
        for kind in range(2):
            where_to = column if kind == 0 else beside
            slot = odd if kind == 0 else 3 - odd
            source = send_ref.at[target + 16 * kind]
            place = got_ref.at[slot, gj]
            here = (target == gi) & (where_to == gj)

            @pl.when(here)
            def _():
                pltpu.make_async_copy(source, place, recv_sem).start()

            @pl.when(jnp.logical_not(here))
            def _():
                pltpu.make_async_remote_copy(
                    src_ref=source,
                    dst_ref=place,
                    send_sem=send_sem,
                    recv_sem=recv_sem,
                    device_id=(target, where_to),
                    device_id_type=MESH,
                ).start()

        return carry

    lax.fori_loop(0, 16, send, 0)
    pltpu.make_async_copy(got_ref, got_ref, recv_sem).wait()

    @pl.when(at_home)
    def _():
        pltpu.make_async_copy(send_ref.at[0:31], send_ref.at[0:31], send_sem).wait()

    @pl.when(jnp.logical_not(at_home))
    def _():
        pltpu.make_async_copy(send_ref, send_ref, send_sem).wait()


def exchange(raw):
    return pl.pallas_call(
        exchange_kernel,
        out_shape=jax.ShapeDtypeStruct((4, 8, 16, 128), BF16),
        in_specs=[pl.BlockSpec(memory_space=pltpu.VMEM)],
        out_specs=pl.BlockSpec(memory_space=pl.ANY),
        scratch_shapes=[
            pltpu.VMEM((32, 16, 128), BF16),
            pltpu.SemaphoreType.DMA,
            pltpu.SemaphoreType.DMA,
        ],
        compiler_params=pltpu.CompilerParams(collective_id=0, has_side_effects=True),
    )(jnp.transpose(raw, (0, 2, 1)))


def tiled_taps(pad_ref, first, taps):
    tiles = []
    for start in range(0, taps, 4):
        tile = None
        for q in range(min(4, taps - start)):
            part = pad_ref[first + start + q].astype(F32)
            part = part if q == 0 else pltpu.roll(part, 32 * q, 1)
            tile = part if tile is None else tile + part
        tiles.append(tile)
    return jnp.concatenate(tiles, axis=1)


def as_column(row, size):
    shape = (size, row.shape[1])
    return jnp.sum(jnp.where(iota(shape, 0) == iota(shape, 1), row, 0.0), axis=1, keepdims=True)


def split(x):
    high = x.astype(BF16)
    return high, (x - high.astype(F32)).astype(BF16)


def pooling_table():
    core = np.zeros((2, 128, 3, 128), np.float32)
    side = np.zeros((128, 5, 3, 128), np.float32)

    def add(pair, dx, lane, section, coarse, left, right):
        for fine in (2 * coarse, 2 * coarse + 1):
            if left and -2 <= fine <= 3:
                side[16 * section + fine + 2, pair, dx, lane] = 0.25
            elif right and 124 <= fine <= 129:
                side[16 * section + 10 + fine - 124, pair, dx, lane] = 0.25
            elif not left and not right:
                core[section % 2, fine, dx, lane] = 0.25

    for section in range(8):
        for dx in range(3):
            for m in range(64):
                at = m + dx - 1
                add(section // 2, dx, 64 * (section % 2) + m, section, at, at < 0, at > 63)
            for n, m in enumerate((0, 1, 62, 63)):
                add(4, dx, 4 * section + n, section, m + dx - 1, n < 2, n >= 2)
    core = np.concatenate([np.concatenate([core[n], core[n]]) for n in range(2)]).reshape(512, 384)
    side = np.concatenate([side, side]).reshape(256, 5 * 384)
    return core.astype(ml_dtypes.bfloat16), side.astype(ml_dtypes.bfloat16)


def network_kernel(
    place,
    order_ref,
    margins_ref,
    b_o_ref,
    got_ref,
    w_in_ref,
    b_in_ref,
    w_a_ref,
    b_a_ref,
    w_d_ref,
    b_d_ref,
    w_u_ref,
    w_o_ref,
    pool_core_ref,
    pool_side_ref,
    out_ref,
    pad_ref,
    conv_in_ref,
    conv_a_ref,
    conv_d_ref,
    raw_ref,
    h_ref,
    a_ref,
    d_ref,
    e_ref,
):
    gi, gj = place()

    pad_ref[...] = jnp.zeros_like(pad_ref)
    pad_ref[0:27, 0:28, 0:28] = w_a_ref[...]
    lane = iota((32, 512), 1)
    for dz in range(3):
        taps = tiled_taps(pad_ref, 9 * dz, 9)
        taps = jnp.concatenate([taps, jnp.zeros((32, 128), F32)], axis=1)
        for n in range(5):
            moved = taps if n in (1, 4) else pltpu.roll(taps, 96 if n == 2 else 192, 1)
            if n == 0:
                moved = jnp.where(lane < 384, moved, 0.0)
            if n == 4:
                moved = jnp.where(lane >= 96, moved, 0.0)
            conv_a_ref[96 * n + 32 * dz : 96 * n + 32 * dz + 32] = moved.astype(BF16)
    pad_ref[0:9] = jnp.zeros((9, 32, 128), BF16)
    pad_ref[0:9, 0:28, 0:36] = w_d_ref[...]
    taps = pad_ref[0:12].astype(F32).reshape(384, 128)
    taps = jnp.where(iota((384, 128), 0) < 288, taps, 0.0)
    taps = jnp.concatenate([taps[128 * n : 128 * n + 128].T[0:40] for n in range(3)], axis=1)
    taps = jnp.concatenate([taps, jnp.zeros((40, 384), F32)], axis=1)
    lane = iota((40, 768), 1)
    for n in range(8):
        if n < 4:
            moved = taps if n == 0 else pltpu.roll(taps, 96 * n, 1)
        elif n == 4:
            moved = jnp.where(lane < 192, taps, 0.0) + jnp.where(
                lane >= 576, pltpu.roll(taps, 384, 1), 0.0
            )
        elif n == 5:
            moved = jnp.where(within(lane, 96, 191), pltpu.roll(taps, 96, 1), 0.0) + jnp.where(
                within(lane, 576, 671), pltpu.roll(taps, 480, 1), 0.0
            )
        elif n == 6:
            moved = jnp.where(within(lane, 384, 479), pltpu.roll(taps, 192, 1), 0.0) + jnp.where(
                lane >= 672, pltpu.roll(taps, 576, 1), 0.0
            )
        else:
            moved = jnp.where(within(lane, 384, 575), pltpu.roll(taps, 288, 1), 0.0) + jnp.where(
                lane >= 672, pltpu.roll(taps, 672, 1), 0.0
            )
        conv_d_ref[40 * n : 40 * n + 40] = moved
    bias_a = as_column(b_a_ref[...], 32)
    bias_d = jnp.concatenate([as_column(b_d_ref[...], 40)] * 8, axis=0)

    pad_ref[0] = jnp.zeros((32, 128), BF16)
    pad_ref[0, 0:9, 0:28] = w_in_ref[...]
    tap = iota((32, 128), 0)
    lane = iota((32, 128), 1)
    put = (lane == 16 * (tap % 3) + tap // 3) & (tap < 9)
    base = lax.dot_general(
        pad_ref[0],
        put.astype(F32).astype(BF16),
        (((0,), (0,)), ((), ())),
        preferred_element_type=F32,
    )[0:32]
    bias = as_column(b_in_ref[...], 32)
    rest = bias
    extra = jnp.where(lane == 51, BIG, 0.0)
    for n in range(3):
        part = rest.astype(BF16).astype(F32)
        extra = extra + jnp.where(lane == 48 + n, part, 0.0)
        rest = rest - part
    for y in range(14):
        taps = extra + (base if y == 0 else pltpu.roll(base, y, 1))
        if y < 3:
            taps = taps + jnp.where(lane == 52, BIG, 0.0)
        if y >= 11:
            taps = taps + jnp.where(lane == 53, BIG, 0.0)
        conv_in_ref[32 * y : 32 * y + 32] = taps.astype(BF16)

    w_o = w_o_ref[...].astype(F32)
    w_o = jnp.concatenate([jnp.broadcast_to(w_o[o : o + 1], (8, 28)) for o in range(3)], axis=0)
    w_o = jnp.concatenate([w_o, jnp.zeros((24, 4), F32)], axis=1)
    pad_ref[0] = jnp.zeros((32, 128), BF16)
    pad_ref[0, 0:28, 0:36] = w_u_ref[...]
    w_u = pad_ref[0].astype(F32)
    w_u = jnp.concatenate([w_u, jnp.zeros_like(w_u)], axis=1)
    w_u = w_u + pltpu.roll(w_u, 40, 1)
    w_u = w_u + pltpu.roll(w_u, 80, 1)
    w_q = dot(w_o.astype(BF16), w_u.astype(BF16))
    lane = iota((24, 256), 1)
    w_q = jnp.where(lane // 40 == (iota((24, 256), 0) % 8) // 2, w_q, 0.0)[:, 0:160]
    w_q_high, w_q_low = split(w_q)
    w_q = jnp.concatenate([w_q_high.astype(F32), w_q_low.astype(F32)], axis=0).astype(BF16)
    w_o = jnp.concatenate([w_o] * 12, axis=1)
    w_o = jnp.concatenate([w_o, w_o], axis=0)
    lane = iota((48, 384), 1) // 32
    row = iota((48, 384), 0)
    block = jnp.where(row < 24, row % 8, jnp.where(within(row % 8, 3, 4), row % 8 + 5, row % 8))
    w_o = jnp.where(lane == block, w_o, 0.0).astype(BF16)[:, 0:320]
    row = iota((48, 1), 0) % 24
    bias_o = jnp.where(row < 8, b_o_ref[0], jnp.where(row < 16, b_o_ref[1], b_o_ref[2]))

    row = iota((256, 256), 0) % 128
    spread = (row == iota((256, 256), 1) // 2).astype(F32).astype(BF16)
    row = iota((256, 128), 0) % 128
    lane = iota((256, 128), 1)
    which = jnp.where(
        within(lane % 16, 2, 5), lane % 16 // 2 - 1, jnp.where(within(lane % 16, 10, 13), lane % 16 // 2 - 3, -999)
    )
    spread_side = (row == 4 * (lane // 16) + which).astype(F32).astype(BF16)

    def margin(step_y, step_x):
        y, x = gi + step_y, gj + step_x
        inside = (y >= 0) & (y < 16) & (x >= 0) & (x < 8)
        value = margins_ref[jnp.clip(x, 0, 7), jnp.clip(y, 0, 15)]
        return value.astype(F32), jnp.where(inside, 1.0, 0.0)

    def ramp(distance, width):
        return jnp.clip(1.0 - distance / (width + 1.0), 0.0, 1.0)

    y = iota((8, 128), 0)
    lane = iota((8, 128), 1)
    upper = y < 4
    off_y = jnp.where(upper, y + 1, 8 - y).astype(F32)
    nth = lane % 16
    leftward = nth < 8
    off_x = jnp.where(
        within(nth, 2, 5), nth - 1, jnp.where(within(nth, 10, 13), 14 - nth, 99)
    ).astype(F32)

    def by_place(pairs):
        m = jnp.where(leftward, pairs[0][0], pairs[1][0])
        there = jnp.where(leftward, pairs[0][1], pairs[1][1])
        return m, there

    m_up, in_up = margin(-1, 0)
    m_down, in_down = margin(1, 0)
    weight_y = ramp(off_y, jnp.where(upper, m_up, m_down)) * jnp.where(upper, in_up, in_down)
    m, there = by_place((margin(0, -1), margin(0, 1)))
    weight_x = ramp(off_x, m) * there
    m_top, there_top = by_place((margin(-1, -1), margin(-1, 1)))
    m_low, there_low = by_place((margin(1, -1), margin(1, 1)))
    m = jnp.where(upper, m_top, m_low)
    weight_xy = ramp(off_y, m) * ramp(off_x, m) * jnp.where(upper, there_top, there_low)

    def fold(core, beyond, z):
        left = jnp.where(lane < 4, pltpu.roll(beyond, (126 - 16 * z) % 128, 1), 0.0)
        right = jnp.where(lane >= 124, pltpu.roll(beyond, (114 - 16 * z) % 128, 1), 0.0)
        return core + left + right

    scale = 1.0 / fold(1.0 + weight_y, weight_x + weight_xy, 0)

    tile = iota((16, 128), 1)
    sides = [jnp.zeros((16, 128), F32) for _ in range(5)]
    for z in range(8):
        slab = jnp.int32(0)
        for k in range(8):
            slab = slab + jnp.where(order_ref[k] == z, k, 0)
        near, far, before, after = [got_ref[n, slab].astype(F32) for n in range(4)]
        core = jnp.where(tile < 64, near, far)
        low = jnp.where(tile < 6, far, after)
        high = jnp.where(tile >= 122, near, before)
        beside = jnp.where(tile < 64, low, high)
        for n in range(5):
            s = n - 2
            moved = core if s == 0 else pltpu.roll(core, -s % 128, 1)
            if s > 0:
                moved = jnp.where(tile >= 128 - s, pltpu.roll(beside, 122 - s, 1), moved)
            if s < 0:
                moved = jnp.where(tile < -s, pltpu.roll(beside, 6 - s, 1), moved)
            raw_ref[16 * n : 16 * n + 16, 128 * z : 128 * z + 128] = moved.astype(BF16)
            moved = pltpu.roll(beside, (16 * z + 8 - s) % 128, 1)
            sides[n] = jnp.where(tile // 16 == z, moved, sides[n])
    for n in range(5):
        raw_ref[16 * n : 16 * n + 16, 1024:1152] = sides[n].astype(BF16)

    def flags(dx, side):
        kind = iota((16, 128), 0)
        nth = tile % 16
        if side:
            column = jnp.where(nth < 8, nth - 3 + dx, 113 + nth + dx)
            cut = jnp.where(nth < 8, 4, 123)
            outside = column == cut
        else:
            column = tile + dx - 1
            outside = tile < 0
        outside = outside | ((column < 0) & (gj == 0)) | ((column > 127) & (gj == 7))
        value = jnp.where(kind < 3, 1.0, 0.0)
        value = jnp.where((kind == 3) & outside, 1.0, value)
        value = jnp.where((kind == 4) & (gi == 0), 1.0, value)
        return jnp.where((kind == 5) & (gi == 15), 1.0, value).astype(BF16)

    for dx in range(3):
        flag = flags(dx, False)
        flag = jnp.concatenate([flag, flag], axis=1)
        for q in range(5):
            at = slice(256 * q, 256 * q + 256) if q < 4 else slice(1024, 1152)
            taps = jnp.concatenate(
                [raw_ref[16 * dx : 16 * dx + 48, at], flag if q < 4 else flags(dx, True)], axis=0
            )
            h = jnp.maximum(dot(conv_in_ref[:, 0:64], taps).astype(BF16), 0)
            h_ref[:, dx, :, at] = h.reshape(14, 32, h.shape[1])

    def residual(three):
        extra = three in (1, 2)
        first = 0 if three == 1 else 1
        names = [None, 3 * three, 3 * three + 1, 3 * three + 2, None]
        names[0], names[4] = 10, 11
        names = [n if n < 10 or k in (0, 4) else n + 2 for k, n in enumerate(names)]
        count = 4 if extra else 3
        lane = iota((count, 32, 128), 2)

        def finish(total, at):
            total = jnp.maximum(total + bias_a, 0.0)
            for n in range(count):
                which = first + n
                step = (2, 0, 1, 2, 0)[which]
                centre = h_ref[3 * three + 1 + step, 1, :, at].astype(F32)
                a_ref[names[which], :, at] = (centre + total[n]).astype(BF16)

        parts = []
        for q in range(5):
            at = slice(256 * q, 256 * q + 256) if q < 4 else slice(1024, 1152)
            rows = h_ref[3 * three : 3 * three + 5, :, :, at].reshape(480, at.stop - at.start)
            product = dot(conv_a_ref[96 * first : 96 * (first + count), 0:480], rows)
            product = product.reshape(count, 3, 32, at.stop - at.start)
            if q == 4:
                total = product[:, 1]
                total = total + jnp.where(lane >= 16, pltpu.roll(product[:, 0], 16, 2), 0.0)
                total = total + jnp.where(lane < 112, pltpu.roll(product[:, 2], 112, 2), 0.0)
                finish(total, at)
                break
            for half in range(2):
                parts.append(product[:, :, :, 128 * half : 128 * half + 128])
                z = len(parts) - 2
                if z >= 0:
                    total = parts[z][:, 1] + parts[z + 1][:, 2]
                    if z > 0:
                        total = total + parts[z - 1][:, 0]
                    finish(total, slice(128 * z, 128 * z + 128))
        finish(parts[7][:, 1] + parts[6][:, 0], slice(896, 1024))

    for three in range(4):
        residual(three)

    def pooled_rows(at):
        even = jnp.concatenate([a_ref[n, :, at] for n in (0, 2, 4, 6, 8, 12, 4, 11)], axis=0)
        late = jnp.concatenate([a_ref[n, :, at] for n in (1, 3, 5, 7, 9, 13, 10, 7)], axis=0)
        return jnp.concatenate([even, late], axis=1)

    side = pooled_rows(slice(1024, 1152))
    for q in range(5):
        d = dot(side, pool_side_ref[:, 384 * q : 384 * q + 384])
        if q < 4:
            for half in range(2):
                z = 2 * q + half
                core = pooled_rows(slice(128 * z, 128 * z + 128))
                d = d + dot(core, pool_core_ref[256 * half : 256 * half + 256])
        for dx in range(3):
            part = d[:, 128 * dx : 128 * dx + 128].astype(BF16)
            d_ref[:, dx, :, 128 * q : 128 * q + 128] = part.reshape(8, 32, 128)

    conv_d = conv_d_ref[...].astype(BF16)
    for at in (slice(0, 256), slice(256, 512), slice(512, 640)):
        e = dot(conv_d, d_ref[:, :, :, at].reshape(768, at.stop - at.start))
        e_ref[:, at] = jnp.maximum(e + bias_d, 0.0).astype(BF16)

    lifted = []
    for kind in range(2):
        q = dot(w_q, e_ref[160 * kind : 160 * kind + 160])
        lifted.append(q[0:24] + q[24:48])
    q = jnp.concatenate(lifted, axis=0)
    high = q.astype(BF16).astype(F32)
    low = q - high

    def both(n):
        at = slice(128 * n, 128 * n + 128)
        return jnp.concatenate([high[:, at], low[:, at]], axis=1).astype(BF16)

    def logits(at):
        return dot(w_o, a_ref[2:12, :, at].reshape(320, at.stop - at.start)) + bias_o

    at = slice(1024, 1152)
    beyond = jax.nn.sigmoid(logits(at) + dot(both(4), spread_side))
    beyond = [
        beyond[8 * o : 8 * o + 8] * weight_x + beyond[24 + 8 * o : 32 + 8 * o] * weight_xy
        for o in range(3)
    ]
    up = dot(jnp.concatenate([both(n) for n in range(4)], axis=0), spread)
    for n in range(4):
        at = slice(256 * n, 256 * n + 256)
        s = jax.nn.sigmoid(logits(at) + up[48 * n : 48 * n + 48])
        for half in range(2):
            z = 2 * n + half
            for o in range(3):
                own = s[8 * o : 8 * o + 8, 128 * half : 128 * half + 128]
                other = s[24 + 8 * o : 32 + 8 * o, 128 * half : 128 * half + 128]
                out_ref[o, z] = fold(own + other * weight_y, beyond[o], z) * scale


def network(place, order, margins, b_o, got, w_in, b_in, w_a, b_a, w_d, b_d, w_u, w_o, **options):
    smem = pl.BlockSpec(memory_space=pltpu.SMEM)
    vmem = pl.BlockSpec(memory_space=pltpu.VMEM)
    return pl.pallas_call(
        functools.partial(network_kernel, place),
        out_shape=jax.ShapeDtypeStruct((3, 8, 8, 128), F32),
        in_specs=[smem] * 3 + [vmem] * 11,
        out_specs=vmem,
        scratch_shapes=[
            pltpu.VMEM((27, 32, 128), BF16),
            pltpu.VMEM((448, 128), BF16),
            pltpu.VMEM((480, 512), BF16),
            pltpu.VMEM((320, 768), F32),
            pltpu.VMEM((80, 1152), BF16),
            pltpu.VMEM((14, 3, 32, 1152), BF16),
            pltpu.VMEM((14, 32, 1152), BF16),
            pltpu.VMEM((8, 3, 32, 640), BF16),
            pltpu.VMEM((320, 640), BF16),
        ],
        compiler_params=pltpu.CompilerParams(vmem_limit_bytes=48 * 1024 * 1024),
        **options,
    )(
        order,
        margins.T,
        b_o,
        got,
        w_in.T,
        b_in[None],
        w_a,
        b_a[None],
        jnp.transpose(w_d, (0, 2, 1)),
        b_d[None],
        w_u,
        w_o,
        *pooling_table(),
    )


def whereabouts():
    return lax.axis_index("gx"), lax.axis_index("gy")


def per_device(raw, section_order, margins, w_in, b_in, w_a, b_a, w_d, b_d, w_u, w_o, b_o):
    got = exchange(raw)
    return network(
        whereabouts, section_order, margins, b_o, got, w_in, b_in, w_a, b_a, w_d, b_d, w_u, w_o
    )


def solution(mesh):
    placed = (P("gy", None, "gx"), P(), P(), P(), P(), P(), P(), P(), P(), P(), P(), P())
    return jax.shard_map(
        per_device, mesh=mesh, in_specs=placed, out_specs=P(None, None, "gx", "gy"), check_vma=False
    )
```

```python
import functools

import jax
import jax.numpy as jnp
import ml_dtypes
import numpy as np
from jax import lax
from jax.experimental import pallas as pl
from jax.experimental.pallas import tpu as pltpu
from jax.sharding import PartitionSpec as P

MESH = pl.DeviceIdType.MESH
F32 = jnp.float32
BF16 = jnp.bfloat16
BIG = -1e30


def iota(shape, dim):
    return lax.broadcasted_iota(jnp.int32, shape, dim)


def within(x, low, high):
    return (x >= low) & (x <= high)


def dot(a, b):
    return jnp.dot(a, b, preferred_element_type=F32)


def neighbours(gi):
    odd = lax.rem(gi, 2)
    column = lax.div(gi, 2)
    beside = lax.rem(column + 7 + 2 * odd, 8)
    return odd, column, beside


def as_column(row, size):
    shape = (size, row.shape[1])
    return jnp.sum(jnp.where(iota(shape, 0) == iota(shape, 1), row, 0.0), axis=1, keepdims=True)


def tiled_taps(pad_ref, first, taps):
    tiles = []
    for start in range(0, taps, 4):
        tile = None
        for q in range(min(4, taps - start)):
            part = pad_ref[first + start + q].astype(F32)
            part = part if q == 0 else pltpu.roll(part, 32 * q, 1)
            tile = part if tile is None else tile + part
        tiles.append(tile)
    return jnp.concatenate(tiles, axis=1)


def prepare(
    pad_ref,
    w_in_ref,
    b_in_ref,
    w_a_ref,
    b_a_ref,
    w_d_ref,
    b_d_ref,
    w_u_ref,
    w_o_ref,
    b_o_ref,
    conv_in_ref,
    conv_a_ref,
    conv_d_ref,
    w_q_ref,
    w_s_ref,
    bias_ref,
):
    pad_ref[...] = jnp.zeros_like(pad_ref)
    pad_ref[0:27, 0:28, 0:28] = w_a_ref[...]
    lane = iota((32, 512), 1)
    for dz in range(3):
        taps = tiled_taps(pad_ref, 9 * dz, 9)
        taps = jnp.concatenate([taps, jnp.zeros((32, 128), F32)], axis=1)
        for n in range(5):
            moved = taps if n in (1, 4) else pltpu.roll(taps, 96 if n == 2 else 192, 1)
            if n == 0:
                moved = jnp.where(lane < 384, moved, 0.0)
            if n == 4:
                moved = jnp.where(lane >= 96, moved, 0.0)
            conv_a_ref[96 * n + 32 * dz : 96 * n + 32 * dz + 32] = moved.astype(BF16)
    pad_ref[0:9] = jnp.zeros((9, 32, 128), BF16)
    pad_ref[0:9, 0:28, 0:36] = w_d_ref[...]
    taps = pad_ref[0:12].astype(F32).reshape(384, 128)
    taps = jnp.where(iota((384, 128), 0) < 288, taps, 0.0)
    taps = jnp.concatenate([taps[128 * n : 128 * n + 128].T[0:40] for n in range(3)], axis=1)
    taps = jnp.concatenate([taps, jnp.zeros((40, 384), F32)], axis=1)
    lane = iota((40, 768), 1)
    for n in range(8):
        if n < 4:
            moved = taps if n == 0 else pltpu.roll(taps, 96 * n, 1)
        elif n == 4:
            moved = jnp.where(lane < 192, taps, 0.0) + jnp.where(
                lane >= 576, pltpu.roll(taps, 384, 1), 0.0
            )
        elif n == 5:
            moved = jnp.where(within(lane, 96, 191), pltpu.roll(taps, 96, 1), 0.0) + jnp.where(
                within(lane, 576, 671), pltpu.roll(taps, 480, 1), 0.0
            )
        elif n == 6:
            moved = jnp.where(within(lane, 384, 479), pltpu.roll(taps, 192, 1), 0.0) + jnp.where(
                lane >= 672, pltpu.roll(taps, 576, 1), 0.0
            )
        else:
            moved = jnp.where(within(lane, 384, 575), pltpu.roll(taps, 288, 1), 0.0) + jnp.where(
                lane >= 672, pltpu.roll(taps, 672, 1), 0.0
            )
        conv_d_ref[40 * n : 40 * n + 40] = moved.astype(BF16)
    bias_ref[0:32] = jnp.broadcast_to(as_column(b_a_ref[...], 32), (32, 128))
    bias_ref[32:72] = jnp.broadcast_to(as_column(b_d_ref[...], 40), (40, 128))

    pad_ref[0] = jnp.zeros((32, 128), BF16)
    pad_ref[0, 0:9, 0:28] = w_in_ref[...]
    tap = iota((32, 128), 0)
    lane = iota((32, 128), 1)
    put = (lane == 16 * (tap % 3) + tap // 3) & (tap < 9)
    base = lax.dot_general(
        pad_ref[0],
        put.astype(F32).astype(BF16),
        (((0,), (0,)), ((), ())),
        preferred_element_type=F32,
    )[0:32]
    bias = as_column(b_in_ref[...], 32)
    rest = bias
    extra = jnp.where(lane == 51, BIG, 0.0)
    for n in range(3):
        part = rest.astype(BF16).astype(F32)
        extra = extra + jnp.where(lane == 48 + n, part, 0.0)
        rest = rest - part
    for y in range(14):
        taps = extra + (base if y == 0 else pltpu.roll(base, y, 1))
        if y < 3:
            taps = taps + jnp.where(lane == 52, BIG, 0.0)
        if y >= 11:
            taps = taps + jnp.where(lane == 53, BIG, 0.0)
        conv_in_ref[32 * y : 32 * y + 32] = taps.astype(BF16)

    w_o = w_o_ref[...].astype(F32)
    w_o = jnp.concatenate([jnp.broadcast_to(w_o[o : o + 1], (8, 28)) for o in range(3)], axis=0)
    w_o = jnp.concatenate([w_o, jnp.zeros((24, 4), F32)], axis=1)
    pad_ref[0] = jnp.zeros((32, 128), BF16)
    pad_ref[0, 0:28, 0:36] = w_u_ref[...]
    w_u = pad_ref[0].astype(F32)
    w_u = jnp.concatenate([w_u, jnp.zeros_like(w_u)], axis=1)
    w_u = w_u + pltpu.roll(w_u, 40, 1)
    w_u = w_u + pltpu.roll(w_u, 80, 1)
    w_q = dot(w_o.astype(BF16), w_u.astype(BF16))
    lane = iota((24, 256), 1)
    w_q = jnp.where(lane // 40 == (iota((24, 256), 0) % 8) // 2, w_q, 0.0)
    high = w_q.astype(BF16).astype(F32)
    w_q_ref[...] = jnp.concatenate([high, w_q - high], axis=0).astype(BF16)
    w_o = jnp.concatenate([w_o] * 12, axis=1)
    w_o = jnp.concatenate([w_o, w_o], axis=0)
    lane = iota((48, 384), 1) // 32
    row = iota((48, 384), 0)
    block = jnp.where(row < 24, row % 8, jnp.where(within(row % 8, 3, 4), row % 8 + 5, row % 8))
    w_s_ref[...] = jnp.where(lane == block, w_o, 0.0).astype(BF16)
    row = iota((48, 128), 0) % 24
    bias_ref[72:120] = jnp.where(row < 8, b_o_ref[0], jnp.where(row < 16, b_o_ref[1], b_o_ref[2]))
    bias_ref[120:128] = jnp.zeros((8, 128), F32)


def exchange_kernel(*refs):
    raw_hbm, hbm, b_o_ref = refs[0], refs[1:9], refs[9]
    got_ref, made = refs[10], refs[11:17]
    raw_ref, vmem, pad_ref, send_ref = refs[17], refs[18:26], refs[26], refs[27]
    raw_sem, load_sem, send_sem, recv_sem = refs[28:32]
    gi = lax.axis_index("gx")
    gj = lax.axis_index("gy")
    odd, column, beside = neighbours(gi)
    load_raw = pltpu.make_async_copy(raw_hbm, raw_ref, raw_sem)
    load_raw.start()
    loads = [pltpu.make_async_copy(hbm[n], vmem[n], load_sem.at[n]) for n in range(8)]
    for load in loads:
        load.start()
    barrier = pltpu.get_barrier_semaphore()

    def greet(n, carry):
        strip = lax.rem(2 * gj + 15 + lax.rem(n, 4), 16)
        slab = lax.div(n, 4)

        @pl.when((strip != gi) | (slab != gj))
        def _():
            pl.semaphore_signal(barrier, inc=1, device_id=(strip, slab), device_id_type=MESH)

        return carry

    lax.fori_loop(0, 32, greet, 0)

    lane = iota((128, 256), 1)
    wanted = iota((128, 256), 0) + jnp.where(lane < 128, -4, 4)
    rows = (wanted == lane % 128).astype(F32).astype(BF16)
    load_raw.wait()
    raw = raw_ref[0].astype(F32)
    none = jnp.zeros_like(raw)
    raw = jnp.concatenate(
        [jnp.concatenate([raw, none], axis=1), jnp.concatenate([none, raw], axis=1)], axis=0
    ).astype(BF16)
    message = lax.dot_general(
        rows, raw, (((1,), (1,)), ((), ())), preferred_element_type=F32
    ).astype(BF16)
    lane = iota((128, 128), 1)
    even = jnp.where(within(lane, 6, 9), lane - 6, jnp.where(within(lane, 22, 25), lane + 42, -1))
    uneven = jnp.where(
        within(lane, 118, 121), lane - 58, jnp.where(within(lane, 102, 105), lane + 22, -1)
    )
    cols = jnp.where((gi == 0) | (gi == 15), -1, jnp.where(odd == 1, uneven, even))
    cols = (iota((128, 128), 0) == cols).astype(F32).astype(BF16)
    send_ref[0:16] = message.reshape(16, 8, 128)
    send_ref[16:32] = dot(message, cols).astype(BF16).reshape(16, 8, 128)

    at_home = (gj == column) | (gj == beside)

    @pl.when(at_home)
    def _():
        pl.semaphore_wait(barrier, 31)

    @pl.when(jnp.logical_not(at_home))
    def _():
        pl.semaphore_wait(barrier, 32)

    def send(n, carry):
        target = lax.rem(gi + n, 16)
        for kind in range(2):
            where_to = column if kind == 0 else beside
            slot = odd if kind == 0 else 3 - odd
            source = send_ref.at[target + 16 * kind]
            place = got_ref.at[slot, gj]
            here = (target == gi) & (where_to == gj)

            @pl.when(here)
            def _():
                pltpu.make_async_copy(source, place, recv_sem).start()

            @pl.when(jnp.logical_not(here))
            def _():
                pltpu.make_async_remote_copy(
                    src_ref=source,
                    dst_ref=place,
                    send_sem=send_sem,
                    recv_sem=recv_sem,
                    device_id=(target, where_to),
                    device_id_type=MESH,
                ).start()

        return carry

    lax.fori_loop(0, 16, send, 0)
    for load in loads:
        load.wait()
    prepare(pad_ref, *vmem, b_o_ref, *made)
    pltpu.make_async_copy(got_ref, got_ref, recv_sem).wait()

    @pl.when(at_home)
    def _():
        pltpu.make_async_copy(send_ref.at[0:31], send_ref.at[0:31], send_sem).wait()

    @pl.when(jnp.logical_not(at_home))
    def _():
        pltpu.make_async_copy(send_ref, send_ref, send_sem).wait()


MADE = (
    jax.ShapeDtypeStruct((448, 128), BF16),
    jax.ShapeDtypeStruct((480, 512), BF16),
    jax.ShapeDtypeStruct((320, 768), BF16),
    jax.ShapeDtypeStruct((48, 256), BF16),
    jax.ShapeDtypeStruct((48, 384), BF16),
    jax.ShapeDtypeStruct((128, 128), F32),
)


def as_they_lie(raw, w_in, b_in, w_a, b_a, w_d, b_d, w_u, w_o):
    return (
        jnp.transpose(raw, (0, 2, 1)),
        w_in.T,
        b_in[None],
        w_a,
        b_a[None],
        jnp.transpose(w_d, (0, 2, 1)),
        b_d[None],
        w_u,
        w_o,
    )


def exchange(b_o, *arrays):
    arrays = as_they_lie(*arrays)
    vmem = pl.BlockSpec(memory_space=pltpu.VMEM)
    return pl.pallas_call(
        exchange_kernel,
        out_shape=(jax.ShapeDtypeStruct((4, 8, 8, 128), BF16),) + MADE,
        in_specs=[pl.BlockSpec(memory_space=pltpu.HBM)] * 9
        + [pl.BlockSpec(memory_space=pltpu.SMEM)],
        out_specs=(pl.BlockSpec(memory_space=pl.ANY),) + (vmem,) * 6,
        scratch_shapes=[pltpu.VMEM(x.shape, x.dtype) for x in arrays]
        + [
            pltpu.VMEM((27, 32, 128), BF16),
            pltpu.VMEM((32, 8, 128), BF16),
            pltpu.SemaphoreType.DMA,
            pltpu.SemaphoreType.DMA((8,)),
            pltpu.SemaphoreType.DMA,
            pltpu.SemaphoreType.DMA,
        ],
        compiler_params=pltpu.CompilerParams(
            collective_id=0, has_side_effects=True, vmem_limit_bytes=12 * 1024 * 1024
        ),
    )(*arrays, b_o)


def tables():
    pool = np.zeros((768, 128), np.float32)
    shift = np.zeros((5, 256, 256), np.float32)
    spread = np.zeros((256, 256), np.float32)
    spread_side = np.zeros((256, 128), np.float32)
    for row in range(2):
        for section in range(2):
            for x in range(128):
                pool[256 * section + 128 * row + x, 64 * section + x // 2] = 0.25
        for section in range(8):
            for x in range(6):
                pool[512 + 128 * row + 16 * section + x, 8 * section + x // 2] = 0.25
                pool[512 + 128 * row + 16 * section + 10 + x, 8 * section + 4 + x // 2] = 0.25
        for lane in range(256):
            spread[128 * row + lane // 2, lane] = 1
        for section in range(8):
            for x in range(4):
                at = 128 * row + 8 * section
                spread_side[at + 1 + x // 2, 16 * section + 2 + x] = 1
                spread_side[at + 4 + x // 2, 16 * section + 10 + x] = 1
    for section in range(8):
        for m in range(64):
            lane = 64 * (section % 2) + m
            for side, step in ((0, -1), (1, 1)):
                at = m + step
                if at < 0:
                    source = 128 + 8 * section
                elif at > 63:
                    source = 128 + 8 * section + 6
                else:
                    source = lane + step
                shift[section // 2, source, 128 * side + lane] = 1
        for lane, before, beyond in ((1, 0, 2), (2, 1, None), (4, None, 5), (5, 4, 6)):
            for side, source in ((0, before), (1, beyond)):
                if source is not None:
                    shift[4, 8 * section + source, 128 * side + 8 * section + lane] = 1
    wide = np.concatenate([shift.reshape(1280, 256), spread])
    narrow = np.concatenate([pool, spread_side])
    return wide.astype(ml_dtypes.bfloat16), narrow.astype(ml_dtypes.bfloat16)


def network_kernel(
    place,
    order_ref,
    margins_ref,
    got_ref,
    conv_in_ref,
    conv_a_ref,
    conv_d_ref,
    w_q_ref,
    w_s_ref,
    bias_ref,
    wide_hbm,
    narrow_hbm,
    out_ref,
    wide_ref,
    narrow_ref,
    raw_ref,
    h_ref,
    a_ref,
    d_ref,
    e_ref,
    wide_sem,
    narrow_sem,
):
    gi, gj = place()
    load_wide = pltpu.make_async_copy(wide_hbm, wide_ref, wide_sem)
    load_narrow = pltpu.make_async_copy(narrow_hbm, narrow_ref, narrow_sem)
    load_narrow.start()
    load_wide.start()

    def margin(step_y, step_x):
        y, x = gi + step_y, gj + step_x
        inside = (y >= 0) & (y < 16) & (x >= 0) & (x < 8)
        value = margins_ref[jnp.clip(x, 0, 7), jnp.clip(y, 0, 15)]
        return value.astype(F32), jnp.where(inside, 1.0, 0.0)

    def ramp(distance, width):
        return jnp.clip(1.0 - distance / (width + 1.0), 0.0, 1.0)

    y = iota((8, 128), 0)
    lane = iota((8, 128), 1)
    upper = y < 4
    off_y = jnp.where(upper, y + 1, 8 - y).astype(F32)
    nth = lane % 16
    leftward = nth < 8
    off_x = jnp.where(
        within(nth, 2, 5), nth - 1, jnp.where(within(nth, 10, 13), 14 - nth, 99)
    ).astype(F32)

    def by_place(pairs):
        m = jnp.where(leftward, pairs[0][0], pairs[1][0])
        there = jnp.where(leftward, pairs[0][1], pairs[1][1])
        return m, there

    m_up, in_up = margin(-1, 0)
    m_down, in_down = margin(1, 0)
    weight_y = ramp(off_y, jnp.where(upper, m_up, m_down)) * jnp.where(upper, in_up, in_down)
    m, there = by_place((margin(0, -1), margin(0, 1)))
    weight_x = ramp(off_x, m) * there
    m_top, there_top = by_place((margin(-1, -1), margin(-1, 1)))
    m_low, there_low = by_place((margin(1, -1), margin(1, 1)))
    m = jnp.where(upper, m_top, m_low)
    weight_xy = ramp(off_y, m) * ramp(off_x, m) * jnp.where(upper, there_top, there_low)

    def fold(core, beyond, z):
        left = jnp.where(lane < 4, pltpu.roll(beyond, (126 - 16 * z) % 128, 1), 0.0)
        right = jnp.where(lane >= 124, pltpu.roll(beyond, (114 - 16 * z) % 128, 1), 0.0)
        return core + left + right

    scale = 1.0 / fold(1.0 + weight_y, weight_x + weight_xy, 0)

    tile = iota((16, 128), 1)
    sides = [jnp.zeros((16, 128), F32) for _ in range(5)]
    for z in range(8):
        slab = jnp.int32(0)
        for k in range(8):
            slab = slab + jnp.where(order_ref[k] == z, k, 0)
        near, far, before, after = [got_ref[n, slab].astype(F32) for n in range(4)]
        core = jnp.concatenate(
            [
                jnp.where(lane < 64, near, pltpu.roll(far, 64, 1)),
                jnp.where(lane < 64, pltpu.roll(near, 64, 1), far),
            ],
            axis=0,
        )
        before = jnp.concatenate([before, pltpu.roll(before, 16, 1)], axis=0)
        after = jnp.concatenate([after, pltpu.roll(after, 112, 1)], axis=0)
        low = jnp.where(tile < 6, pltpu.roll(core, 6, 1), after)
        high = jnp.where(tile >= 122, pltpu.roll(core, 122, 1), before)
        beside = jnp.where(tile < 64, low, high)
        for n in range(5):
            s = n - 2
            moved = core if s == 0 else pltpu.roll(core, -s % 128, 1)
            if s > 0:
                moved = jnp.where(tile >= 128 - s, pltpu.roll(beside, 122 - s, 1), moved)
            if s < 0:
                moved = jnp.where(tile < -s, pltpu.roll(beside, 6 - s, 1), moved)
            raw_ref[16 * n : 16 * n + 16, 128 * z : 128 * z + 128] = moved.astype(BF16)
            moved = pltpu.roll(beside, (16 * z + 8 - s) % 128, 1)
            sides[n] = jnp.where(tile // 16 == z, moved, sides[n])
    for n in range(5):
        raw_ref[16 * n : 16 * n + 16, 1024:1152] = sides[n].astype(BF16)

    def flags(dx, side):
        kind = iota((16, 128), 0)
        nth = tile % 16
        if side:
            column = jnp.where(nth < 8, nth - 3 + dx, 113 + nth + dx)
            cut = jnp.where(nth < 8, 4, 123)
            outside = column == cut
        else:
            column = tile + dx - 1
            outside = tile < 0
        outside = outside | ((column < 0) & (gj == 0)) | ((column > 127) & (gj == 7))
        value = jnp.where(kind < 3, 1.0, 0.0)
        value = jnp.where((kind == 3) & outside, 1.0, value)
        value = jnp.where((kind == 4) & (gi == 0), 1.0, value)
        return jnp.where((kind == 5) & (gi == 15), 1.0, value).astype(BF16)

    for dx in range(3):
        flag = flags(dx, False)
        flag = jnp.concatenate([flag, flag], axis=1)
        for q in range(5):
            at = slice(256 * q, 256 * q + 256) if q < 4 else slice(1024, 1152)
            taps = jnp.concatenate(
                [raw_ref[16 * dx : 16 * dx + 48, at], flag if q < 4 else flags(dx, True)], axis=0
            )
            h = jnp.maximum(dot(conv_in_ref[:, 0:64], taps).astype(BF16), 0)
            h_ref[:, dx, :, at] = h.reshape(14, 32, h.shape[1])

    bias_a = bias_ref[0:32]

    def residual(three):
        extra = three in (1, 2)
        first = 0 if three == 1 else 1
        names = [None, 3 * three, 3 * three + 1, 3 * three + 2, None]
        names[0], names[4] = 10, 11
        names = [n if n < 10 or k in (0, 4) else n + 2 for k, n in enumerate(names)]
        count = 4 if extra else 3
        lane = iota((count, 32, 128), 2)

        def finish(total, at):
            total = jnp.maximum(total + bias_a, 0.0)
            for n in range(count):
                which = first + n
                step = (2, 0, 1, 2, 0)[which]
                centre = h_ref[3 * three + 1 + step, 1, :, at].astype(F32)
                a_ref[names[which], :, at] = (centre + total[n]).astype(BF16)

        parts = []
        for q in range(5):
            at = slice(256 * q, 256 * q + 256) if q < 4 else slice(1024, 1152)
            rows = h_ref[3 * three : 3 * three + 5, :, :, at].reshape(480, at.stop - at.start)
            product = dot(conv_a_ref[96 * first : 96 * (first + count), 0:480], rows)
            product = product.reshape(count, 3, 32, at.stop - at.start)
            if q == 4:
                total = product[:, 1]
                total = total + jnp.where(lane >= 16, pltpu.roll(product[:, 0], 16, 2), 0.0)
                total = total + jnp.where(lane < 112, pltpu.roll(product[:, 2], 112, 2), 0.0)
                finish(total, at)
                break
            for half in range(2):
                parts.append(product[:, :, :, 128 * half : 128 * half + 128])
                z = len(parts) - 2
                if z >= 0:
                    total = parts[z][:, 1] + parts[z + 1][:, 2]
                    if z > 0:
                        total = total + parts[z - 1][:, 0]
                    finish(total, slice(128 * z, 128 * z + 128))
        finish(parts[7][:, 1] + parts[6][:, 0], slice(896, 1024))

    for three in range(4):
        residual(three)

    def pooled_rows(at):
        even = jnp.concatenate([a_ref[n, :, at] for n in (0, 2, 4, 6, 8, 12, 4, 11)], axis=0)
        late = jnp.concatenate([a_ref[n, :, at] for n in (1, 3, 5, 7, 9, 13, 10, 7)], axis=0)
        return jnp.concatenate([even, late], axis=1)

    load_narrow.wait()
    load_wide.wait()

    def store(dx, at, value):
        d_ref[:, dx, :, at] = value.reshape(8, 32, 128)

    margins = dot(pooled_rows(slice(1024, 1152)), narrow_ref[512:768]).astype(BF16)
    for q in range(5):
        at = slice(128 * q, 128 * q + 128)
        if q < 4:
            both = [pooled_rows(slice(128 * z, 128 * z + 128)) for z in (2 * q, 2 * q + 1)]
            d = dot(jnp.concatenate(both, axis=1), narrow_ref[0:512]).astype(BF16)
            moved = dot(
                jnp.concatenate([d, margins], axis=1), wide_ref[256 * q : 256 * q + 256]
            ).astype(BF16)
        else:
            d = margins
            moved = dot(d, wide_ref[1024:1152]).astype(BF16)
        store(1, at, d)
        store(0, at, moved[:, 0:128])
        store(2, at, moved[:, 128:256])

    bias_d = jnp.concatenate([bias_ref[32:72]] * 8, axis=0)
    for at in (slice(0, 256), slice(256, 512), slice(512, 640)):
        e = dot(conv_d_ref[...], d_ref[:, :, :, at].reshape(768, at.stop - at.start))
        e = e + (bias_d if e.shape[1] == 128 else jnp.concatenate([bias_d, bias_d], axis=1))
        e_ref[:, at] = jnp.maximum(e, 0.0).astype(BF16)

    lifted = []
    for kind in range(2):
        q = dot(w_q_ref[:, 0:160], e_ref[160 * kind : 160 * kind + 160])
        lifted.append(q[0:24] + q[24:48])
    q = jnp.concatenate(lifted, axis=0)
    high = q.astype(BF16).astype(F32)
    low = q - high

    def both(n):
        at = slice(128 * n, 128 * n + 128)
        return jnp.concatenate([high[:, at], low[:, at]], axis=1).astype(BF16)

    bias_o = bias_ref[72:120]

    def logits(at):
        s = dot(w_s_ref[:, 0:320], a_ref[2:12, :, at].reshape(320, at.stop - at.start))
        return s + (bias_o if s.shape[1] == 128 else jnp.concatenate([bias_o, bias_o], axis=1))

    at = slice(1024, 1152)
    beyond = jax.nn.sigmoid(logits(at) + dot(both(4), narrow_ref[768:1024]))
    beyond = [
        beyond[8 * o : 8 * o + 8] * weight_x + beyond[24 + 8 * o : 32 + 8 * o] * weight_xy
        for o in range(3)
    ]
    up = dot(jnp.concatenate([both(n) for n in range(4)], axis=0), wide_ref[1280:1536])
    for n in range(4):
        at = slice(256 * n, 256 * n + 256)
        s = jax.nn.sigmoid(logits(at) + up[48 * n : 48 * n + 48])
        for half in range(2):
            z = 2 * n + half
            for o in range(3):
                own = s[8 * o : 8 * o + 8, 128 * half : 128 * half + 128]
                other = s[24 + 8 * o : 32 + 8 * o, 128 * half : 128 * half + 128]
                out_ref[o, z] = fold(own + other * weight_y, beyond[o], z) * scale


def network(place, order, margins, got, *made, **options):
    smem = pl.BlockSpec(memory_space=pltpu.SMEM)
    vmem = pl.BlockSpec(memory_space=pltpu.VMEM)
    hbm = pl.BlockSpec(memory_space=pltpu.HBM)
    return pl.pallas_call(
        functools.partial(network_kernel, place),
        out_shape=jax.ShapeDtypeStruct((3, 8, 8, 128), F32),
        in_specs=[smem] * 2 + [vmem] * 7 + [hbm] * 2,
        out_specs=vmem,
        scratch_shapes=[
            pltpu.VMEM((1536, 256), BF16),
            pltpu.VMEM((1024, 128), BF16),
            pltpu.VMEM((80, 1152), BF16),
            pltpu.VMEM((14, 3, 32, 1152), BF16),
            pltpu.VMEM((14, 32, 1152), BF16),
            pltpu.VMEM((8, 3, 32, 640), BF16),
            pltpu.VMEM((320, 640), BF16),
            pltpu.SemaphoreType.DMA,
            pltpu.SemaphoreType.DMA,
        ],
        compiler_params=pltpu.CompilerParams(vmem_limit_bytes=32 * 1024 * 1024),
        **options,
    )(order, margins.T, got, *made, *tables())


def whereabouts():
    return lax.axis_index("gx"), lax.axis_index("gy")


def per_device(raw, section_order, margins, w_in, b_in, w_a, b_a, w_d, b_d, w_u, w_o, b_o):
    got, *made = exchange(b_o, raw, w_in, b_in, w_a, b_a, w_d, b_d, w_u, w_o)
    return network(whereabouts, section_order, margins, got, *made)


def solution(mesh):
    placed = (P("gy", None, "gx"), P(), P(), P(), P(), P(), P(), P(), P(), P(), P(), P())
    return jax.shard_map(
        per_device, mesh=mesh, in_specs=placed, out_specs=P(None, None, "gx", "gy"), check_vma=False
    )
```

```python
import functools

import jax
import jax.numpy as jnp
import ml_dtypes
import numpy as np
from jax import lax
from jax.experimental import pallas as pl
from jax.experimental.pallas import tpu as pltpu
from jax.sharding import PartitionSpec as P

MESH = pl.DeviceIdType.MESH
F32 = jnp.float32
BF16 = jnp.bfloat16
BIG = -1e30


def iota(shape, dim):
    return lax.broadcasted_iota(jnp.int32, shape, dim)


def within(x, low, high):
    return (x >= low) & (x <= high)


def dot(a, b):
    return jnp.dot(a, b, preferred_element_type=F32)


def neighbours(gi):
    odd = lax.rem(gi, 2)
    column = lax.div(gi, 2)
    beside = lax.rem(column + 7 + 2 * odd, 8)
    return odd, column, beside


def unit_row(dx, block, channel):
    if dx == 1:
        return 32 * block + channel
    unit = 3 * (dx // 2) + block
    if unit < 5:
        return 96 + 28 * unit + channel
    return 236 + channel if channel < 20 else 8 + channel if channel < 24 else 36 + channel


def units_table():
    table = np.zeros((3, 3, 32, 256), np.float32)
    for block in range(3):
        for dx in range(3):
            for channel in range(28):
                table[block, dx, channel, unit_row(dx, block, channel)] = 1
    return table.reshape(288, 256).astype(ml_dtypes.bfloat16)


def level_table():
    spread = np.zeros((256, 256), np.float32)
    core = np.zeros((2, 128, 256), np.float32)
    side = np.zeros((2, 128, 512), np.float32)
    spread_side = np.zeros((2, 128, 128), np.float32)
    for lane in range(256):
        spread[lane // 2, lane] = spread[128 + lane // 2, lane] = 1
    for m in range(64):
        for fine in (0, 1):
            if m >= 1:
                core[:, 2 * m - 2 + fine, m] = 0.25
            if m <= 62:
                core[:, 2 * m + 2 + fine, 64 + m] = 0.25
            core[:, 2 * m + fine, 128 + m] = 0.25
    for section in range(8):
        for fine in (0, 1):
            for dx in range(3):
                for m in (0, 1):
                    left, right = m + dx - 1, 62 + m + dx - 1
                    if left <= 1:
                        side[:, 16 * section + 2 + 2 * left + fine, 128 * dx + 8 * section + 1 + m] = 0.25
                    if right >= 62:
                        side[:, 16 * section + 2 * right - 114 + fine, 128 * dx + 8 * section + 4 + m] = 0.25
            at = 384 + 64 * (section % 2) + section // 2
            side[:, 16 * section + fine, at] = 0.25
            side[:, 16 * section + 14 + fine, at + 60] = 0.25
        for x in range(4):
            spread_side[:, 8 * section + 1 + x // 2, 16 * section + 2 + x] = 1
            spread_side[:, 8 * section + 4 + x // 2, 16 * section + 10 + x] = 1
    parts = [spread, core.reshape(256, 256), side.reshape(256, 512), spread_side.reshape(256, 128)]
    return np.concatenate(parts, axis=1).astype(ml_dtypes.bfloat16)


def as_column(row, size):
    shape = (size, row.shape[1])
    return jnp.sum(jnp.where(iota(shape, 0) == iota(shape, 1), row, 0.0), axis=1, keepdims=True)


def tiled_taps(pad_ref, first, taps):
    tiles = []
    for start in range(0, taps, 4):
        tile = None
        for q in range(min(4, taps - start)):
            part = pad_ref[first + start + q].astype(F32)
            part = part if q == 0 else pltpu.roll(part, 32 * q, 1)
            tile = part if tile is None else tile + part
        tiles.append(tile)
    return jnp.concatenate(tiles, axis=1)


def lay_out_weights(
    units_ref,
    w_in_ref,
    b_in_ref,
    w_a_ref,
    b_a_ref,
    w_d_ref,
    b_d_ref,
    w_u_ref,
    w_o_ref,
    b_o_ref,
    pad_ref,
    conv_in_ref,
    conv_a_ref,
    conv_d_ref,
    w_q_ref,
    w_s_ref,
    bias_ref,
):
    pad_ref[...] = jnp.zeros_like(pad_ref)
    pad_ref[0, 0:9, 0:28] = w_in_ref[...]
    tap = iota((32, 128), 0)
    lane = iota((32, 128), 1)
    put = (lane == 16 * (tap % 3) + tap // 3) & (tap < 9)
    base = lax.dot_general(
        pad_ref[0],
        put.astype(F32).astype(BF16),
        (((0,), (0,)), ((), ())),
        preferred_element_type=F32,
    )[0:32]
    rest = as_column(b_in_ref[...], 32)
    flagged = jnp.zeros((32, 128), F32)
    for n in range(3):
        part = rest.astype(BF16).astype(F32)
        flagged = flagged + jnp.where(lane == 80 + n, part, 0.0)
        rest = rest - part
    stack = []
    for block in range(3):
        for dx in range(3):
            row = []
            for tile in range(5):
                y = 3 * tile + block
                if y > 13:
                    row.append(jnp.zeros((32, 128), F32))
                    continue
                moved = base if dx == y == 0 else pltpu.roll(base, 16 * dx + y, 1)
                off = (lane == 83 + dx) | ((lane == 86) & (y < 3)) | ((lane == 87) & (y >= 11))
                row.append(moved + flagged + jnp.where(off, BIG, 0.0))
            stack.append(jnp.concatenate(row, axis=1))
    made = lax.dot_general(
        units_ref[...],
        jnp.concatenate(stack, axis=0).astype(BF16),
        (((0,), (0,)), ((), ())),
        preferred_element_type=F32,
    ).astype(BF16)
    for tile in range(5):
        conv_in_ref[256 * tile : 256 * tile + 256] = made[:, 128 * tile : 128 * tile + 128]

    pad_ref[0] = jnp.zeros((32, 128), BF16)
    pad_ref[0:27, 0:28, 0:28] = w_a_ref[...]
    lane = iota((32, 384), 1)
    parts = [[] for _ in range(7)]
    for dz in range(3):
        taps = tiled_taps(pad_ref, 9 * dz, 9)
        for n, shift in enumerate((-1, -2, -1, 0, 1, 2, 0)):
            moved = taps if shift == 0 else pltpu.roll(taps, 96 * shift % 384, 1)
            low, high = 96 * max(shift, 0), 96 * min(3 + shift, 3)
            if n == 0:
                high = 96
            if n == 6:
                low = 96
            parts[n].append(jnp.where((lane >= low) & (lane < high), moved, 0.0))
    taps = jnp.concatenate([part for shift in parts for part in shift], axis=0).astype(BF16)
    conv_a_ref[...] = dot(taps[:, 0:288], units_ref[...]).astype(BF16)

    pad_ref[0:9] = jnp.zeros((9, 32, 128), BF16)
    pad_ref[0:9, 0:28, 0:36] = w_d_ref[...]
    taps = pad_ref[0:12].astype(F32).reshape(384, 128)
    taps = jnp.where(iota((384, 128), 0) < 288, taps, 0.0)
    taps = jnp.concatenate([taps[128 * n : 128 * n + 128].T[0:40] for n in range(3)], axis=1)
    taps = jnp.concatenate([taps, jnp.zeros((40, 384), F32)], axis=1)
    lane = iota((40, 768), 1)

    def spaced(*moves):
        total = None
        for first, dy, count in moves:
            by = 96 * (first - dy) % 768
            moved = taps if by == 0 else pltpu.roll(taps, by, 1)
            moved = jnp.where(within(lane, 96 * first, 96 * (first + count) - 1), moved, 0.0)
            total = moved if total is None else total + moved
        return total

    outs = [
        spaced((0, 0, 2), (6, 2, 1)),
        spaced((1, 0, 1), (6, 1, 1)),
        spaced((0, 0, 3)),
        spaced((1, 0, 3)),
        spaced((2, 0, 3)),
        spaced((3, 0, 3)),
        spaced((4, 2, 1), (7, 1, 1)),
        spaced((4, 1, 2), (7, 0, 1)),
    ]
    none = [jnp.zeros((8, 256), F32)]
    for at, tile, which in (
        (0, 0, (0, 1, 2, 3, 4)),
        (208, 1, (2, 3, 4, 5, 6, 7)),
        (448, 2, (0, 1, 5, 6, 7)),
    ):
        part = [outs[n][:, 256 * tile : 256 * tile + 256] for n in which]
        part = jnp.concatenate(part if tile == 1 else part + none, axis=0)
        conv_d_ref[at : at + part.shape[0]] = part.astype(BF16)

    w_o = w_o_ref[...].astype(F32)
    w_o = jnp.concatenate([jnp.broadcast_to(w_o[o : o + 1], (8, 28)) for o in range(3)], axis=0)
    w_o = jnp.concatenate([w_o, jnp.zeros((24, 4), F32)], axis=1)
    pad_ref[0] = jnp.zeros((32, 128), BF16)
    pad_ref[0, 0:28, 0:36] = w_u_ref[...]
    w_u = pad_ref[0].astype(F32)
    w_u = jnp.concatenate([w_u, jnp.zeros_like(w_u)], axis=1)
    w_u = w_u + pltpu.roll(w_u, 40, 1)
    w_u = w_u + pltpu.roll(w_u, 80, 1)
    w_q = dot(w_o.astype(BF16), w_u.astype(BF16))
    lane = iota((24, 256), 1)
    w_q = jnp.where(lane // 40 == (iota((24, 256), 0) % 8) // 2, w_q, 0.0)
    high = w_q.astype(BF16).astype(F32)
    w_q_ref[...] = jnp.concatenate([high, w_q - high], axis=0).astype(BF16)
    w_o = jnp.concatenate([w_o] * 12, axis=1)
    w_o = jnp.concatenate([w_o, w_o], axis=0)
    lane = iota((48, 384), 1) // 32
    row = iota((48, 384), 0)
    block = jnp.where(row < 24, row % 8, jnp.where(within(row % 8, 3, 4), row % 8 + 5, row % 8))
    w_s_ref[...] = jnp.where(lane == block, w_o, 0.0).astype(BF16)

    bias_ref[0:32] = jnp.broadcast_to(as_column(b_a_ref[...], 32), (32, 128))
    bias_ref[32:72] = jnp.broadcast_to(as_column(b_d_ref[...], 40), (40, 128))
    row = iota((48, 3), 0) % 24 // 8
    b_o = jnp.sum(jnp.where(row == iota((48, 3), 1), b_o_ref[...], 0.0), axis=1, keepdims=True)
    bias_ref[72:120] = jnp.broadcast_to(b_o, (48, 128))
    bias_ref[120:128] = jnp.zeros((8, 128), F32)


def fold(core, beyond, z):
    lane = iota((8, 128), 1)
    left = jnp.where(lane < 4, pltpu.roll(beyond, (126 - 16 * z) % 128, 1), 0.0)
    right = jnp.where(lane >= 124, pltpu.roll(beyond, (114 - 16 * z) % 128, 1), 0.0)
    return core + left + right


def blend_weights(gi, gj, margins_ref, blend_ref):
    margins = margins_ref[...].astype(F32)
    places = margins.shape

    def margin(step_y, step_x):
        y, x = gi + step_y, gj + step_x
        here = (iota(places, 0) == x) & (iota(places, 1) == y)
        value = jnp.sum(jnp.where(here, margins, 0.0), keepdims=True)
        return value, (y >= 0) & (y < 16) & (x >= 0) & (x < 8)

    def ramp(distance, pair):
        return jnp.clip(1.0 - distance / (pair[0] + 1.0), 0.0, 1.0) * jnp.where(pair[1], 1.0, 0.0)

    y = iota((8, 128), 0)
    lane = iota((8, 128), 1)
    upper = y < 4
    off_y = jnp.where(upper, y + 1, 8 - y).astype(F32)
    nth = lane % 16
    left = nth < 8
    off_x = jnp.where(
        within(nth, 2, 5), nth - 1, jnp.where(within(nth, 10, 13), 14 - nth, 99)
    ).astype(F32)
    m = {(a, b): margin(a, b) for a in (-1, 0, 1) for b in (-1, 0, 1) if (a, b) != (0, 0)}
    weight_y = jnp.where(upper, ramp(off_y, m[-1, 0]), ramp(off_y, m[1, 0]))
    weight_x = jnp.where(left, ramp(off_x, m[0, -1]), ramp(off_x, m[0, 1]))

    def corner(a, b):
        return ramp(off_y, m[a, b]) * ramp(off_x, m[a, b])

    weight_xy = jnp.where(
        upper,
        jnp.where(left, corner(-1, -1), corner(-1, 1)),
        jnp.where(left, corner(1, -1), corner(1, 1)),
    )
    blend_ref[0:8] = weight_y
    blend_ref[8:16] = weight_x
    blend_ref[16:24] = weight_xy
    blend_ref[24:32] = 1.0 / fold(1.0 + weight_y, weight_x + weight_xy, 0)


def flag_rows(gi, gj, side):
    kind = iota((16, 128), 0)
    lane = iota((16, 128), 1)
    dx = kind - 3
    if side:
        nth = lane % 16
        column = jnp.where(nth < 8, nth - 3 + dx, 113 + nth + dx)
        outside = column == jnp.where(nth < 8, 4, 123)
    else:
        column = lane + dx - 1
        outside = lane < 0
    outside = outside | ((column < 0) & (gj == 0)) | ((column > 127) & (gj == 7))
    value = (kind < 3) | (within(kind, 3, 5) & outside)
    value = value | ((kind == 6) & (gi == 0)) | ((kind == 7) & (gi == 15))
    return jnp.where(value, 1.0, 0.0).astype(BF16)


def shift_raw(order_ref, got_ref, got_edge_ref, taps_ref):
    lane = iota((8, 128), 1)
    tile = iota((16, 128), 1)
    sides = [jnp.zeros((16, 128), F32) for _ in range(5)]
    for z in range(8):
        slab = jnp.int32(0)
        for k in range(8):
            slab = jnp.maximum(slab, jnp.where(order_ref[k] == z, k, 0))
        near, far = [got_ref[n, slab].astype(F32) for n in range(2)]
        before, after = [jnp.broadcast_to(got_edge_ref[n, slab], (8, 128)) for n in range(2)]
        core = jnp.concatenate(
            [
                jnp.where(lane < 64, near, pltpu.roll(far, 64, 1)),
                jnp.where(lane < 64, pltpu.roll(near, 64, 1), far),
            ],
            axis=0,
        )
        before = jnp.concatenate(
            [pltpu.roll(before, n, 1, stride=16, stride_axis=0) for n in (6, 2)], axis=0
        )
        after = jnp.concatenate(
            [pltpu.roll(after, n, 1, stride=16, stride_axis=0) for n in (14, 10)], axis=0
        )
        low = jnp.where(tile < 6, pltpu.roll(core, 6, 1), after)
        high = jnp.where(tile >= 122, pltpu.roll(core, 122, 1), before)
        beside = jnp.where(tile < 64, low, high)
        for n in range(5):
            s = n - 2
            moved = core if s == 0 else pltpu.roll(core, -s % 128, 1)
            if s > 0:
                moved = jnp.where(tile >= 128 - s, pltpu.roll(beside, 122 - s, 1), moved)
            if s < 0:
                moved = jnp.where(tile < -s, pltpu.roll(beside, 6 - s, 1), moved)
            taps_ref[16 * n : 16 * n + 16, 128 * z : 128 * z + 128] = moved.astype(BF16)
            moved = pltpu.roll(beside, (16 * z + 8 - s) % 128, 1)
            sides[n] = jnp.where(tile // 16 == z, moved, sides[n])
    for n in range(5):
        taps_ref[16 * n : 16 * n + 16, 1024:1152] = sides[n].astype(BF16)


def exchange_kernel(*refs):
    hbm, refs = refs[0:14], refs[14:]
    taps_ref, made, blend_ref, table_ref, refs = refs[0], refs[1:7], refs[7], refs[8], refs[9:]
    loaded, refs = refs[0:13], refs[13:]
    pad_ref, send_ref, send_edge_ref, got_ref, got_edge_ref, load_sem, send_sem, recv_sem = refs
    raw_ref, order_ref, margins_ref, weights = loaded[0], loaded[1], loaded[2], loaded[3:]
    gi = lax.axis_index("gx")
    gj = lax.axis_index("gy")
    odd, column, beside = neighbours(gi)
    inner = (gi > 0) & (gi < 15)
    loads = [
        pltpu.make_async_copy(source, place, load_sem.at[n])
        for n, (source, place) in enumerate(zip(hbm, loaded + (table_ref,)))
    ]
    loads[0].start()
    barrier = pltpu.get_barrier_semaphore()

    for slab in range(8):
        for strip in (2 * gj, 2 * gj + 1):
            pl.semaphore_signal(barrier, inc=1, device_id=(strip, slab), device_id_type=MESH)

    @pl.when(gj > 0)
    def _():
        for slab in range(8):
            peer = (2 * gj - 1, slab)
            pl.semaphore_signal(barrier, inc=1, device_id=peer, device_id_type=MESH)

    @pl.when(gj < 7)
    def _():
        for slab in range(8):
            peer = (2 * gj + 2, slab)
            pl.semaphore_signal(barrier, inc=1, device_id=peer, device_id_type=MESH)
    for load in loads[1:]:
        load.start()

    lane = iota((128, 256), 1)
    wanted = iota((128, 256), 0) + jnp.where(lane < 128, -4, 4)
    rows = (wanted == lane % 128).astype(F32).astype(BF16)
    lane = iota((128, 128), 1)
    nth = lane % 16 - 8 * (1 - odd)
    cols = jnp.where(within(nth, 0, 3), nth, jnp.where(within(nth, 4, 7), nth + 60, -99)) + 60 * odd
    cols = (iota((128, 128), 0) == cols).astype(F32).astype(BF16)
    own = lane // 16 == 7 - iota((128, 128), 0) % 8
    gather = (iota((16, 128), 0) == iota((16, 128), 1) // 8).astype(F32).astype(BF16)
    loads[0].wait()
    raw = raw_ref[0].astype(F32)
    none = jnp.zeros_like(raw)
    raw = jnp.concatenate(
        [jnp.concatenate([raw, none], axis=1), jnp.concatenate([none, raw], axis=1)], axis=0
    ).astype(BF16)
    message = lax.dot_general(
        rows, raw, (((1,), (1,)), ((), ())), preferred_element_type=F32
    ).astype(BF16)
    send_ref[...] = message.reshape(16, 8, 128)
    edge = dot(gather, jnp.where(own, dot(message, cols), 0.0).astype(BF16))
    for row in range(16):
        send_edge_ref[row] = edge[row : row + 1]

    @pl.when(inner)
    def _():
        pl.semaphore_wait(barrier, 32)

    @pl.when(jnp.logical_not(inner))
    def _():
        pl.semaphore_wait(barrier, 16)

    for row in ROWS:
        for kind, source, target, place, wanted in (
            (0, send_ref.at[row], got_ref.at[odd, gj], column, True),
            (1, send_edge_ref.at[row], got_edge_ref.at[1 - odd, gj], beside, inner),
        ):
            here = (gi == row) & (gj == place)

            @pl.when(jnp.logical_not(here) & wanted)
            def _():
                pltpu.make_async_remote_copy(
                    src_ref=source,
                    dst_ref=target,
                    send_sem=send_sem.at[kind],
                    recv_sem=recv_sem.at[kind],
                    device_id=(row, place),
                    device_id_type=MESH,
                ).start()

            @pl.when(here & wanted)
            def _():
                pltpu.make_async_copy(source, target, recv_sem.at[kind]).start()

    for load in loads[1:]:
        load.wait()
    lay_out_weights(*weights, pad_ref, *made)
    blend_weights(gi, gj, margins_ref, blend_ref)
    flags = flag_rows(gi, gj, False)
    for z in range(8):
        taps_ref[80:96, 128 * z : 128 * z + 128] = flags
    taps_ref[80:96, 1024:1152] = flag_rows(gi, gj, True)


    def got(ref, kind):
        pltpu.make_async_copy(ref, ref, recv_sem.at[kind]).wait()

    got(got_ref, 0)

    @pl.when(within(gj, 1, 6))
    def _():
        got(got_edge_ref, 1)

    @pl.when(gj == 0)
    def _():
        got(got_edge_ref.at[1], 1)
        got_edge_ref[0] = jnp.zeros((8, 1, 128), F32)

    @pl.when(gj == 7)
    def _():
        got(got_edge_ref.at[0], 1)
        got_edge_ref[1] = jnp.zeros((8, 1, 128), F32)

    shift_raw(order_ref, got_ref, got_edge_ref, taps_ref)

    def sent(ref, count):
        kind = 0 if ref is send_ref else 1
        ref = ref.at[0:count]
        pltpu.make_async_copy(ref, ref, send_sem.at[kind]).wait()

    @pl.when(gj == column)
    def _():
        sent(send_ref, 15)

    @pl.when(gj != column)
    def _():
        sent(send_ref, 16)

    @pl.when(inner & (gj == beside))
    def _():
        sent(send_edge_ref, 15)

    @pl.when(inner & (gj != beside))
    def _():
        sent(send_edge_ref, 16)


ROWS = (0, 1, 3, 4, 12, 2, 5, 7, 8, 13, 15, 6, 9, 11, 14, 10)


TAPS = jax.ShapeDtypeStruct((96, 1152), BF16)
MADE = (
    jax.ShapeDtypeStruct((1280, 128), BF16),
    jax.ShapeDtypeStruct((672, 256), BF16),
    jax.ShapeDtypeStruct((656, 256), BF16),
    jax.ShapeDtypeStruct((48, 256), BF16),
    jax.ShapeDtypeStruct((48, 384), BF16),
    jax.ShapeDtypeStruct((128, 128), F32),
)
BLEND = jax.ShapeDtypeStruct((32, 128), F32)
TABLE = jax.ShapeDtypeStruct((256, 1152), BF16)


def as_they_lie(raw, section_order, margins, w_in, b_in, w_a, b_a, w_d, b_d, w_u, w_o, b_o):
    return (
        jnp.transpose(raw, (0, 2, 1)),
        section_order,
        margins.T,
        jnp.asarray(units_table()),
        w_in.T,
        b_in[None],
        w_a,
        b_a[None],
        jnp.transpose(w_d, (0, 2, 1)),
        b_d[None],
        w_u,
        w_o,
        b_o[None],
        jnp.asarray(level_table()),
    )


def exchange(*arrays):
    arrays = [pltpu.with_memory_space_constraint(x, pltpu.HBM) for x in as_they_lie(*arrays)]
    vmem = pl.BlockSpec(memory_space=pltpu.VMEM)
    places = [pltpu.SMEM if n == 1 else pltpu.VMEM for n in range(13)]
    return pl.pallas_call(
        exchange_kernel,
        out_shape=(TAPS,) + MADE + (BLEND, TABLE),
        in_specs=[pl.BlockSpec(memory_space=pltpu.HBM)] * 14,
        out_specs=(vmem,) * 9,
        scratch_shapes=[place(x.shape, x.dtype) for place, x in zip(places, arrays)]
        + [
            pltpu.VMEM((27, 32, 128), BF16),
            pltpu.VMEM((16, 8, 128), BF16),
            pltpu.VMEM((16, 1, 128), F32),
            pltpu.VMEM((2, 8, 8, 128), BF16),
            pltpu.VMEM((2, 8, 1, 128), F32),
            pltpu.SemaphoreType.DMA((14,)),
            pltpu.SemaphoreType.DMA((2,)),
            pltpu.SemaphoreType.DMA((2,)),
        ],
        compiler_params=pltpu.CompilerParams(
            collective_id=0, has_side_effects=True, vmem_limit_bytes=12 * 1024 * 1024
        ),
    )(*arrays)


def network_kernel(
    taps_ref,
    conv_in_ref,
    conv_a_ref,
    conv_d_ref,
    w_q_ref,
    w_s_ref,
    bias_ref,
    blend_ref,
    table_ref,
    out_ref,
    h_ref,
    a_ref,
    d_ref,
    e_ref,
):
    bias_a = bias_ref[0:32]
    bias_d = jnp.concatenate([bias_ref[32:72]] * 8, axis=0)
    bias_o = bias_ref[72:120]
    weight_y, weight_x, weight_xy, scale = [blend_ref[8 * n : 8 * n + 8] for n in range(4)]
    margins = slice(1024, 1152)
    lane = iota((256, 128), 1)

    def pair(q):
        return slice(256 * q, 256 * q + 256)

    def section(z):
        return slice(128 * z, 128 * z + 128)

    def wide(column, at):
        return column if at.stop - at.start == 128 else jnp.concatenate([column, column], axis=1)

    def first_level(at):
        for tile in range(5):
            h = dot(conv_in_ref[256 * tile : 256 * tile + 256, 0:96], taps_ref[:, at])
            h_ref[tile, :, at] = jnp.maximum(h.astype(BF16), 0)

    places = (0, 1, 2, 3, 4, 5, 6, 7, 8, 9, 12, 13, 10, 11)

    def products(at):
        sums = [None] * 14
        width = at.stop - at.start
        for tile, first, rows in (
            (0, 3, (0, 1, 2)),
            (1, 1, (1, 2, 3, 4, 5)),
            (2, 0, (12, 4, 5, 6, 7, 8, 13)),
            (3, 1, (7, 8, 9, 10, 11)),
            (4, 1, (10, 11)),
        ):
            product = dot(conv_a_ref[96 * first : 96 * (first + len(rows))], h_ref[tile, :, at])
            product = product.reshape(len(rows), 3, 32, width)
            for n, row in enumerate(rows):
                part = product[n]
                sums[row] = part if sums[row] is None else sums[row] + part
                if tile == 1 and row == 5:
                    sums[12] = part
        return sums

    def finish(row, at, total):
        block = (row + 1 if row < 12 else row - 6) if row != 12 else 6
        tile, nth = block // 3, block % 3
        centre = h_ref[tile, 32 * nth : 32 * nth + 32, at].astype(F32)
        a_ref[places[row], :, at] = (centre + jnp.maximum(total + bias_a, 0.0)).astype(BF16)

    def pooled_rows(at):
        even = jnp.concatenate([a_ref[n, :, at] for n in (0, 2, 4, 6, 8, 12, 4, 11)], axis=0)
        late = jnp.concatenate([a_ref[n, :, at] for n in (1, 3, 5, 7, 9, 13, 10, 7)], axis=0)
        return jnp.concatenate([even, late], axis=1)

    def keep(dx, at, value):
        d_ref[:, dx, :, at] = value.astype(BF16).reshape(8, 32, 128)

    def pool(q, ends):
        both = jnp.concatenate([pooled_rows(section(2 * q)), pooled_rows(section(2 * q + 1))], axis=0)
        d = dot(both, table_ref[:, 256:512])
        one, two = d[0:256, 0:128], pltpu.roll(d[256:512, 0:128], 64, 1)
        low = lane < 64
        keep(1, section(q), jnp.where(low, d[0:256, 128:256], pltpu.roll(d[256:512, 128:256], 64, 1)))
        end = ends if q == 0 else pltpu.roll(ends, 128 - q, 1)
        keep(0, section(q), jnp.where(lane % 64 == 0, end, jnp.where(low, one, two)))
        end = ends if q == 3 else pltpu.roll(ends, 3 - q, 1)
        moved = pltpu.roll(jnp.where(low, two, one), 64, 1)
        keep(2, section(q), jnp.where(lane % 64 == 63, end, moved))

    def coarse(at):
        d = d_ref[:, :, :, at].reshape(768, at.stop - at.start)
        one = dot(conv_d_ref[0:208], d[0:256])
        two = dot(conv_d_ref[208:448], d[256:512])
        three = dot(conv_d_ref[448:656], d[512:768])
        e = jnp.concatenate(
            [
                one[0:80] + three[0:80],
                one[80:200] + two[0:120],
                two[120:240] + three[80:200],
            ],
            axis=0,
        )
        e_ref[:, at] = jnp.maximum(e + wide(bias_d, at), 0.0).astype(BF16)

    def lifted(at, table):
        own = dot(w_q_ref[:, 0:160], e_ref[80:240, at])
        other = dot(w_q_ref[:, 0:160], jnp.concatenate([e_ref[0:80, at], e_ref[240:320, at]], axis=0))
        q = jnp.concatenate([own[0:24] + own[24:48], other[0:24] + other[24:48]], axis=0)
        high = q.astype(BF16).astype(F32)
        return dot(jnp.concatenate([high, q - high], axis=1).astype(BF16), table)

    def chances(at, up):
        s = dot(w_s_ref[:, 0:320], a_ref[2:12, :, at].reshape(320, at.stop - at.start))
        return jax.nn.sigmoid(s + up + wide(bias_o, at))

    def head(q, beyond):
        s = chances(pair(q), lifted(section(q), table_ref[:, 0:256]))
        for half in range(2):
            for o in range(3):
                own = s[8 * o : 8 * o + 8, 128 * half : 128 * half + 128]
                other = s[24 + 8 * o : 32 + 8 * o, 128 * half : 128 * half + 128]
                z = 2 * q + half
                out_ref[o, z] = fold(own + other * weight_y, beyond[o], z) * scale

    first_level(margins)
    first_level(pair(0))
    sums = products(margins)
    along = iota((32, 128), 1)
    for row in range(14):
        before, here, after = sums[row][0], sums[row][1], sums[row][2]
        before = jnp.where(along >= 16, pltpu.roll(before, 16, 1), 0.0)
        after = jnp.where(along < 112, pltpu.roll(after, 112, 1), 0.0)
        finish(row, margins, here + before + after)
    first_level(pair(1))
    previous = products(pair(0))
    d = dot(pooled_rows(margins), table_ref[:, 512:1024])
    ends = d[:, 384:512]
    for dx in range(3):
        keep(dx, slice(512, 640), d[:, 128 * dx : 128 * dx + 128])
    current = None
    beyond = None
    older = None
    for q in range(4):
        current = products(pair(q + 1)) if q < 3 else None
        for row in range(14):
            p = previous[row]
            total = p[1, :, 0:128] + p[2, :, 128:256]
            if q > 0:
                total = total + older[row][0, :, 128:256]
            finish(row, section(2 * q), total)
            total = p[1, :, 128:256] + p[0, :, 0:128]
            if q < 3:
                total = total + current[row][2, :, 0:128]
            finish(row, section(2 * q + 1), total)
        older, previous = previous, current
        if q < 2:
            first_level(pair(q + 2))
        if q == 0:
            coarse(slice(512, 640))
            beyond = chances(margins, lifted(slice(512, 640), table_ref[:, 1024:1152]))
            beyond = [
                beyond[8 * o : 8 * o + 8] * weight_x + beyond[24 + 8 * o : 32 + 8 * o] * weight_xy
                for o in range(3)
            ]
        pool(q, ends)
        if q % 2 == 1:
            coarse(slice(128 * q - 128, 128 * q + 128))
            head(q - 1, beyond)
            head(q, beyond)


def network(*made, **options):
    vmem = pl.BlockSpec(memory_space=pltpu.VMEM)
    return pl.pallas_call(
        network_kernel,
        out_shape=jax.ShapeDtypeStruct((3, 8, 8, 128), F32),
        in_specs=[vmem] * 9,
        out_specs=vmem,
        scratch_shapes=[
            pltpu.VMEM((5, 256, 1152), BF16),
            pltpu.VMEM((14, 32, 1152), BF16),
            pltpu.VMEM((8, 3, 32, 640), BF16),
            pltpu.VMEM((320, 640), BF16),
        ],
        compiler_params=pltpu.CompilerParams(vmem_limit_bytes=32 * 1024 * 1024),
        **options,
    )(*made)


def per_device(*arrays):
    return network(*exchange(*arrays))


def solution(mesh):
    placed = (P("gy", None, "gx"), P(), P(), P(), P(), P(), P(), P(), P(), P(), P(), P())
    return jax.shard_map(
        per_device, mesh=mesh, in_specs=placed, out_specs=P(None, None, "gx", "gy"), check_vma=False
    )
```

```python
import functools

import jax
import jax.numpy as jnp
import ml_dtypes
import numpy as np
from jax import lax
from jax.experimental import pallas as pl
from jax.experimental.pallas import tpu as pltpu
from jax.sharding import PartitionSpec as P

MESH = pl.DeviceIdType.MESH
F32 = jnp.float32
BF16 = jnp.bfloat16
BIG = -1e30


def iota(shape, dim):
    return lax.broadcasted_iota(jnp.int32, shape, dim)


def within(x, low, high):
    return (x >= low) & (x <= high)


def dot(a, b):
    return jnp.dot(a, b, preferred_element_type=F32)


def neighbours(gi):
    odd = lax.rem(gi, 2)
    column = lax.div(gi, 2)
    beside = lax.rem(column + 7 + 2 * odd, 8)
    return odd, column, beside


def unit_row(dx, block, channel):
    if dx == 1:
        return 32 * block + channel
    unit = 3 * (dx // 2) + block
    if unit < 5:
        return 96 + 28 * unit + channel
    return 236 + channel if channel < 20 else 8 + channel if channel < 24 else 36 + channel


def units_table():
    table = np.zeros((3, 3, 32, 256), np.float32)
    for block in range(3):
        for dx in range(3):
            for channel in range(28):
                table[block, dx, channel, unit_row(dx, block, channel)] = 1
    return table.reshape(288, 256).astype(ml_dtypes.bfloat16)


def level_table():
    spread = np.zeros((256, 256), np.float32)
    core = np.zeros((2, 128, 256), np.float32)
    side = np.zeros((2, 128, 512), np.float32)
    spread_side = np.zeros((2, 128, 128), np.float32)
    for lane in range(256):
        spread[lane // 2, lane] = spread[128 + lane // 2, lane] = 1
    for m in range(64):
        for fine in (0, 1):
            if m >= 1:
                core[:, 2 * m - 2 + fine, m] = 0.25
            if m <= 62:
                core[:, 2 * m + 2 + fine, 64 + m] = 0.25
            core[:, 2 * m + fine, 128 + m] = 0.25
    for section in range(8):
        for fine in (0, 1):
            for dx in range(3):
                for m in (0, 1):
                    left, right = m + dx - 1, 62 + m + dx - 1
                    if left <= 1:
                        side[:, 16 * section + 2 + 2 * left + fine, 128 * dx + 8 * section + 1 + m] = 0.25
                    if right >= 62:
                        side[:, 16 * section + 2 * right - 114 + fine, 128 * dx + 8 * section + 4 + m] = 0.25
            at = 384 + 64 * (section % 2) + section // 2
            side[:, 16 * section + fine, at] = 0.25
            side[:, 16 * section + 14 + fine, at + 60] = 0.25
        for x in range(4):
            spread_side[:, 8 * section + 1 + x // 2, 16 * section + 2 + x] = 1
            spread_side[:, 8 * section + 4 + x // 2, 16 * section + 10 + x] = 1
    parts = [spread, core.reshape(256, 256), side.reshape(256, 512), spread_side.reshape(256, 128)]
    return np.concatenate(parts, axis=1).astype(ml_dtypes.bfloat16)


def as_column(row, size):
    shape = (size, row.shape[1])
    return jnp.sum(jnp.where(iota(shape, 0) == iota(shape, 1), row, 0.0), axis=1, keepdims=True)


def tiled_taps(pad_ref, first, taps):
    tiles = []
    for start in range(0, taps, 4):
        tile = None
        for q in range(min(4, taps - start)):
            part = pad_ref[first + start + q].astype(F32)
            part = part if q == 0 else pltpu.roll(part, 32 * q, 1)
            tile = part if tile is None else tile + part
        tiles.append(tile)
    return jnp.concatenate(tiles, axis=1)


def lay_out_weights(
    units_ref,
    w_in_ref,
    b_in_ref,
    w_a_ref,
    b_a_ref,
    w_d_ref,
    b_d_ref,
    w_u_ref,
    w_o_ref,
    b_o_ref,
    pad_ref,
    conv_in_ref,
    conv_a_ref,
    conv_d_ref,
    w_q_ref,
    w_s_ref,
    bias_ref,
):
    pad_ref[...] = jnp.zeros_like(pad_ref)
    pad_ref[0, 0:9, 0:28] = w_in_ref[...]
    tap = iota((32, 128), 0)
    lane = iota((32, 128), 1)
    put = (lane == 16 * (tap % 3) + tap // 3) & (tap < 9)
    base = lax.dot_general(
        pad_ref[0],
        put.astype(F32).astype(BF16),
        (((0,), (0,)), ((), ())),
        preferred_element_type=F32,
    )[0:32]
    rest = as_column(b_in_ref[...], 32)
    flagged = jnp.zeros((32, 128), F32)
    for n in range(3):
        part = rest.astype(BF16).astype(F32)
        flagged = flagged + jnp.where(lane == 80 + n, part, 0.0)
        rest = rest - part
    stack = []
    for block in range(3):
        for dx in range(3):
            row = []
            for tile in range(5):
                y = 3 * tile + block
                if y > 13:
                    row.append(jnp.zeros((32, 128), F32))
                    continue
                moved = base if dx == y == 0 else pltpu.roll(base, 16 * dx + y, 1)
                off = (lane == 83 + dx) | ((lane == 86) & (y < 3)) | ((lane == 87) & (y >= 11))
                row.append(moved + flagged + jnp.where(off, BIG, 0.0))
            stack.append(jnp.concatenate(row, axis=1))
    made = lax.dot_general(
        units_ref[...],
        jnp.concatenate(stack, axis=0).astype(BF16),
        (((0,), (0,)), ((), ())),
        preferred_element_type=F32,
    ).astype(BF16)
    for tile in range(5):
        conv_in_ref[256 * tile : 256 * tile + 256] = made[:, 128 * tile : 128 * tile + 128]

    pad_ref[0] = jnp.zeros((32, 128), BF16)
    pad_ref[0:27, 0:28, 0:28] = w_a_ref[...]
    lane = iota((32, 384), 1)
    parts = [[] for _ in range(7)]
    for dz in range(3):
        taps = tiled_taps(pad_ref, 9 * dz, 9)
        for n, shift in enumerate((-1, -2, -1, 0, 1, 2, 0)):
            moved = taps if shift == 0 else pltpu.roll(taps, 96 * shift % 384, 1)
            low, high = 96 * max(shift, 0), 96 * min(3 + shift, 3)
            if n == 0:
                high = 96
            if n == 6:
                low = 96
            parts[n].append(jnp.where((lane >= low) & (lane < high), moved, 0.0))
    taps = jnp.concatenate([part for shift in parts for part in shift], axis=0).astype(BF16)
    conv_a_ref[...] = dot(taps[:, 0:288], units_ref[...]).astype(BF16)

    pad_ref[0:9] = jnp.zeros((9, 32, 128), BF16)
    pad_ref[0:9, 0:28, 0:36] = w_d_ref[...]
    taps = pad_ref[0:12].astype(F32).reshape(384, 128)
    taps = jnp.where(iota((384, 128), 0) < 288, taps, 0.0)
    taps = jnp.concatenate([taps[128 * n : 128 * n + 128].T[0:40] for n in range(3)], axis=1)
    taps = jnp.concatenate([taps, jnp.zeros((40, 384), F32)], axis=1)
    lane = iota((40, 768), 1)

    def spaced(*moves):
        total = None
        for first, dy, count in moves:
            by = 96 * (first - dy) % 768
            moved = taps if by == 0 else pltpu.roll(taps, by, 1)
            moved = jnp.where(within(lane, 96 * first, 96 * (first + count) - 1), moved, 0.0)
            total = moved if total is None else total + moved
        return total

    outs = [
        spaced((0, 0, 2), (6, 2, 1)),
        spaced((1, 0, 1), (6, 1, 1)),
        spaced((0, 0, 3)),
        spaced((1, 0, 3)),
        spaced((2, 0, 3)),
        spaced((3, 0, 3)),
        spaced((4, 2, 1), (7, 1, 1)),
        spaced((4, 1, 2), (7, 0, 1)),
    ]
    none = [jnp.zeros((8, 256), F32)]
    for at, tile, which in (
        (0, 0, (0, 1, 2, 3, 4)),
        (208, 1, (2, 3, 4, 5, 6, 7)),
        (448, 2, (0, 1, 5, 6, 7)),
    ):
        part = [outs[n][:, 256 * tile : 256 * tile + 256] for n in which]
        part = jnp.concatenate(part if tile == 1 else part + none, axis=0)
        conv_d_ref[at : at + part.shape[0]] = part.astype(BF16)

    w_o = w_o_ref[...].astype(F32)
    w_o = jnp.concatenate([jnp.broadcast_to(w_o[o : o + 1], (8, 28)) for o in range(3)], axis=0)
    w_o = jnp.concatenate([w_o, jnp.zeros((24, 4), F32)], axis=1)
    pad_ref[0] = jnp.zeros((32, 128), BF16)
    pad_ref[0, 0:28, 0:36] = w_u_ref[...]
    w_u = pad_ref[0].astype(F32)
    w_u = jnp.concatenate([w_u, jnp.zeros_like(w_u)], axis=1)
    w_u = w_u + pltpu.roll(w_u, 40, 1)
    w_u = w_u + pltpu.roll(w_u, 80, 1)
    w_q = dot(w_o.astype(BF16), w_u.astype(BF16))
    lane = iota((24, 256), 1)
    w_q = jnp.where(lane // 40 == (iota((24, 256), 0) % 8) // 2, w_q, 0.0)
    high = w_q.astype(BF16).astype(F32)
    w_q_ref[...] = jnp.concatenate([high, w_q - high], axis=0).astype(BF16)
    w_o = jnp.concatenate([w_o] * 12, axis=1)
    w_o = jnp.concatenate([w_o, w_o], axis=0)
    lane = iota((48, 384), 1) // 32
    row = iota((48, 384), 0)
    block = jnp.where(row < 24, row % 8, jnp.where(within(row % 8, 3, 4), row % 8 + 5, row % 8))
    w_s_ref[...] = jnp.where(lane == block, w_o, 0.0).astype(BF16)

    bias_ref[0:32] = jnp.broadcast_to(as_column(b_a_ref[...], 32), (32, 128))
    bias_ref[32:72] = jnp.broadcast_to(as_column(b_d_ref[...], 40), (40, 128))
    row = iota((48, 3), 0) % 24 // 8
    b_o = jnp.sum(jnp.where(row == iota((48, 3), 1), b_o_ref[...], 0.0), axis=1, keepdims=True)
    bias_ref[72:120] = jnp.broadcast_to(b_o, (48, 128))
    bias_ref[120:128] = jnp.zeros((8, 128), F32)


def fold(core, beyond, z):
    lane = iota((8, 128), 1)
    left = jnp.where(lane < 4, pltpu.roll(beyond, (126 - 16 * z) % 128, 1), 0.0)
    right = jnp.where(lane >= 124, pltpu.roll(beyond, (114 - 16 * z) % 128, 1), 0.0)
    return core + left + right


def blend_weights(gi, gj, margins_ref, blend_ref):
    margins = margins_ref[...].astype(F32)
    places = margins.shape

    def margin(step_y, step_x):
        y, x = gi + step_y, gj + step_x
        here = (iota(places, 0) == x) & (iota(places, 1) == y)
        value = jnp.sum(jnp.where(here, margins, 0.0), keepdims=True)
        return value, (y >= 0) & (y < 16) & (x >= 0) & (x < 8)

    def ramp(distance, pair):
        return jnp.clip(1.0 - distance / (pair[0] + 1.0), 0.0, 1.0) * jnp.where(pair[1], 1.0, 0.0)

    y = iota((8, 128), 0)
    lane = iota((8, 128), 1)
    upper = y < 4
    off_y = jnp.where(upper, y + 1, 8 - y).astype(F32)
    nth = lane % 16
    left = nth < 8
    off_x = jnp.where(
        within(nth, 2, 5), nth - 1, jnp.where(within(nth, 10, 13), 14 - nth, 99)
    ).astype(F32)
    m = {(a, b): margin(a, b) for a in (-1, 0, 1) for b in (-1, 0, 1) if (a, b) != (0, 0)}
    weight_y = jnp.where(upper, ramp(off_y, m[-1, 0]), ramp(off_y, m[1, 0]))
    weight_x = jnp.where(left, ramp(off_x, m[0, -1]), ramp(off_x, m[0, 1]))

    def corner(a, b):
        return ramp(off_y, m[a, b]) * ramp(off_x, m[a, b])

    weight_xy = jnp.where(
        upper,
        jnp.where(left, corner(-1, -1), corner(-1, 1)),
        jnp.where(left, corner(1, -1), corner(1, 1)),
    )
    blend_ref[0:8] = weight_y
    blend_ref[8:16] = weight_x
    blend_ref[16:24] = weight_xy
    blend_ref[24:32] = 1.0 / fold(1.0 + weight_y, weight_x + weight_xy, 0)


def flag_rows(gi, gj, side):
    kind = iota((16, 128), 0)
    lane = iota((16, 128), 1)
    dx = kind - 3
    if side:
        nth = lane % 16
        column = jnp.where(nth < 8, nth - 3 + dx, 113 + nth + dx)
        outside = column == jnp.where(nth < 8, 4, 123)
    else:
        column = lane + dx - 1
        outside = lane < 0
    outside = outside | ((column < 0) & (gj == 0)) | ((column > 127) & (gj == 7))
    value = (kind < 3) | (within(kind, 3, 5) & outside)
    value = value | ((kind == 6) & (gi == 0)) | ((kind == 7) & (gi == 15))
    return jnp.where(value, 1.0, 0.0).astype(BF16)


def shift_raw(order_ref, got_ref, got_edge_ref, taps_ref):
    lane = iota((8, 128), 1)
    tile = iota((16, 128), 1)
    sides = [jnp.zeros((16, 128), F32) for _ in range(5)]
    for z in range(8):
        slab = jnp.int32(0)
        for k in range(8):
            slab = jnp.maximum(slab, jnp.where(order_ref[k] == z, k, 0))
        near, far = [got_ref[n, slab].astype(F32) for n in range(2)]
        before, after = [jnp.broadcast_to(got_edge_ref[n, slab], (8, 128)) for n in range(2)]
        core = jnp.concatenate(
            [
                jnp.where(lane < 64, near, pltpu.roll(far, 64, 1)),
                jnp.where(lane < 64, pltpu.roll(near, 64, 1), far),
            ],
            axis=0,
        )
        before = jnp.concatenate(
            [pltpu.roll(before, n, 1, stride=16, stride_axis=0) for n in (6, 2)], axis=0
        )
        after = jnp.concatenate(
            [pltpu.roll(after, n, 1, stride=16, stride_axis=0) for n in (14, 10)], axis=0
        )
        low = jnp.where(tile < 6, pltpu.roll(core, 6, 1), after)
        high = jnp.where(tile >= 122, pltpu.roll(core, 122, 1), before)
        beside = jnp.where(tile < 64, low, high)
        for n in range(5):
            s = n - 2
            moved = core if s == 0 else pltpu.roll(core, -s % 128, 1)
            if s > 0:
                moved = jnp.where(tile >= 128 - s, pltpu.roll(beside, 122 - s, 1), moved)
            if s < 0:
                moved = jnp.where(tile < -s, pltpu.roll(beside, 6 - s, 1), moved)
            taps_ref[16 * n : 16 * n + 16, 128 * z : 128 * z + 128] = moved.astype(BF16)
            moved = pltpu.roll(beside, (16 * z + 8 - s) % 128, 1)
            sides[n] = jnp.where(tile // 16 == z, moved, sides[n])
    for n in range(5):
        taps_ref[16 * n : 16 * n + 16, 1024:1152] = sides[n].astype(BF16)


def exchange_kernel(*refs):
    hbm, refs = refs[0:14], refs[14:]
    taps_ref, made, blend_ref, table_ref, refs = refs[0], refs[1:7], refs[7], refs[8], refs[9:]
    loaded, refs = refs[0:13], refs[13:]
    pad_ref, send_ref, send_edge_ref, got_ref, got_edge_ref, load_sem, send_sem, recv_sem, mate_sem = refs
    raw_ref, order_ref, margins_ref, weights = loaded[0], loaded[1], loaded[2], loaded[3:]
    gi = lax.axis_index("gx")
    gj = lax.axis_index("gy")
    odd, column, beside = neighbours(gi)
    inner = (gi > 0) & (gi < 15)
    loads = [
        pltpu.make_async_copy(source, place, load_sem.at[n])
        for n, (source, place) in enumerate(zip(hbm, loaded + (table_ref,)))
    ]
    loads[0].start()
    barrier = pltpu.get_barrier_semaphore()

    core = lax.rem(gj, 2)
    mate = (gi, gj + 1 - 2 * core)
    group = jnp.int32(1)
    for row in SOON:
        group = jnp.where(gi == row, 0, group)

    @pl.when(core == 1)
    def _():
        pl.semaphore_signal(barrier, inc=1, device_id=mate, device_id_type=MESH)

    for chip in range(4):
        for strip in (2 * gj, 2 * gj + 1):
            peer = (strip, 2 * chip + group)
            pl.semaphore_signal(barrier, inc=1, device_id=peer, device_id_type=MESH)

    @pl.when(gj > 0)
    def _():
        for chip in range(4):
            peer = (2 * gj - 1, 2 * chip + group)
            pl.semaphore_signal(barrier, inc=1, device_id=peer, device_id_type=MESH)

    @pl.when(gj < 7)
    def _():
        for chip in range(4):
            peer = (2 * gj + 2, 2 * chip + group)
            pl.semaphore_signal(barrier, inc=1, device_id=peer, device_id_type=MESH)

    for load in loads[1:]:
        load.start()

    lane = iota((128, 256), 1)
    wanted = iota((128, 256), 0) + jnp.where(lane < 128, -4, 4)
    rows = (wanted == lane % 128).astype(F32).astype(BF16)
    lane = iota((128, 128), 1)
    nth = lane % 16 - 8 * (1 - odd)
    cols = jnp.where(within(nth, 0, 3), nth, jnp.where(within(nth, 4, 7), nth + 60, -99)) + 60 * odd
    cols = (iota((128, 128), 0) == cols).astype(F32).astype(BF16)
    own = lane // 16 == 7 - iota((128, 128), 0) % 8
    gather = (iota((16, 128), 0) == iota((16, 128), 1) // 8).astype(F32).astype(BF16)
    loads[0].wait()
    raw = raw_ref[0].astype(F32)
    none = jnp.zeros_like(raw)
    raw = jnp.concatenate(
        [jnp.concatenate([raw, none], axis=1), jnp.concatenate([none, raw], axis=1)], axis=0
    ).astype(BF16)
    message = lax.dot_general(
        rows, raw, (((1,), (1,)), ((), ())), preferred_element_type=F32
    ).astype(BF16)
    send_ref[...] = message.reshape(16, 8, 128)
    edge = dot(gather, jnp.where(own, dot(message, cols), 0.0).astype(BF16))
    for row in range(16):
        send_edge_ref[row] = edge[row : row + 1]

    soon = jnp.where(inner, 2 * len(SOON), len(SOON))
    late = jnp.where(inner, 2 * len(LATE), len(LATE))

    @pl.when(core == 0)
    def _():
        pl.semaphore_wait(barrier, soon + 1)
        pl.semaphore_signal(mate_sem, inc=1, device_id=mate, device_id_type=MESH)

    @pl.when(core == 1)
    def _():
        pl.semaphore_wait(mate_sem, 1)

    def send(row):
        for kind, source, target, place, wanted in (
            (0, send_ref.at[row], got_ref.at[odd, gj], column, True),
            (1, send_edge_ref.at[row], got_edge_ref.at[1 - odd, gj], beside, inner),
        ):
            here = (gi == row) & (gj == place)

            @pl.when(jnp.logical_not(here) & wanted)
            def _():
                pltpu.make_async_remote_copy(
                    src_ref=source,
                    dst_ref=target,
                    send_sem=send_sem.at[kind],
                    recv_sem=recv_sem.at[kind],
                    device_id=(row, place),
                    device_id_type=MESH,
                ).start()

            @pl.when(here & wanted)
            def _():
                pltpu.make_async_copy(source, target, recv_sem.at[kind]).start()

    for row in SOON:
        send(row)

    for load in loads[1:]:
        load.wait()
    lay_out_weights(*weights, pad_ref, *made)
    blend_weights(gi, gj, margins_ref, blend_ref)
    flags = flag_rows(gi, gj, False)
    for z in range(8):
        taps_ref[80:96, 128 * z : 128 * z + 128] = flags
    taps_ref[80:96, 1024:1152] = flag_rows(gi, gj, True)

    @pl.when(core == 0)
    def _():
        pl.semaphore_wait(mate_sem, 1)

    @pl.when(core == 1)
    def _():
        pl.semaphore_wait(barrier, late)
        pl.semaphore_signal(mate_sem, inc=1, device_id=mate, device_id_type=MESH)

    for row in LATE:
        send(row)

    def got(ref, kind):
        pltpu.make_async_copy(ref, ref, recv_sem.at[kind]).wait()

    got(got_ref, 0)

    @pl.when(within(gj, 1, 6))
    def _():
        got(got_edge_ref, 1)

    @pl.when(gj == 0)
    def _():
        got(got_edge_ref.at[1], 1)
        got_edge_ref[0] = jnp.zeros((8, 1, 128), F32)

    @pl.when(gj == 7)
    def _():
        got(got_edge_ref.at[0], 1)
        got_edge_ref[1] = jnp.zeros((8, 1, 128), F32)

    shift_raw(order_ref, got_ref, got_edge_ref, taps_ref)

    def sent(ref, count):
        kind = 0 if ref is send_ref else 1
        ref = ref.at[0:count]
        pltpu.make_async_copy(ref, ref, send_sem.at[kind]).wait()

    @pl.when(gj == column)
    def _():
        sent(send_ref, 15)

    @pl.when(gj != column)
    def _():
        sent(send_ref, 16)

    @pl.when(inner & (gj == beside))
    def _():
        sent(send_edge_ref, 15)

    @pl.when(inner & (gj != beside))
    def _():
        sent(send_edge_ref, 16)


ROWS = (0, 1, 4, 8, 12, 5, 2, 9, 13, 3, 6, 7, 10, 14, 11, 15)
SOON = ROWS[:5]
LATE = ROWS[5:]


TAPS = jax.ShapeDtypeStruct((96, 1152), BF16)
MADE = (
    jax.ShapeDtypeStruct((1280, 128), BF16),
    jax.ShapeDtypeStruct((672, 256), BF16),
    jax.ShapeDtypeStruct((656, 256), BF16),
    jax.ShapeDtypeStruct((48, 256), BF16),
    jax.ShapeDtypeStruct((48, 384), BF16),
    jax.ShapeDtypeStruct((128, 128), F32),
)
BLEND = jax.ShapeDtypeStruct((32, 128), F32)
TABLE = jax.ShapeDtypeStruct((256, 1152), BF16)


def as_they_lie(raw, section_order, margins, w_in, b_in, w_a, b_a, w_d, b_d, w_u, w_o, b_o):
    return (
        jnp.transpose(raw, (0, 2, 1)),
        section_order,
        margins.T,
        jnp.asarray(units_table()),
        w_in.T,
        b_in[None],
        w_a,
        b_a[None],
        jnp.transpose(w_d, (0, 2, 1)),
        b_d[None],
        w_u,
        w_o,
        b_o[None],
        jnp.asarray(level_table()),
    )


def exchange(*arrays):
    arrays = [pltpu.with_memory_space_constraint(x, pltpu.HBM) for x in as_they_lie(*arrays)]
    vmem = pl.BlockSpec(memory_space=pltpu.VMEM)
    places = [pltpu.SMEM if n == 1 else pltpu.VMEM for n in range(13)]
    return pl.pallas_call(
        exchange_kernel,
        out_shape=(TAPS,) + MADE + (BLEND, TABLE),
        in_specs=[pl.BlockSpec(memory_space=pltpu.HBM)] * 14,
        out_specs=(vmem,) * 9,
        scratch_shapes=[place(x.shape, x.dtype) for place, x in zip(places, arrays)]
        + [
            pltpu.VMEM((27, 32, 128), BF16),
            pltpu.VMEM((16, 8, 128), BF16),
            pltpu.VMEM((16, 1, 128), F32),
            pltpu.VMEM((2, 8, 8, 128), BF16),
            pltpu.VMEM((2, 8, 1, 128), F32),
            pltpu.SemaphoreType.DMA((14,)),
            pltpu.SemaphoreType.DMA((2,)),
            pltpu.SemaphoreType.DMA((2,)),
            pltpu.SemaphoreType.REGULAR,
        ],
        compiler_params=pltpu.CompilerParams(
            collective_id=0, has_side_effects=True, vmem_limit_bytes=12 * 1024 * 1024
        ),
    )(*arrays)


def network_kernel(
    taps_ref,
    conv_in_ref,
    conv_a_ref,
    conv_d_ref,
    w_q_ref,
    w_s_ref,
    bias_ref,
    blend_ref,
    table_ref,
    out_ref,
    h_ref,
    a_ref,
    d_ref,
    e_ref,
):
    bias_a = bias_ref[0:32]
    bias_d = jnp.concatenate([bias_ref[32:72]] * 8, axis=0)
    bias_o = bias_ref[72:120]
    weight_y, weight_x, weight_xy, scale = [blend_ref[8 * n : 8 * n + 8] for n in range(4)]
    margins = slice(1024, 1152)
    lane = iota((256, 128), 1)

    def pair(q):
        return slice(256 * q, 256 * q + 256)

    def section(z):
        return slice(128 * z, 128 * z + 128)

    def wide(column, at):
        return column if at.stop - at.start == 128 else jnp.concatenate([column, column], axis=1)

    def first_level(at):
        for tile in range(5):
            h = dot(conv_in_ref[256 * tile : 256 * tile + 256, 0:96], taps_ref[:, at])
            h_ref[tile, :, at] = jnp.maximum(h.astype(BF16), 0)

    places = (0, 1, 2, 3, 4, 5, 6, 7, 8, 9, 12, 13, 10, 11)

    def products(at):
        sums = [None] * 14
        width = at.stop - at.start
        for tile, first, rows in (
            (0, 3, (0, 1, 2)),
            (1, 1, (1, 2, 3, 4, 5)),
            (2, 0, (12, 4, 5, 6, 7, 8, 13)),
            (3, 1, (7, 8, 9, 10, 11)),
            (4, 1, (10, 11)),
        ):
            product = dot(conv_a_ref[96 * first : 96 * (first + len(rows))], h_ref[tile, :, at])
            product = product.reshape(len(rows), 3, 32, width)
            for n, row in enumerate(rows):
                part = product[n]
                sums[row] = part if sums[row] is None else sums[row] + part
                if tile == 1 and row == 5:
                    sums[12] = part
        return sums

    def finish(row, at, total):
        block = (row + 1 if row < 12 else row - 6) if row != 12 else 6
        tile, nth = block // 3, block % 3
        centre = h_ref[tile, 32 * nth : 32 * nth + 32, at].astype(F32)
        a_ref[places[row], :, at] = (centre + jnp.maximum(total + bias_a, 0.0)).astype(BF16)

    def pooled_rows(at):
        even = jnp.concatenate([a_ref[n, :, at] for n in (0, 2, 4, 6, 8, 12, 4, 11)], axis=0)
        late = jnp.concatenate([a_ref[n, :, at] for n in (1, 3, 5, 7, 9, 13, 10, 7)], axis=0)
        return jnp.concatenate([even, late], axis=1)

    def keep(dx, at, value):
        d_ref[:, dx, :, at] = value.astype(BF16).reshape(8, 32, 128)

    def pool(q, ends):
        both = jnp.concatenate([pooled_rows(section(2 * q)), pooled_rows(section(2 * q + 1))], axis=0)
        d = dot(both, table_ref[:, 256:512])
        one, two = d[0:256, 0:128], pltpu.roll(d[256:512, 0:128], 64, 1)
        low = lane < 64
        keep(1, section(q), jnp.where(low, d[0:256, 128:256], pltpu.roll(d[256:512, 128:256], 64, 1)))
        end = ends if q == 0 else pltpu.roll(ends, 128 - q, 1)
        keep(0, section(q), jnp.where(lane % 64 == 0, end, jnp.where(low, one, two)))
        end = ends if q == 3 else pltpu.roll(ends, 3 - q, 1)
        moved = pltpu.roll(jnp.where(low, two, one), 64, 1)
        keep(2, section(q), jnp.where(lane % 64 == 63, end, moved))

    def coarse(at):
        d = d_ref[:, :, :, at].reshape(768, at.stop - at.start)
        one = dot(conv_d_ref[0:208], d[0:256])
        two = dot(conv_d_ref[208:448], d[256:512])
        three = dot(conv_d_ref[448:656], d[512:768])
        e = jnp.concatenate(
            [
                one[0:80] + three[0:80],
                one[80:200] + two[0:120],
                two[120:240] + three[80:200],
            ],
            axis=0,
        )
        e_ref[:, at] = jnp.maximum(e + wide(bias_d, at), 0.0).astype(BF16)

    def lifted(at, table):
        own = dot(w_q_ref[:, 0:160], e_ref[80:240, at])
        other = dot(w_q_ref[:, 0:160], jnp.concatenate([e_ref[0:80, at], e_ref[240:320, at]], axis=0))
        q = jnp.concatenate([own[0:24] + own[24:48], other[0:24] + other[24:48]], axis=0)
        high = q.astype(BF16).astype(F32)
        return dot(jnp.concatenate([high, q - high], axis=1).astype(BF16), table)

    def chances(at, up):
        s = dot(w_s_ref[:, 0:320], a_ref[2:12, :, at].reshape(320, at.stop - at.start))
        return jax.nn.sigmoid(s + up + wide(bias_o, at))

    def head(q, beyond):
        s = chances(pair(q), lifted(section(q), table_ref[:, 0:256]))
        for half in range(2):
            for o in range(3):
                own = s[8 * o : 8 * o + 8, 128 * half : 128 * half + 128]
                other = s[24 + 8 * o : 32 + 8 * o, 128 * half : 128 * half + 128]
                z = 2 * q + half
                out_ref[o, z] = fold(own + other * weight_y, beyond[o], z) * scale

    first_level(margins)
    first_level(pair(0))
    sums = products(margins)
    along = iota((32, 128), 1)
    for row in range(14):
        before, here, after = sums[row][0], sums[row][1], sums[row][2]
        before = jnp.where(along >= 16, pltpu.roll(before, 16, 1), 0.0)
        after = jnp.where(along < 112, pltpu.roll(after, 112, 1), 0.0)
        finish(row, margins, here + before + after)
    first_level(pair(1))
    previous = products(pair(0))
    d = dot(pooled_rows(margins), table_ref[:, 512:1024])
    ends = d[:, 384:512]
    for dx in range(3):
        keep(dx, slice(512, 640), d[:, 128 * dx : 128 * dx + 128])
    current = None
    beyond = None
    older = None
    for q in range(4):
        current = products(pair(q + 1)) if q < 3 else None
        for row in range(14):
            p = previous[row]
            total = p[1, :, 0:128] + p[2, :, 128:256]
            if q > 0:
                total = total + older[row][0, :, 128:256]
            finish(row, section(2 * q), total)
            total = p[1, :, 128:256] + p[0, :, 0:128]
            if q < 3:
                total = total + current[row][2, :, 0:128]
            finish(row, section(2 * q + 1), total)
        older, previous = previous, current
        if q < 2:
            first_level(pair(q + 2))
        if q == 0:
            coarse(slice(512, 640))
            beyond = chances(margins, lifted(slice(512, 640), table_ref[:, 1024:1152]))
            beyond = [
                beyond[8 * o : 8 * o + 8] * weight_x + beyond[24 + 8 * o : 32 + 8 * o] * weight_xy
                for o in range(3)
            ]
        pool(q, ends)
        if q % 2 == 1:
            coarse(slice(128 * q - 128, 128 * q + 128))
            head(q - 1, beyond)
            head(q, beyond)


def network(*made, **options):
    vmem = pl.BlockSpec(memory_space=pltpu.VMEM)
    return pl.pallas_call(
        network_kernel,
        out_shape=jax.ShapeDtypeStruct((3, 8, 8, 128), F32),
        in_specs=[vmem] * 9,
        out_specs=vmem,
        scratch_shapes=[
            pltpu.VMEM((5, 256, 1152), BF16),
            pltpu.VMEM((14, 32, 1152), BF16),
            pltpu.VMEM((8, 3, 32, 640), BF16),
            pltpu.VMEM((320, 640), BF16),
        ],
        compiler_params=pltpu.CompilerParams(vmem_limit_bytes=32 * 1024 * 1024),
        **options,
    )(*made)


def per_device(*arrays):
    return network(*exchange(*arrays))


def solution(mesh):
    placed = (P("gy", None, "gx"), P(), P(), P(), P(), P(), P(), P(), P(), P(), P(), P())
    return jax.shard_map(
        per_device, mesh=mesh, in_specs=placed, out_specs=P(None, None, "gx", "gy"), check_vma=False
    )
```

```python
import functools

import jax
import jax.numpy as jnp
import ml_dtypes
import numpy as np
from jax import lax
from jax.experimental import pallas as pl
from jax.experimental.pallas import tpu as pltpu
from jax.sharding import PartitionSpec as P

MESH = pl.DeviceIdType.MESH
F32 = jnp.float32
BF16 = jnp.bfloat16
BIG = -1e30


def iota(shape, dim):
    return lax.broadcasted_iota(jnp.int32, shape, dim)


def within(x, low, high):
    return (x >= low) & (x <= high)


def dot(a, b):
    return jnp.dot(a, b, preferred_element_type=F32)


def neighbours(gi):
    odd = lax.rem(gi, 2)
    column = lax.div(gi, 2)
    beside = lax.rem(column + 7 + 2 * odd, 8)
    return odd, column, beside


def unit_row(dx, block, channel):
    if dx == 1:
        return 32 * block + channel
    unit = 3 * (dx // 2) + block
    if unit < 5:
        return 96 + 28 * unit + channel
    return 236 + channel if channel < 20 else 8 + channel if channel < 24 else 36 + channel


def units_table():
    table = np.zeros((3, 3, 32, 256), np.float32)
    for block in range(3):
        for dx in range(3):
            for channel in range(28):
                table[block, dx, channel, unit_row(dx, block, channel)] = 1
    return table.reshape(288, 256).astype(ml_dtypes.bfloat16)


def level_table():
    spread = np.zeros((256, 256), np.float32)
    core = np.zeros((2, 128, 256), np.float32)
    side = np.zeros((2, 128, 512), np.float32)
    spread_side = np.zeros((2, 128, 128), np.float32)
    for lane in range(256):
        spread[lane // 2, lane] = spread[128 + lane // 2, lane] = 1
    for m in range(64):
        for fine in (0, 1):
            if m >= 1:
                core[:, 2 * m - 2 + fine, m] = 0.25
            if m <= 62:
                core[:, 2 * m + 2 + fine, 64 + m] = 0.25
            core[:, 2 * m + fine, 128 + m] = 0.25
    for section in range(8):
        for fine in (0, 1):
            for dx in range(3):
                for m in (0, 1):
                    left, right = m + dx - 1, 62 + m + dx - 1
                    if left <= 1:
                        side[:, 16 * section + 2 + 2 * left + fine, 128 * dx + 8 * section + 1 + m] = 0.25
                    if right >= 62:
                        side[:, 16 * section + 2 * right - 114 + fine, 128 * dx + 8 * section + 4 + m] = 0.25
            at = 384 + 64 * (section % 2) + section // 2
            side[:, 16 * section + fine, at] = 0.25
            side[:, 16 * section + 14 + fine, at + 60] = 0.25
        for x in range(4):
            spread_side[:, 8 * section + 1 + x // 2, 16 * section + 2 + x] = 1
            spread_side[:, 8 * section + 4 + x // 2, 16 * section + 10 + x] = 1
    parts = [spread, core.reshape(256, 256), side.reshape(256, 512), spread_side.reshape(256, 128)]
    return np.concatenate(parts, axis=1).astype(ml_dtypes.bfloat16)


def as_column(row, size):
    shape = (size, row.shape[1])
    return jnp.sum(jnp.where(iota(shape, 0) == iota(shape, 1), row, 0.0), axis=1, keepdims=True)


def tiled_taps(pad_ref, first, taps):
    tiles = []
    for start in range(0, taps, 4):
        tile = None
        for q in range(min(4, taps - start)):
            part = pad_ref[first + start + q].astype(F32)
            part = part if q == 0 else pltpu.roll(part, 32 * q, 1)
            tile = part if tile is None else tile + part
        tiles.append(tile)
    return jnp.concatenate(tiles, axis=1)


def lay_out_weights(
    units_ref,
    w_in_ref,
    b_in_ref,
    w_a_ref,
    b_a_ref,
    w_d_ref,
    b_d_ref,
    w_u_ref,
    w_o_ref,
    b_o_ref,
    pad_ref,
    conv_in_ref,
    conv_a_ref,
    conv_d_ref,
    w_q_ref,
    w_s_ref,
    bias_ref,
):
    pad_ref[...] = jnp.zeros_like(pad_ref)
    pad_ref[0, 0:9, 0:28] = w_in_ref[...]
    tap = iota((32, 128), 0)
    lane = iota((32, 128), 1)
    put = (lane == 16 * (tap % 3) + tap // 3) & (tap < 9)
    base = lax.dot_general(
        pad_ref[0],
        put.astype(F32).astype(BF16),
        (((0,), (0,)), ((), ())),
        preferred_element_type=F32,
    )[0:32]
    rest = as_column(b_in_ref[...], 32)
    flagged = jnp.zeros((32, 128), F32)
    for n in range(3):
        part = rest.astype(BF16).astype(F32)
        flagged = flagged + jnp.where(lane == 80 + n, part, 0.0)
        rest = rest - part
    stack = []
    for block in range(3):
        for dx in range(3):
            row = []
            for tile in range(5):
                y = 3 * tile + block
                if y > 13:
                    row.append(jnp.zeros((32, 128), F32))
                    continue
                moved = base if dx == y == 0 else pltpu.roll(base, 16 * dx + y, 1)
                off = (lane == 83 + dx) | ((lane == 86) & (y < 3)) | ((lane == 87) & (y >= 11))
                row.append(moved + flagged + jnp.where(off, BIG, 0.0))
            stack.append(jnp.concatenate(row, axis=1))
    made = lax.dot_general(
        units_ref[...],
        jnp.concatenate(stack, axis=0).astype(BF16),
        (((0,), (0,)), ((), ())),
        preferred_element_type=F32,
    ).astype(BF16)
    for tile in range(5):
        conv_in_ref[256 * tile : 256 * tile + 256] = made[:, 128 * tile : 128 * tile + 128]

    pad_ref[0] = jnp.zeros((32, 128), BF16)
    pad_ref[0:27, 0:28, 0:28] = w_a_ref[...]
    lane = iota((32, 384), 1)
    parts = [[] for _ in range(7)]
    for dz in range(3):
        taps = tiled_taps(pad_ref, 9 * dz, 9)
        for n, shift in enumerate((-1, -2, -1, 0, 1, 2, 0)):
            moved = taps if shift == 0 else pltpu.roll(taps, 96 * shift % 384, 1)
            low, high = 96 * max(shift, 0), 96 * min(3 + shift, 3)
            if n == 0:
                high = 96
            if n == 6:
                low = 96
            parts[n].append(jnp.where((lane >= low) & (lane < high), moved, 0.0))
    taps = jnp.concatenate([part for shift in parts for part in shift], axis=0).astype(BF16)
    conv_a_ref[...] = dot(taps[:, 0:288], units_ref[...]).astype(BF16)

    pad_ref[0:9] = jnp.zeros((9, 32, 128), BF16)
    pad_ref[0:9, 0:28, 0:36] = w_d_ref[...]
    taps = pad_ref[0:12].astype(F32).reshape(384, 128)
    taps = jnp.where(iota((384, 128), 0) < 288, taps, 0.0)
    taps = jnp.concatenate([taps[128 * n : 128 * n + 128].T[0:40] for n in range(3)], axis=1)
    taps = jnp.concatenate([taps, jnp.zeros((40, 384), F32)], axis=1)
    lane = iota((40, 768), 1)

    def spaced(*moves):
        total = None
        for first, dy, count in moves:
            by = 96 * (first - dy) % 768
            moved = taps if by == 0 else pltpu.roll(taps, by, 1)
            moved = jnp.where(within(lane, 96 * first, 96 * (first + count) - 1), moved, 0.0)
            total = moved if total is None else total + moved
        return total

    outs = [
        spaced((0, 0, 2), (6, 2, 1)),
        spaced((1, 0, 1), (6, 1, 1)),
        spaced((0, 0, 3)),
        spaced((1, 0, 3)),
        spaced((2, 0, 3)),
        spaced((3, 0, 3)),
        spaced((4, 2, 1), (7, 1, 1)),
        spaced((4, 1, 2), (7, 0, 1)),
    ]
    none = [jnp.zeros((8, 256), F32)]
    for at, tile, which in (
        (0, 0, (0, 1, 2, 3, 4)),
        (208, 1, (2, 3, 4, 5, 6, 7)),
        (448, 2, (0, 1, 5, 6, 7)),
    ):
        part = [outs[n][:, 256 * tile : 256 * tile + 256] for n in which]
        part = jnp.concatenate(part if tile == 1 else part + none, axis=0)
        conv_d_ref[at : at + part.shape[0]] = part.astype(BF16)

    w_o = w_o_ref[...].astype(F32)
    w_o = jnp.concatenate([jnp.broadcast_to(w_o[o : o + 1], (8, 28)) for o in range(3)], axis=0)
    w_o = jnp.concatenate([w_o, jnp.zeros((24, 4), F32)], axis=1)
    pad_ref[0] = jnp.zeros((32, 128), BF16)
    pad_ref[0, 0:28, 0:36] = w_u_ref[...]
    w_u = pad_ref[0].astype(F32)
    w_u = jnp.concatenate([w_u, jnp.zeros_like(w_u)], axis=1)
    w_u = w_u + pltpu.roll(w_u, 40, 1)
    w_u = w_u + pltpu.roll(w_u, 80, 1)
    w_q = dot(w_o.astype(BF16), w_u.astype(BF16))
    lane = iota((24, 256), 1)
    w_q = jnp.where(lane // 40 == (iota((24, 256), 0) % 8) // 2, w_q, 0.0)
    high = w_q.astype(BF16).astype(F32)
    w_q_ref[...] = jnp.concatenate([high, w_q - high], axis=0).astype(BF16)
    w_o = jnp.concatenate([w_o] * 12, axis=1)
    w_o = jnp.concatenate([w_o, w_o], axis=0)
    lane = iota((48, 384), 1) // 32
    row = iota((48, 384), 0)
    block = jnp.where(row < 24, row % 8, jnp.where(within(row % 8, 3, 4), row % 8 + 5, row % 8))
    w_s_ref[...] = jnp.where(lane == block, w_o, 0.0).astype(BF16)

    bias_ref[0:32] = jnp.broadcast_to(as_column(b_a_ref[...], 32), (32, 128))
    bias_ref[32:72] = jnp.broadcast_to(as_column(b_d_ref[...], 40), (40, 128))
    row = iota((48, 3), 0) % 24 // 8
    b_o = jnp.sum(jnp.where(row == iota((48, 3), 1), b_o_ref[...], 0.0), axis=1, keepdims=True)
    bias_ref[72:120] = jnp.broadcast_to(b_o, (48, 128))
    bias_ref[120:128] = jnp.zeros((8, 128), F32)


def fold(core, beyond, z):
    lane = iota((8, 128), 1)
    left = jnp.where(lane < 4, pltpu.roll(beyond, (126 - 16 * z) % 128, 1), 0.0)
    right = jnp.where(lane >= 124, pltpu.roll(beyond, (114 - 16 * z) % 128, 1), 0.0)
    return core + left + right


def blend_weights(gi, gj, margins_ref, blend_ref):
    margins = margins_ref[...].astype(F32)
    places = margins.shape

    def margin(step_y, step_x):
        y, x = gi + step_y, gj + step_x
        here = (iota(places, 0) == x) & (iota(places, 1) == y)
        value = jnp.sum(jnp.where(here, margins, 0.0), keepdims=True)
        return value, (y >= 0) & (y < 16) & (x >= 0) & (x < 8)

    def ramp(distance, pair):
        return jnp.clip(1.0 - distance / (pair[0] + 1.0), 0.0, 1.0) * jnp.where(pair[1], 1.0, 0.0)

    y = iota((8, 128), 0)
    lane = iota((8, 128), 1)
    upper = y < 4
    off_y = jnp.where(upper, y + 1, 8 - y).astype(F32)
    nth = lane % 16
    left = nth < 8
    off_x = jnp.where(
        within(nth, 2, 5), nth - 1, jnp.where(within(nth, 10, 13), 14 - nth, 99)
    ).astype(F32)
    m = {(a, b): margin(a, b) for a in (-1, 0, 1) for b in (-1, 0, 1) if (a, b) != (0, 0)}
    weight_y = jnp.where(upper, ramp(off_y, m[-1, 0]), ramp(off_y, m[1, 0]))
    weight_x = jnp.where(left, ramp(off_x, m[0, -1]), ramp(off_x, m[0, 1]))

    def corner(a, b):
        return ramp(off_y, m[a, b]) * ramp(off_x, m[a, b])

    weight_xy = jnp.where(
        upper,
        jnp.where(left, corner(-1, -1), corner(-1, 1)),
        jnp.where(left, corner(1, -1), corner(1, 1)),
    )
    blend_ref[0:8] = weight_y
    blend_ref[8:16] = weight_x
    blend_ref[16:24] = weight_xy
    blend_ref[24:32] = 1.0 / fold(1.0 + weight_y, weight_x + weight_xy, 0)


def flag_rows(gi, gj, side):
    kind = iota((16, 128), 0)
    lane = iota((16, 128), 1)
    dx = kind - 3
    if side:
        nth = lane % 16
        column = jnp.where(nth < 8, nth - 3 + dx, 113 + nth + dx)
        outside = column == jnp.where(nth < 8, 4, 123)
    else:
        column = lane + dx - 1
        outside = lane < 0
    outside = outside | ((column < 0) & (gj == 0)) | ((column > 127) & (gj == 7))
    value = (kind < 3) | (within(kind, 3, 5) & outside)
    value = value | ((kind == 6) & (gi == 0)) | ((kind == 7) & (gi == 15))
    return jnp.where(value, 1.0, 0.0).astype(BF16)


def shift_raw(slabs, got_ref, got_edge_ref, taps_ref):
    lane = iota((8, 128), 1)
    tile = iota((16, 128), 1)
    sides = [jnp.zeros((16, 128), F32) for _ in range(5)]
    for z in range(8):
        slab = slabs[z]
        near, far = [got_ref[n, slab].astype(F32) for n in range(2)]
        before, after = [jnp.broadcast_to(got_edge_ref[n, slab], (8, 128)) for n in range(2)]
        core = jnp.concatenate(
            [
                jnp.where(lane < 64, near, pltpu.roll(far, 64, 1)),
                jnp.where(lane < 64, pltpu.roll(near, 64, 1), far),
            ],
            axis=0,
        )
        before = jnp.concatenate(
            [pltpu.roll(before, n, 1, stride=16, stride_axis=0) for n in (6, 2)], axis=0
        )
        after = jnp.concatenate(
            [pltpu.roll(after, n, 1, stride=16, stride_axis=0) for n in (14, 10)], axis=0
        )
        low = jnp.where(tile < 6, pltpu.roll(core, 6, 1), after)
        high = jnp.where(tile >= 122, pltpu.roll(core, 122, 1), before)
        beside = jnp.where(tile < 64, low, high)
        for n in range(5):
            s = n - 2
            moved = core if s == 0 else pltpu.roll(core, -s % 128, 1)
            if s > 0:
                moved = jnp.where(tile >= 128 - s, pltpu.roll(beside, 122 - s, 1), moved)
            if s < 0:
                moved = jnp.where(tile < -s, pltpu.roll(beside, 6 - s, 1), moved)
            taps_ref[16 * n : 16 * n + 16, 128 * z : 128 * z + 128] = moved.astype(BF16)
            moved = pltpu.roll(beside, (16 * z + 8 - s) % 128, 1)
            sides[n] = jnp.where(tile // 16 == z, moved, sides[n])
    for n in range(5):
        taps_ref[16 * n : 16 * n + 16, 1024:1152] = sides[n].astype(BF16)


def exchange_kernel(*refs):
    hbm, refs = refs[0:14], refs[14:]
    taps_ref, made, blend_ref, table_ref, refs = refs[0], refs[1:7], refs[7], refs[8], refs[9:]
    loaded, refs = refs[0:13], refs[13:]
    pad_ref, send_ref, send_edge_ref, got_ref, got_edge_ref, load_sem, send_sem, recv_sem, mate_sem = refs
    raw_ref, order_ref, margins_ref, weights = loaded[0], loaded[1], loaded[2], loaded[3:]
    gi = lax.axis_index("gx")
    gj = lax.axis_index("gy")
    odd, column, beside = neighbours(gi)
    inner = (gi > 0) & (gi < 15)
    loads = [
        pltpu.make_async_copy(source, place, load_sem.at[n])
        for n, (source, place) in enumerate(zip(hbm, loaded + (table_ref,)))
    ]
    loads[0].start()
    barrier = pltpu.get_barrier_semaphore()

    core = lax.rem(gj, 2)
    mate = (gi, gj + 1 - 2 * core)
    group = jnp.int32(1)
    for row in SOON:
        group = jnp.where(gi == row, 0, group)

    @pl.when(core == 1)
    def _():
        pl.semaphore_signal(barrier, inc=1, device_id=mate, device_id_type=MESH)

    for chip in range(4):
        for strip in (2 * gj, 2 * gj + 1):
            peer = (strip, 2 * chip + group)
            pl.semaphore_signal(barrier, inc=1, device_id=peer, device_id_type=MESH)

    @pl.when(gj > 0)
    def _():
        for chip in range(4):
            peer = (2 * gj - 1, 2 * chip + group)
            pl.semaphore_signal(barrier, inc=1, device_id=peer, device_id_type=MESH)

    @pl.when(gj < 7)
    def _():
        for chip in range(4):
            peer = (2 * gj + 2, 2 * chip + group)
            pl.semaphore_signal(barrier, inc=1, device_id=peer, device_id_type=MESH)

    for load in loads[1:]:
        load.start()

    lane = iota((128, 256), 1)
    wanted = iota((128, 256), 0) + jnp.where(lane < 128, -4, 4)
    rows = (wanted == lane % 128).astype(F32).astype(BF16)
    lane = iota((128, 128), 1)
    nth = lane % 16 - 8 * (1 - odd)
    cols = jnp.where(within(nth, 0, 3), nth, jnp.where(within(nth, 4, 7), nth + 60, -99)) + 60 * odd
    cols = (iota((128, 128), 0) == cols).astype(F32).astype(BF16)
    own = lane // 16 == 7 - iota((128, 128), 0) % 8
    gather = (iota((16, 128), 0) == iota((16, 128), 1) // 8).astype(F32).astype(BF16)
    loads[0].wait()
    raw = raw_ref[0].astype(F32)
    none = jnp.zeros_like(raw)
    raw = jnp.concatenate(
        [jnp.concatenate([raw, none], axis=1), jnp.concatenate([none, raw], axis=1)], axis=0
    ).astype(BF16)
    message = lax.dot_general(
        rows, raw, (((1,), (1,)), ((), ())), preferred_element_type=F32
    ).astype(BF16)
    send_ref[...] = message.reshape(16, 8, 128)
    edge = dot(gather, jnp.where(own, dot(message, cols), 0.0).astype(BF16))
    for row in range(16):
        send_edge_ref[row] = edge[row : row + 1]

    soon = jnp.where(inner, 2 * len(SOON), len(SOON))
    late = jnp.where(inner, 2 * len(LATE), len(LATE))

    @pl.when(core == 0)
    def _():
        pl.semaphore_wait(barrier, soon + 1)
        pl.semaphore_signal(mate_sem, inc=1, device_id=mate, device_id_type=MESH)

    @pl.when(core == 1)
    def _():
        pl.semaphore_wait(mate_sem, 1)

    def send(row):
        for kind, source, target, place, wanted in (
            (0, send_ref.at[row], got_ref.at[odd, gj], column, True),
            (1, send_edge_ref.at[row], got_edge_ref.at[1 - odd, gj], beside, inner),
        ):
            here = (gi == row) & (gj == place)

            @pl.when(jnp.logical_not(here) & wanted)
            def _():
                pltpu.make_async_remote_copy(
                    src_ref=source,
                    dst_ref=target,
                    send_sem=send_sem.at[kind],
                    recv_sem=recv_sem.at[kind],
                    device_id=(row, place),
                    device_id_type=MESH,
                ).start()

            @pl.when(here & wanted)
            def _():
                pltpu.make_async_copy(source, target, recv_sem.at[kind]).start()

    for row in SOON:
        send(row)

    for load in loads[1:]:
        load.wait()
    lay_out_weights(*weights, pad_ref, *made)
    blend_weights(gi, gj, margins_ref, blend_ref)
    flags = flag_rows(gi, gj, False)
    for z in range(8):
        taps_ref[80:96, 128 * z : 128 * z + 128] = flags
    taps_ref[80:96, 1024:1152] = flag_rows(gi, gj, True)

    @pl.when(core == 0)
    def _():
        pl.semaphore_wait(mate_sem, 1)

    @pl.when(core == 1)
    def _():
        pl.semaphore_wait(barrier, late)
        pl.semaphore_signal(mate_sem, inc=1, device_id=mate, device_id_type=MESH)

    for row in LATE:
        send(row)

    slabs = []
    for z in range(8):
        slab = jnp.int32(0)
        for k in range(8):
            slab = jnp.maximum(slab, jnp.where(order_ref[k] == z, k, 0))
        slabs.append(slab)

    def got(ref, kind):
        pltpu.make_async_copy(ref, ref, recv_sem.at[kind]).wait()

    got(got_ref, 0)

    @pl.when(within(gj, 1, 6))
    def _():
        got(got_edge_ref, 1)

    @pl.when(gj == 0)
    def _():
        got(got_edge_ref.at[1], 1)
        got_edge_ref[0] = jnp.zeros((8, 1, 128), F32)

    @pl.when(gj == 7)
    def _():
        got(got_edge_ref.at[0], 1)
        got_edge_ref[1] = jnp.zeros((8, 1, 128), F32)

    shift_raw(slabs, got_ref, got_edge_ref, taps_ref)

    def sent(ref, count):
        kind = 0 if ref is send_ref else 1
        ref = ref.at[0:count]
        pltpu.make_async_copy(ref, ref, send_sem.at[kind]).wait()

    @pl.when(gj == column)
    def _():
        sent(send_ref, 15)

    @pl.when(gj != column)
    def _():
        sent(send_ref, 16)

    @pl.when(inner & (gj == beside))
    def _():
        sent(send_edge_ref, 15)

    @pl.when(inner & (gj != beside))
    def _():
        sent(send_edge_ref, 16)


ROWS = (0, 1, 4, 8, 12, 5, 2, 9, 13, 3, 6, 7, 10, 14, 11, 15)
SOON = ROWS[:5]
LATE = ROWS[5:]


TAPS = jax.ShapeDtypeStruct((96, 1152), BF16)
MADE = (
    jax.ShapeDtypeStruct((1280, 128), BF16),
    jax.ShapeDtypeStruct((672, 256), BF16),
    jax.ShapeDtypeStruct((656, 256), BF16),
    jax.ShapeDtypeStruct((48, 256), BF16),
    jax.ShapeDtypeStruct((48, 384), BF16),
    jax.ShapeDtypeStruct((128, 128), F32),
)
BLEND = jax.ShapeDtypeStruct((32, 128), F32)
TABLE = jax.ShapeDtypeStruct((256, 1152), BF16)


def as_they_lie(raw, section_order, margins, w_in, b_in, w_a, b_a, w_d, b_d, w_u, w_o, b_o):
    return (
        jnp.transpose(raw, (0, 2, 1)),
        section_order,
        margins.T,
        jnp.asarray(units_table()),
        w_in.T,
        b_in[None],
        w_a,
        b_a[None],
        jnp.transpose(w_d, (0, 2, 1)),
        b_d[None],
        w_u,
        w_o,
        b_o[None],
        jnp.asarray(level_table()),
    )


def exchange(*arrays):
    arrays = [pltpu.with_memory_space_constraint(x, pltpu.HBM) for x in as_they_lie(*arrays)]
    vmem = pl.BlockSpec(memory_space=pltpu.VMEM)
    places = [pltpu.SMEM if n == 1 else pltpu.VMEM for n in range(13)]
    return pl.pallas_call(
        exchange_kernel,
        out_shape=(TAPS,) + MADE + (BLEND, TABLE),
        in_specs=[pl.BlockSpec(memory_space=pltpu.HBM)] * 14,
        out_specs=(vmem,) * 9,
        scratch_shapes=[place(x.shape, x.dtype) for place, x in zip(places, arrays)]
        + [
            pltpu.VMEM((27, 32, 128), BF16),
            pltpu.VMEM((16, 8, 128), BF16),
            pltpu.VMEM((16, 1, 128), F32),
            pltpu.VMEM((2, 8, 8, 128), BF16),
            pltpu.VMEM((2, 8, 1, 128), F32),
            pltpu.SemaphoreType.DMA((14,)),
            pltpu.SemaphoreType.DMA((2,)),
            pltpu.SemaphoreType.DMA((2,)),
            pltpu.SemaphoreType.REGULAR,
        ],
        compiler_params=pltpu.CompilerParams(
            collective_id=0, has_side_effects=True, vmem_limit_bytes=12 * 1024 * 1024
        ),
    )(*arrays)


def network_kernel(
    taps_ref,
    conv_in_ref,
    conv_a_ref,
    conv_d_ref,
    w_q_ref,
    w_s_ref,
    bias_ref,
    blend_ref,
    table_ref,
    out_ref,
    h_ref,
    a_ref,
    d_ref,
    e_ref,
):
    bias_a = bias_ref[0:32]
    bias_d = jnp.concatenate([bias_ref[32:72]] * 8, axis=0)
    bias_o = bias_ref[72:120]
    weight_y, weight_x, weight_xy, scale = [blend_ref[8 * n : 8 * n + 8] for n in range(4)]
    margins = slice(1024, 1152)

    def pair(q):
        return slice(256 * q, 256 * q + 256)

    def section(z):
        return slice(128 * z, 128 * z + 128)

    def wide(column, at):
        return column if at.stop - at.start == 128 else jnp.concatenate([column, column], axis=1)

    def first_level(at):
        h = dot(conv_in_ref[:, 0:96], taps_ref[:, at]).astype(BF16)
        h_ref[:, :, at] = jnp.maximum(h, 0).reshape(5, 256, at.stop - at.start)

    places = (0, 1, 2, 3, 4, 5, 6, 7, 8, 9, 12, 13, 10, 11)

    tiles = (
        (3, (0, 1, 2), (0,)),
        (1, (1, 2, 3, 4, 5), (1, 2, 3)),
        (0, (12, 4, 5, 6, 7, 8, 13), (4, 5, 6, 12, 13)),
        (1, (7, 8, 9, 10, 11), (7, 8, 9)),
        (1, (10, 11), (10, 11)),
    )

    def products(tile, at, sums):
        first, rows, _ = tiles[tile]
        product = dot(conv_a_ref[96 * first : 96 * (first + len(rows))], h_ref[tile, :, at])
        product = product.reshape(len(rows), 3, 32, at.stop - at.start)
        for n, row in enumerate(rows):
            part = product[n]
            sums[row] = sums[row] + part if row in sums else part
            if tile == 1 and row == 5:
                sums[12] = part

    def finish(row, at, total):
        block = (row + 1 if row < 12 else row - 6) if row != 12 else 6
        tile, nth = block // 3, block % 3
        centre = h_ref[tile, 32 * nth : 32 * nth + 32, at].astype(F32)
        a_ref[places[row], :, at] = (centre + jnp.maximum(total + bias_a, 0.0)).astype(BF16)

    def pooled_rows(at):
        even = jnp.concatenate([a_ref[n, :, at] for n in (0, 2, 4, 6, 8, 12, 4, 11)], axis=0)
        late = jnp.concatenate([a_ref[n, :, at] for n in (1, 3, 5, 7, 9, 13, 10, 7)], axis=0)
        return jnp.concatenate([even, late], axis=1)

    def keep(dx, at, value):
        d_ref[:, dx, :, at] = value.astype(BF16).reshape(8, 32, 128)

    def pool(q):
        both = jnp.concatenate([pooled_rows(section(2 * q)), pooled_rows(section(2 * q + 1))], axis=0)
        return dot(both, table_ref[:, 256:512])

    def pooled(q, d, ends):
        lane = iota((32, 128), 1)
        low = lane < 64
        for block in range(8):
            rows, more = slice(32 * block, 32 * block + 32), slice(256 + 32 * block, 288 + 32 * block)
            one, two = d[rows, 0:128], pltpu.roll(d[more, 0:128], 64, 1)
            end = ends[rows]
            before = end if q == 0 else pltpu.roll(end, 128 - q, 1)
            after = end if q == 3 else pltpu.roll(end, 3 - q, 1)
            moved = pltpu.roll(jnp.where(low, two, one), 64, 1)
            for dx, value in (
                (0, jnp.where(lane % 64 == 0, before, jnp.where(low, one, two))),
                (1, jnp.where(low, d[rows, 128:256], pltpu.roll(d[more, 128:256], 64, 1))),
                (2, jnp.where(lane % 64 == 63, after, moved)),
            ):
                d_ref[block, dx, :, section(q)] = value.astype(BF16)

    def coarse(at):
        d = d_ref[:, :, :, at].reshape(768, at.stop - at.start)
        one = dot(conv_d_ref[0:208], d[0:256])
        two = dot(conv_d_ref[208:448], d[256:512])
        three = dot(conv_d_ref[448:656], d[512:768])
        return one, two, three

    def coarsened(at, parts):
        one, two, three = parts
        e = jnp.concatenate(
            [
                one[0:80] + three[0:80],
                one[80:200] + two[0:120],
                two[120:240] + three[80:200],
            ],
            axis=0,
        )
        e_ref[:, at] = jnp.maximum(e + wide(bias_d, at), 0.0).astype(BF16)

    def lift(at):
        own = dot(w_q_ref[:, 0:160], e_ref[80:240, at])
        other = dot(w_q_ref[:, 0:160], jnp.concatenate([e_ref[0:80, at], e_ref[240:320, at]], axis=0))
        return own, other

    def spread(parts, table):
        own, other = parts
        q = jnp.concatenate([own[0:24] + own[24:48], other[0:24] + other[24:48]], axis=0)
        high = q.astype(BF16).astype(F32)
        return dot(jnp.concatenate([high, q - high], axis=1).astype(BF16), table)

    def fine(at):
        s = dot(w_s_ref[:, 0:320], a_ref[2:12, :, at].reshape(320, at.stop - at.start))
        return s + wide(bias_o, at)

    def blend(q, s, beyond):
        s = jax.nn.sigmoid(s)
        for half in range(2):
            for o in range(3):
                own = s[8 * o : 8 * o + 8, 128 * half : 128 * half + 128]
                other = s[24 + 8 * o : 32 + 8 * o, 128 * half : 128 * half + 128]
                z = 2 * q + half
                out_ref[o, z] = fold(own + other * weight_y, beyond[o], z) * scale

    first_level(margins)
    first_level(pair(0))
    sums = {}
    along = iota((32, 128), 1)

    def finish_margins(tile):
        for row in tiles[tile][2]:
            before, here, after = sums[row][0], sums[row][1], sums[row][2]
            before = jnp.where(along >= 16, pltpu.roll(before, 16, 1), 0.0)
            after = jnp.where(along < 112, pltpu.roll(after, 112, 1), 0.0)
            finish(row, margins, here + before + after)

    for tile in range(5):
        products(tile, margins, sums)
        if tile > 0:
            finish_margins(tile - 1)
    first_level(pair(1))
    finish_margins(4)

    p = [{}, {}, {}, {}]

    def finish_sections(q, tile):
        for row in tiles[tile][2]:
            here = p[q][row]
            if q > 0:
                last = p[q - 1][row]
                total = last[1, :, 128:256] + last[0, :, 0:128] + here[2, :, 0:128]
                finish(row, section(2 * q - 1), total)
            total = here[1, :, 0:128] + here[2, :, 128:256]
            if q > 0:
                total = total + p[q - 1][row][0, :, 128:256]
            finish(row, section(2 * q), total)
            if q == 3:
                finish(row, section(7), here[1, :, 128:256] + here[0, :, 0:128])

    def residual(q, beside):
        for tile in range(5):
            products(tile, pair(q), p[q])
            if tile > 0:
                finish_sections(q, tile - 1)
            for task in beside[tile : tile + 1]:
                task()

    got = {}

    def margins_pool():
        got["side"] = dot(pooled_rows(margins), table_ref[:, 512:1024])

    def margins_pooled():
        for dx in range(3):
            keep(dx, slice(512, 640), got["side"][:, 128 * dx : 128 * dx + 128])
        got["ends"] = got["side"][:, 384:512]

    def margins_coarse():
        got["e"] = coarse(slice(512, 640))
        got["fine"] = fine(margins)

    def margins_coarsened():
        coarsened(slice(512, 640), got["e"])

    def margins_lift():
        got["q"] = lift(slice(512, 640))

    def margins_spread():
        got["up"] = spread(got["q"], table_ref[:, 1024:1152])

    def margins_done():
        s = jax.nn.sigmoid(got["fine"] + got["up"])
        got["beyond"] = [
            s[8 * o : 8 * o + 8] * weight_x + s[24 + 8 * o : 32 + 8 * o] * weight_xy
            for o in range(3)
        ]

    def pool_of(q):
        def task():
            got["pool", q] = pool(q)

        return task

    def pooled_of(q):
        return lambda: pooled(q, got["pool", q], got["ends"])

    def fine_of(q):
        def task():
            got["fine", q] = fine(pair(q))

        return task

    low, high = slice(0, 256), slice(256, 512)

    def low_coarse():
        got["e", 0] = coarse(low)

    def low_lift():
        coarsened(low, got["e", 0])
        got["q", 0], got["q", 1] = lift(section(0)), lift(section(1))

    residual(0, [margins_pool, margins_pooled, margins_coarse, margins_coarsened, margins_lift])
    first_level(pair(2))
    finish_sections(0, 4)
    residual(1, [margins_spread, margins_done])
    first_level(pair(3))
    finish_sections(1, 4)
    residual(2, [pool_of(0), pooled_of(0), fine_of(0)])
    finish_sections(2, 4)
    residual(3, [pool_of(1), pooled_of(1), fine_of(1), low_coarse, low_lift])
    finish_sections(3, 4)
    pool_of(2)()
    pool_of(3)()
    got["up", 0] = spread(got["q", 0], table_ref[:, 0:256])
    got["up", 1] = spread(got["q", 1], table_ref[:, 0:256])
    pooled_of(2)()
    got["e", 1] = coarse(section(2))
    fine_of(2)()
    pooled_of(3)()
    coarsened(section(2), got["e", 1])
    got["e", 1] = coarse(section(3))
    fine_of(3)()
    blend(0, got["fine", 0] + got["up", 0], got["beyond"])
    coarsened(section(3), got["e", 1])
    got["q", 2], got["q", 3] = lift(section(2)), lift(section(3))
    blend(1, got["fine", 1] + got["up", 1], got["beyond"])
    got["up", 2] = spread(got["q", 2], table_ref[:, 0:256])
    got["up", 3] = spread(got["q", 3], table_ref[:, 0:256])
    blend(2, got["fine", 2] + got["up", 2], got["beyond"])
    blend(3, got["fine", 3] + got["up", 3], got["beyond"])


def network(*made, **options):
    vmem = pl.BlockSpec(memory_space=pltpu.VMEM)
    return pl.pallas_call(
        network_kernel,
        out_shape=jax.ShapeDtypeStruct((3, 8, 8, 128), F32),
        in_specs=[vmem] * 9,
        out_specs=vmem,
        scratch_shapes=[
            pltpu.VMEM((5, 256, 1152), BF16),
            pltpu.VMEM((14, 32, 1152), BF16),
            pltpu.VMEM((8, 3, 32, 640), BF16),
            pltpu.VMEM((320, 640), BF16),
        ],
        compiler_params=pltpu.CompilerParams(vmem_limit_bytes=32 * 1024 * 1024),
        **options,
    )(*made)


def per_device(*arrays):
    return network(*exchange(*arrays))


def solution(mesh):
    placed = (P("gy", None, "gx"), P(), P(), P(), P(), P(), P(), P(), P(), P(), P(), P())
    return jax.shard_map(
        per_device, mesh=mesh, in_specs=placed, out_specs=P(None, None, "gx", "gy"), check_vma=False
    )
```

```python
import functools

import jax
import jax.numpy as jnp
import ml_dtypes
import numpy as np
from jax import lax
from jax.experimental import pallas as pl
from jax.experimental.pallas import tpu as pltpu
from jax.sharding import PartitionSpec as P

MESH = pl.DeviceIdType.MESH
F32 = jnp.float32
BF16 = jnp.bfloat16
BIG = -1e30


def iota(shape, dim):
    return lax.broadcasted_iota(jnp.int32, shape, dim)


def within(x, low, high):
    return (x >= low) & (x <= high)


def dot(a, b):
    return jnp.dot(a, b, preferred_element_type=F32)


def neighbours(gi):
    odd = lax.rem(gi, 2)
    column = lax.div(gi, 2)
    beside = lax.rem(column + 7 + 2 * odd, 8)
    return odd, column, beside


def unit_row(dx, block, channel):
    if dx == 1:
        return 32 * block + channel
    unit = 3 * (dx // 2) + block
    if unit < 5:
        return 96 + 28 * unit + channel
    return 236 + channel if channel < 20 else 8 + channel if channel < 24 else 36 + channel


def units_table():
    table = np.zeros((3, 3, 32, 256), np.float32)
    for block in range(3):
        for dx in range(3):
            for channel in range(28):
                table[block, dx, channel, unit_row(dx, block, channel)] = 1
    return table.reshape(288, 256).astype(ml_dtypes.bfloat16)


def level_table():
    spread = np.zeros((256, 256), np.float32)
    core = np.zeros((2, 128, 256), np.float32)
    side = np.zeros((2, 128, 512), np.float32)
    spread_side = np.zeros((2, 128, 128), np.float32)
    for lane in range(256):
        spread[lane // 2, lane] = spread[128 + lane // 2, lane] = 1
    for m in range(64):
        for fine in (0, 1):
            if m >= 1:
                core[:, 2 * m - 2 + fine, m] = 0.25
            if m <= 62:
                core[:, 2 * m + 2 + fine, 64 + m] = 0.25
            core[:, 2 * m + fine, 128 + m] = 0.25
    for section in range(8):
        for fine in (0, 1):
            for dx in range(3):
                for m in (0, 1):
                    left, right = m + dx - 1, 62 + m + dx - 1
                    if left <= 1:
                        side[:, 16 * section + 2 + 2 * left + fine, 128 * dx + 8 * section + 1 + m] = 0.25
                    if right >= 62:
                        side[:, 16 * section + 2 * right - 114 + fine, 128 * dx + 8 * section + 4 + m] = 0.25
            at = 384 + 64 * (section % 2) + section // 2
            side[:, 16 * section + fine, at] = 0.25
            side[:, 16 * section + 14 + fine, at + 60] = 0.25
        for x in range(4):
            spread_side[:, 8 * section + 1 + x // 2, 16 * section + 2 + x] = 1
            spread_side[:, 8 * section + 4 + x // 2, 16 * section + 10 + x] = 1
    parts = [spread, core.reshape(256, 256), side.reshape(256, 512), spread_side.reshape(256, 128)]
    return np.concatenate(parts, axis=1).astype(ml_dtypes.bfloat16)


def as_column(row, size):
    shape = (size, row.shape[1])
    return jnp.sum(jnp.where(iota(shape, 0) == iota(shape, 1), row, 0.0), axis=1, keepdims=True)


def tiled_taps(pad_ref, first, taps):
    tiles = []
    for start in range(0, taps, 4):
        tile = None
        for q in range(min(4, taps - start)):
            part = pad_ref[first + start + q].astype(F32)
            part = part if q == 0 else pltpu.roll(part, 32 * q, 1)
            tile = part if tile is None else tile + part
        tiles.append(tile)
    return jnp.concatenate(tiles, axis=1)


def lay_out_weights(
    units_ref,
    w_in_ref,
    b_in_ref,
    w_a_ref,
    b_a_ref,
    w_d_ref,
    b_d_ref,
    w_u_ref,
    w_o_ref,
    b_o_ref,
    pad_ref,
    conv_in_ref,
    conv_a_ref,
    conv_d_ref,
    w_q_ref,
    w_s_ref,
    bias_ref,
):
    pad_ref[...] = jnp.zeros_like(pad_ref)
    pad_ref[0, 0:9, 0:28] = w_in_ref[...]
    tap = iota((32, 128), 0)
    lane = iota((32, 128), 1)
    put = (lane == 16 * (tap % 3) + tap // 3) & (tap < 9)
    base = lax.dot_general(
        pad_ref[0],
        put.astype(F32).astype(BF16),
        (((0,), (0,)), ((), ())),
        preferred_element_type=F32,
    )[0:32]
    rest = as_column(b_in_ref[...], 32)
    flagged = jnp.zeros((32, 128), F32)
    for n in range(3):
        part = rest.astype(BF16).astype(F32)
        flagged = flagged + jnp.where(lane == 80 + n, part, 0.0)
        rest = rest - part
    stack = []
    for block in range(3):
        for dx in range(3):
            row = []
            for tile in range(5):
                y = 3 * tile + block
                if y > 13:
                    row.append(jnp.zeros((32, 128), F32))
                    continue
                moved = base if dx == y == 0 else pltpu.roll(base, 16 * dx + y, 1)
                off = (lane == 83 + dx) | ((lane == 86) & (y < 3)) | ((lane == 87) & (y >= 11))
                row.append(moved + flagged + jnp.where(off, BIG, 0.0))
            stack.append(jnp.concatenate(row, axis=1))
    made = lax.dot_general(
        units_ref[...],
        jnp.concatenate(stack, axis=0).astype(BF16),
        (((0,), (0,)), ((), ())),
        preferred_element_type=F32,
    )
    ones = within(iota((256, 640), 0), 92, 94) & (iota((256, 640), 1) % 128 == 80)
    made = jnp.where(ones, 1.0, made).astype(BF16)
    for tile in range(5):
        conv_in_ref[256 * tile : 256 * tile + 256] = made[:, 128 * tile : 128 * tile + 128]

    pad_ref[0] = jnp.zeros((32, 128), BF16)
    pad_ref[0:27, 0:28, 0:28] = w_a_ref[...]
    lane = iota((32, 384), 1)
    parts = [[] for _ in range(7)]
    for dz in range(3):
        taps = tiled_taps(pad_ref, 9 * dz, 9)
        for n, shift in enumerate((-1, -2, -1, 0, 1, 2, 0)):
            moved = taps if shift == 0 else pltpu.roll(taps, 96 * shift % 384, 1)
            low, high = 96 * max(shift, 0), 96 * min(3 + shift, 3)
            if n == 0:
                high = 96
            if n == 6:
                low = 96
            parts[n].append(jnp.where((lane >= low) & (lane < high), moved, 0.0))
    taps = jnp.concatenate([part for shift in parts for part in shift], axis=0).astype(BF16)
    made = dot(taps[:, 0:288], units_ref[...])
    rest = as_column(b_a_ref[...], 32)
    lane = iota((32, 256), 1)
    bias = jnp.zeros((32, 256), F32)
    for n in range(3):
        part = rest.astype(BF16).astype(F32)
        bias = bias + jnp.where(lane == 92 + n, part, 0.0)
        rest = rest - part
    none = jnp.zeros((32, 256), F32)
    once = jnp.concatenate([none, bias, none], axis=0)
    none = jnp.concatenate([none] * 9, axis=0)
    conv_a_ref[...] = (made + jnp.concatenate([none, once, once, once, once], axis=0)).astype(BF16)

    pad_ref[0:9] = jnp.zeros((9, 32, 128), BF16)
    pad_ref[0:9, 0:28, 0:36] = w_d_ref[...]
    taps = pad_ref[0:12].astype(F32).reshape(384, 128)
    taps = jnp.where(iota((384, 128), 0) < 288, taps, 0.0)
    taps = jnp.concatenate([taps[128 * n : 128 * n + 128].T[0:40] for n in range(3)], axis=1)
    taps = jnp.concatenate([taps, jnp.zeros((40, 384), F32)], axis=1)
    lane = iota((40, 768), 1)

    def spaced(*moves):
        total = None
        for first, dy, count in moves:
            by = 96 * (first - dy) % 768
            moved = taps if by == 0 else pltpu.roll(taps, by, 1)
            moved = jnp.where(within(lane, 96 * first, 96 * (first + count) - 1), moved, 0.0)
            total = moved if total is None else total + moved
        return total

    outs = [
        spaced((0, 0, 2), (6, 2, 1)),
        spaced((1, 0, 1), (6, 1, 1)),
        spaced((0, 0, 3)),
        spaced((1, 0, 3)),
        spaced((2, 0, 3)),
        spaced((3, 0, 3)),
        spaced((4, 2, 1), (7, 1, 1)),
        spaced((4, 1, 2), (7, 0, 1)),
    ]
    none = [jnp.zeros((8, 256), F32)]
    for at, tile, which in (
        (0, 0, (0, 1, 2, 3, 4)),
        (208, 1, (2, 3, 4, 5, 6, 7)),
        (448, 2, (0, 1, 5, 6, 7)),
    ):
        part = [outs[n][:, 256 * tile : 256 * tile + 256] for n in which]
        part = jnp.concatenate(part if tile == 1 else part + none, axis=0)
        conv_d_ref[at : at + part.shape[0]] = part.astype(BF16)

    w_o = w_o_ref[...].astype(F32)
    w_o = jnp.concatenate([jnp.broadcast_to(w_o[o : o + 1], (8, 28)) for o in range(3)], axis=0)
    w_o = jnp.concatenate([w_o, jnp.zeros((24, 4), F32)], axis=1)
    pad_ref[0] = jnp.zeros((32, 128), BF16)
    pad_ref[0, 0:28, 0:36] = w_u_ref[...]
    w_u = pad_ref[0].astype(F32)
    w_u = jnp.concatenate([w_u, jnp.zeros_like(w_u)], axis=1)
    w_u = w_u + pltpu.roll(w_u, 40, 1)
    w_u = w_u + pltpu.roll(w_u, 80, 1)
    w_q = dot(w_o.astype(BF16), w_u.astype(BF16))
    lane = iota((24, 256), 1)
    w_q = jnp.where(lane // 40 == (iota((24, 256), 0) % 8) // 2, w_q, 0.0)
    high = w_q.astype(BF16).astype(F32)
    w_q_ref[...] = jnp.concatenate([high, w_q - high], axis=0).astype(BF16)
    w_o = jnp.concatenate([w_o] * 12, axis=1)
    w_o = jnp.concatenate([w_o, w_o], axis=0)
    lane = iota((48, 384), 1) // 32
    row = iota((48, 384), 0)
    block = jnp.where(row < 24, row % 8, jnp.where(within(row % 8, 3, 4), row % 8 + 5, row % 8))
    w_s_ref[...] = jnp.where(lane == block, w_o, 0.0).astype(BF16)

    bias_ref[0:32] = jnp.zeros((32, 128), F32)
    bias_ref[32:72] = jnp.broadcast_to(as_column(b_d_ref[...], 40), (40, 128))
    row = iota((48, 3), 0) % 24 // 8
    b_o = jnp.sum(jnp.where(row == iota((48, 3), 1), b_o_ref[...], 0.0), axis=1, keepdims=True)
    bias_ref[72:120] = jnp.broadcast_to(b_o, (48, 128))
    bias_ref[120:128] = jnp.zeros((8, 128), F32)


def fold(core, beyond, z):
    lane = iota((8, 128), 1)
    left = jnp.where(lane < 4, pltpu.roll(beyond, (126 - 16 * z) % 128, 1), 0.0)
    right = jnp.where(lane >= 124, pltpu.roll(beyond, (114 - 16 * z) % 128, 1), 0.0)
    return core + left + right


def blend_weights(gi, gj, margins_ref, blend_ref):
    margins = margins_ref[...].astype(F32)
    places = margins.shape

    def margin(step_y, step_x):
        y, x = gi + step_y, gj + step_x
        here = (iota(places, 0) == x) & (iota(places, 1) == y)
        value = jnp.sum(jnp.where(here, margins, 0.0), keepdims=True)
        return value, (y >= 0) & (y < 16) & (x >= 0) & (x < 8)

    def ramp(distance, pair):
        return jnp.clip(1.0 - distance / (pair[0] + 1.0), 0.0, 1.0) * jnp.where(pair[1], 1.0, 0.0)

    y = iota((8, 128), 0)
    lane = iota((8, 128), 1)
    upper = y < 4
    off_y = jnp.where(upper, y + 1, 8 - y).astype(F32)
    nth = lane % 16
    left = nth < 8
    off_x = jnp.where(
        within(nth, 2, 5), nth - 1, jnp.where(within(nth, 10, 13), 14 - nth, 99)
    ).astype(F32)
    m = {(a, b): margin(a, b) for a in (-1, 0, 1) for b in (-1, 0, 1) if (a, b) != (0, 0)}
    weight_y = jnp.where(upper, ramp(off_y, m[-1, 0]), ramp(off_y, m[1, 0]))
    weight_x = jnp.where(left, ramp(off_x, m[0, -1]), ramp(off_x, m[0, 1]))

    def corner(a, b):
        return ramp(off_y, m[a, b]) * ramp(off_x, m[a, b])

    weight_xy = jnp.where(
        upper,
        jnp.where(left, corner(-1, -1), corner(-1, 1)),
        jnp.where(left, corner(1, -1), corner(1, 1)),
    )
    blend_ref[0:8] = weight_y
    blend_ref[8:16] = weight_x
    blend_ref[16:24] = weight_xy
    blend_ref[24:32] = 1.0 / fold(1.0 + weight_y, weight_x + weight_xy, 0)


def flag_rows(gi, gj, side):
    kind = iota((16, 128), 0)
    lane = iota((16, 128), 1)
    dx = kind - 3
    if side:
        nth = lane % 16
        column = jnp.where(nth < 8, nth - 3 + dx, 113 + nth + dx)
        outside = column == jnp.where(nth < 8, 4, 123)
    else:
        column = lane + dx - 1
        outside = lane < 0
    outside = outside | ((column < 0) & (gj == 0)) | ((column > 127) & (gj == 7))
    value = (kind < 3) | (within(kind, 3, 5) & outside)
    value = value | ((kind == 6) & (gi == 0)) | ((kind == 7) & (gi == 15))
    return jnp.where(value, 1.0, 0.0).astype(BF16)


def shift_raw(slabs, got_ref, got_edge_ref, taps_ref):
    lane = iota((8, 128), 1)
    tile = iota((16, 128), 1)
    sides = [jnp.zeros((16, 128), F32) for _ in range(5)]
    for z in range(8):
        slab = slabs[z]
        near, far = [got_ref[n, slab].astype(F32) for n in range(2)]
        before, after = [jnp.broadcast_to(got_edge_ref[n, slab], (8, 128)) for n in range(2)]
        core = jnp.concatenate(
            [
                jnp.where(lane < 64, near, pltpu.roll(far, 64, 1)),
                jnp.where(lane < 64, pltpu.roll(near, 64, 1), far),
            ],
            axis=0,
        )
        before = jnp.concatenate(
            [pltpu.roll(before, n, 1, stride=16, stride_axis=0) for n in (6, 2)], axis=0
        )
        after = jnp.concatenate(
            [pltpu.roll(after, n, 1, stride=16, stride_axis=0) for n in (14, 10)], axis=0
        )
        low = jnp.where(tile < 6, pltpu.roll(core, 6, 1), after)
        high = jnp.where(tile >= 122, pltpu.roll(core, 122, 1), before)
        beside = jnp.where(tile < 64, low, high)
        for n in range(5):
            s = n - 2
            moved = core if s == 0 else pltpu.roll(core, -s % 128, 1)
            if s > 0:
                moved = jnp.where(tile >= 128 - s, pltpu.roll(beside, 122 - s, 1), moved)
            if s < 0:
                moved = jnp.where(tile < -s, pltpu.roll(beside, 6 - s, 1), moved)
            taps_ref[16 * n : 16 * n + 16, 128 * z : 128 * z + 128] = moved.astype(BF16)
            moved = pltpu.roll(beside, (16 * z + 8 - s) % 128, 1)
            sides[n] = jnp.where(tile // 16 == z, moved, sides[n])
    for n in range(5):
        taps_ref[16 * n : 16 * n + 16, 1024:1152] = sides[n].astype(BF16)


def exchange_kernel(*refs):
    hbm, refs = refs[0:14], refs[14:]
    taps_ref, made, blend_ref, table_ref, refs = refs[0], refs[1:7], refs[7], refs[8], refs[9:]
    loaded, refs = refs[0:13], refs[13:]
    pad_ref, send_ref, send_edge_ref, got_ref, got_edge_ref, load_sem, send_sem, recv_sem, mate_sem = refs
    raw_ref, order_ref, margins_ref, weights = loaded[0], loaded[1], loaded[2], loaded[3:]
    gi = lax.axis_index("gx")
    gj = lax.axis_index("gy")
    odd, column, beside = neighbours(gi)
    inner = (gi > 0) & (gi < 15)
    loads = [
        pltpu.make_async_copy(source, place, load_sem.at[n])
        for n, (source, place) in enumerate(zip(hbm, loaded + (table_ref,)))
    ]
    loads[0].start()
    barrier = pltpu.get_barrier_semaphore()

    core = lax.rem(gj, 2)
    mate = (gi, gj + 1 - 2 * core)
    group = jnp.int32(1)
    for row in SOON:
        group = jnp.where(gi == row, 0, group)

    @pl.when(core == 1)
    def _():
        pl.semaphore_signal(barrier, inc=1, device_id=mate, device_id_type=MESH)

    for chip in range(4):
        for strip in (2 * gj, 2 * gj + 1):
            peer = (strip, 2 * chip + group)
            pl.semaphore_signal(barrier, inc=1, device_id=peer, device_id_type=MESH)

    @pl.when(gj > 0)
    def _():
        for chip in range(4):
            peer = (2 * gj - 1, 2 * chip + group)
            pl.semaphore_signal(barrier, inc=1, device_id=peer, device_id_type=MESH)

    @pl.when(gj < 7)
    def _():
        for chip in range(4):
            peer = (2 * gj + 2, 2 * chip + group)
            pl.semaphore_signal(barrier, inc=1, device_id=peer, device_id_type=MESH)

    for load in loads[1:]:
        load.start()

    lane = iota((128, 256), 1)
    wanted = iota((128, 256), 0) + jnp.where(lane < 128, -4, 4)
    rows = (wanted == lane % 128).astype(F32).astype(BF16)
    lane = iota((128, 128), 1)
    nth = lane % 16 - 8 * (1 - odd)
    cols = jnp.where(within(nth, 0, 3), nth, jnp.where(within(nth, 4, 7), nth + 60, -99)) + 60 * odd
    cols = (iota((128, 128), 0) == cols).astype(F32).astype(BF16)
    own = lane // 16 == 7 - iota((128, 128), 0) % 8
    gather = (iota((16, 128), 0) == iota((16, 128), 1) // 8).astype(F32).astype(BF16)
    loads[0].wait()
    raw = raw_ref[0].astype(F32)
    none = jnp.zeros_like(raw)
    raw = jnp.concatenate(
        [jnp.concatenate([raw, none], axis=1), jnp.concatenate([none, raw], axis=1)], axis=0
    ).astype(BF16)
    message = lax.dot_general(
        rows, raw, (((1,), (1,)), ((), ())), preferred_element_type=F32
    ).astype(BF16)
    send_ref[...] = message.reshape(16, 8, 128)
    edge = dot(gather, jnp.where(own, dot(message, cols), 0.0).astype(BF16))
    for row in range(16):
        send_edge_ref[row] = edge[row : row + 1]

    soon = jnp.where(inner, 2 * len(SOON), len(SOON))
    late = jnp.where(inner, 2 * len(LATE), len(LATE))

    @pl.when(core == 0)
    def _():
        pl.semaphore_wait(barrier, soon + 1)
        pl.semaphore_signal(mate_sem, inc=1, device_id=mate, device_id_type=MESH)

    @pl.when(core == 1)
    def _():
        pl.semaphore_wait(mate_sem, 1)

    def send(row):
        for kind, source, target, place, wanted in (
            (0, send_ref.at[row], got_ref.at[odd, gj], column, True),
            (1, send_edge_ref.at[row], got_edge_ref.at[1 - odd, gj], beside, inner),
        ):
            here = (gi == row) & (gj == place)

            @pl.when(jnp.logical_not(here) & wanted)
            def _():
                pltpu.make_async_remote_copy(
                    src_ref=source,
                    dst_ref=target,
                    send_sem=send_sem.at[kind],
                    recv_sem=recv_sem.at[kind],
                    device_id=(row, place),
                    device_id_type=MESH,
                ).start()

            @pl.when(here & wanted)
            def _():
                pltpu.make_async_copy(source, target, recv_sem.at[kind]).start()

    for row in SOON:
        send(row)

    for load in loads[1:]:
        load.wait()
    lay_out_weights(*weights, pad_ref, *made)
    blend_weights(gi, gj, margins_ref, blend_ref)
    flags = flag_rows(gi, gj, False)
    for z in range(8):
        taps_ref[80:96, 128 * z : 128 * z + 128] = flags
    taps_ref[80:96, 1024:1152] = flag_rows(gi, gj, True)

    @pl.when(core == 0)
    def _():
        pl.semaphore_wait(mate_sem, 1)

    @pl.when(core == 1)
    def _():
        pl.semaphore_wait(barrier, late)
        pl.semaphore_signal(mate_sem, inc=1, device_id=mate, device_id_type=MESH)

    for row in LATE:
        send(row)

    slabs = []
    for z in range(8):
        slab = jnp.int32(0)
        for k in range(8):
            slab = jnp.maximum(slab, jnp.where(order_ref[k] == z, k, 0))
        slabs.append(slab)

    def got(ref, kind):
        pltpu.make_async_copy(ref, ref, recv_sem.at[kind]).wait()

    got(got_ref, 0)

    @pl.when(within(gj, 1, 6))
    def _():
        got(got_edge_ref, 1)

    @pl.when(gj == 0)
    def _():
        got(got_edge_ref.at[1], 1)
        got_edge_ref[0] = jnp.zeros((8, 1, 128), F32)

    @pl.when(gj == 7)
    def _():
        got(got_edge_ref.at[0], 1)
        got_edge_ref[1] = jnp.zeros((8, 1, 128), F32)

    shift_raw(slabs, got_ref, got_edge_ref, taps_ref)

    def sent(ref, count):
        kind = 0 if ref is send_ref else 1
        ref = ref.at[0:count]
        pltpu.make_async_copy(ref, ref, send_sem.at[kind]).wait()

    @pl.when(gj == column)
    def _():
        sent(send_ref, 15)

    @pl.when(gj != column)
    def _():
        sent(send_ref, 16)

    @pl.when(inner & (gj == beside))
    def _():
        sent(send_edge_ref, 15)

    @pl.when(inner & (gj != beside))
    def _():
        sent(send_edge_ref, 16)


ROWS = (0, 1, 4, 8, 12, 2, 3, 5, 9, 13, 6, 7, 10, 14, 11, 15)
SOON = ROWS[:5]
LATE = ROWS[5:]


TAPS = jax.ShapeDtypeStruct((96, 1152), BF16)
MADE = (
    jax.ShapeDtypeStruct((1280, 128), BF16),
    jax.ShapeDtypeStruct((672, 256), BF16),
    jax.ShapeDtypeStruct((656, 256), BF16),
    jax.ShapeDtypeStruct((48, 256), BF16),
    jax.ShapeDtypeStruct((48, 384), BF16),
    jax.ShapeDtypeStruct((128, 128), F32),
)
BLEND = jax.ShapeDtypeStruct((32, 128), F32)
TABLE = jax.ShapeDtypeStruct((256, 1152), BF16)


def as_they_lie(raw, section_order, margins, w_in, b_in, w_a, b_a, w_d, b_d, w_u, w_o, b_o):
    return (
        jnp.transpose(raw, (0, 2, 1)),
        section_order,
        margins.T,
        jnp.asarray(units_table()),
        w_in.T,
        b_in[None],
        w_a,
        b_a[None],
        jnp.transpose(w_d, (0, 2, 1)),
        b_d[None],
        w_u,
        w_o,
        b_o[None],
        jnp.asarray(level_table()),
    )


def exchange(*arrays):
    arrays = [pltpu.with_memory_space_constraint(x, pltpu.HBM) for x in as_they_lie(*arrays)]
    vmem = pl.BlockSpec(memory_space=pltpu.VMEM)
    places = [pltpu.SMEM if n == 1 else pltpu.VMEM for n in range(13)]
    return pl.pallas_call(
        exchange_kernel,
        out_shape=(TAPS,) + MADE + (BLEND, TABLE),
        in_specs=[pl.BlockSpec(memory_space=pltpu.HBM)] * 14,
        out_specs=(vmem,) * 9,
        scratch_shapes=[place(x.shape, x.dtype) for place, x in zip(places, arrays)]
        + [
            pltpu.VMEM((27, 32, 128), BF16),
            pltpu.VMEM((16, 8, 128), BF16),
            pltpu.VMEM((16, 1, 128), F32),
            pltpu.VMEM((2, 8, 8, 128), BF16),
            pltpu.VMEM((2, 8, 1, 128), F32),
            pltpu.SemaphoreType.DMA((14,)),
            pltpu.SemaphoreType.DMA((2,)),
            pltpu.SemaphoreType.DMA((2,)),
            pltpu.SemaphoreType.REGULAR,
        ],
        compiler_params=pltpu.CompilerParams(
            collective_id=0, has_side_effects=True, vmem_limit_bytes=12 * 1024 * 1024
        ),
    )(*arrays)


def network_kernel(
    taps_ref,
    conv_in_ref,
    conv_a_ref,
    conv_d_ref,
    w_q_ref,
    w_s_ref,
    bias_ref,
    blend_ref,
    table_ref,
    out_ref,
    h_ref,
    a_ref,
    d_ref,
    e_ref,
):
    bias_d = jnp.concatenate([bias_ref[32:72]] * 8, axis=0)
    bias_o = bias_ref[72:120]
    weight_y, weight_x, weight_xy, scale = [blend_ref[8 * n : 8 * n + 8] for n in range(4)]
    margins = slice(1024, 1152)

    def pair(q):
        return slice(256 * q, 256 * q + 256)

    def section(z):
        return slice(128 * z, 128 * z + 128)

    def wide(column, at):
        return column if at.stop - at.start == 128 else jnp.concatenate([column, column], axis=1)

    def first_level(at):
        h = dot(conv_in_ref[:, 0:96], taps_ref[:, at]).astype(BF16)
        h_ref[:, :, at] = jnp.maximum(h, 0).reshape(5, 256, at.stop - at.start)

    places = (0, 1, 2, 3, 4, 5, 6, 7, 8, 9, 12, 13, 10, 11)

    tiles = (
        (3, (0, 1, 2), (0,)),
        (1, (1, 2, 3, 4, 5), (1, 2, 3)),
        (0, (12, 4, 5, 6, 7, 8, 13), (4, 5, 6, 12, 13)),
        (1, (7, 8, 9, 10, 11), (7, 8, 9)),
        (1, (10, 11), (10, 11)),
    )

    def products(tile, at, sums):
        first, rows, _ = tiles[tile]
        product = dot(conv_a_ref[96 * first : 96 * (first + len(rows))], h_ref[tile, :, at])
        product = product.reshape(len(rows), 3, 32, at.stop - at.start)
        for n, row in enumerate(rows):
            part = product[n]
            sums[row] = sums[row] + part if row in sums else part
            if tile == 1 and row == 5:
                sums[12] = part

    def finish(row, at, total):
        block = (row + 1 if row < 12 else row - 6) if row != 12 else 6
        tile, nth = block // 3, block % 3
        centre = h_ref[tile, 32 * nth : 32 * nth + 32, at].astype(F32)
        a_ref[places[row], :, at] = (centre + jnp.maximum(total, 0.0)).astype(BF16)

    def pooled_rows(at):
        even = jnp.concatenate([a_ref[n, :, at] for n in (0, 2, 4, 6, 8, 12, 4, 11)], axis=0)
        late = jnp.concatenate([a_ref[n, :, at] for n in (1, 3, 5, 7, 9, 13, 10, 7)], axis=0)
        return jnp.concatenate([even, late], axis=1)

    def keep(dx, at, value):
        d_ref[:, dx, :, at] = value.astype(BF16).reshape(8, 32, 128)

    def pool(q):
        both = jnp.concatenate([pooled_rows(section(2 * q)), pooled_rows(section(2 * q + 1))], axis=0)
        return dot(both, table_ref[:, 256:512])

    def pooled(q, d, ends):
        lane = iota((32, 128), 1)
        low = lane < 64
        for block in range(8):
            rows, more = slice(32 * block, 32 * block + 32), slice(256 + 32 * block, 288 + 32 * block)
            one, two = d[rows, 0:128], pltpu.roll(d[more, 0:128], 64, 1)
            end = ends[rows]
            before = end if q == 0 else pltpu.roll(end, 128 - q, 1)
            after = end if q == 3 else pltpu.roll(end, 3 - q, 1)
            moved = pltpu.roll(jnp.where(low, two, one), 64, 1)
            for dx, value in (
                (0, jnp.where(lane % 64 == 0, before, jnp.where(low, one, two))),
                (1, jnp.where(low, d[rows, 128:256], pltpu.roll(d[more, 128:256], 64, 1))),
                (2, jnp.where(lane % 64 == 63, after, moved)),
            ):
                d_ref[block, dx, :, section(q)] = value.astype(BF16)

    def coarse(at):
        d = d_ref[:, :, :, at].reshape(768, at.stop - at.start)
        one = dot(conv_d_ref[0:208], d[0:256])
        two = dot(conv_d_ref[208:448], d[256:512])
        three = dot(conv_d_ref[448:656], d[512:768])
        return one, two, three

    def coarsened(at, parts):
        one, two, three = parts
        e = jnp.concatenate(
            [
                one[0:80] + three[0:80],
                one[80:200] + two[0:120],
                two[120:240] + three[80:200],
            ],
            axis=0,
        )
        e_ref[:, at] = jnp.maximum(e + wide(bias_d, at), 0.0).astype(BF16)

    def lift(at):
        own = dot(w_q_ref[:, 0:160], e_ref[80:240, at])
        other = dot(w_q_ref[:, 0:160], jnp.concatenate([e_ref[0:80, at], e_ref[240:320, at]], axis=0))
        return own, other

    def spread(parts, table):
        own, other = parts
        q = jnp.concatenate([own[0:24] + own[24:48], other[0:24] + other[24:48]], axis=0)
        high = q.astype(BF16).astype(F32)
        low = q - high
        rows = [
            jnp.concatenate([high[:, at : at + 128], low[:, at : at + 128]], axis=1)
            for at in range(0, q.shape[1], 128)
        ]
        return dot(jnp.concatenate(rows, axis=0).astype(BF16), table)

    def fine(at):
        s = dot(w_s_ref[:, 0:320], a_ref[2:12, :, at].reshape(320, at.stop - at.start))
        return s + wide(bias_o, at)

    def blend(q, s, beyond):
        s = jax.nn.sigmoid(s)
        for half in range(2):
            for o in range(3):
                own = s[8 * o : 8 * o + 8, 128 * half : 128 * half + 128]
                other = s[24 + 8 * o : 32 + 8 * o, 128 * half : 128 * half + 128]
                z = 2 * q + half
                out_ref[o, z] = fold(own + other * weight_y, beyond[o], z) * scale

    first_level(margins)
    first_level(pair(0))
    sums = {}
    along = iota((32, 128), 1)

    def finish_margins(tile):
        for row in tiles[tile][2]:
            before, here, after = sums[row][0], sums[row][1], sums[row][2]
            before = jnp.where(along >= 16, pltpu.roll(before, 16, 1), 0.0)
            after = jnp.where(along < 112, pltpu.roll(after, 112, 1), 0.0)
            finish(row, margins, here + before + after)

    for tile in range(5):
        products(tile, margins, sums)
        if tile > 0:
            finish_margins(tile - 1)
    first_level(pair(1))
    finish_margins(4)

    p = [{}, {}, {}, {}]

    def finish_sections(q, tile):
        for row in tiles[tile][2]:
            here = p[q][row]
            if q > 0:
                last = p[q - 1][row]
                total = last[1, :, 128:256] + last[0, :, 0:128] + here[2, :, 0:128]
                finish(row, section(2 * q - 1), total)
            total = here[1, :, 0:128] + here[2, :, 128:256]
            if q > 0:
                total = total + p[q - 1][row][0, :, 128:256]
            finish(row, section(2 * q), total)
            if q == 3:
                finish(row, section(7), here[1, :, 128:256] + here[0, :, 0:128])

    def residual(q, beside):
        for tile in range(5):
            products(tile, pair(q), p[q])
            if tile > 0:
                finish_sections(q, tile - 1)
            for task in beside[tile : tile + 1]:
                task()

    got = {}

    def margins_pool():
        got["side"] = dot(pooled_rows(margins), table_ref[:, 512:1024])

    def margins_pooled():
        for dx in range(3):
            keep(dx, slice(512, 640), got["side"][:, 128 * dx : 128 * dx + 128])
        got["ends"] = got["side"][:, 384:512]

    def margins_coarse():
        got["e"] = coarse(slice(512, 640))
        got["fine"] = fine(margins)

    def margins_coarsened():
        coarsened(slice(512, 640), got["e"])

    def margins_lift():
        got["q"] = lift(slice(512, 640))

    def margins_spread():
        got["up"] = spread(got["q"], table_ref[:, 1024:1152])

    def margins_done():
        s = jax.nn.sigmoid(got["fine"] + got["up"])
        got["beyond"] = [
            s[8 * o : 8 * o + 8] * weight_x + s[24 + 8 * o : 32 + 8 * o] * weight_xy
            for o in range(3)
        ]

    def pool_of(q):
        def task():
            got["pool", q] = pool(q)

        return task

    def pooled_of(q):
        return lambda: pooled(q, got["pool", q], got["ends"])

    def fine_of(q):
        def task():
            got["fine", q] = fine(pair(q))

        return task

    low, high = slice(0, 256), slice(256, 512)

    def low_coarse():
        got["e", 0] = coarse(low)

    def low_lift():
        coarsened(low, got["e", 0])
        got["q", 0] = lift(low)

    residual(0, [margins_pool, margins_pooled, margins_coarse, margins_coarsened, margins_lift])
    first_level(pair(2))
    finish_sections(0, 4)
    residual(1, [margins_spread, margins_done])
    first_level(pair(3))
    finish_sections(1, 4)
    residual(2, [pool_of(0), pooled_of(0), fine_of(0)])
    finish_sections(2, 4)
    residual(3, [pool_of(1), pooled_of(1), fine_of(1), low_coarse, low_lift])
    finish_sections(3, 4)
    pool_of(2)()
    pool_of(3)()
    up = spread(got["q", 0], table_ref[:, 0:256])
    got["up", 0], got["up", 1] = up[0:48], up[48:96]
    pooled_of(2)()
    got["e", 1] = coarse(section(2))
    fine_of(2)()
    pooled_of(3)()
    coarsened(section(2), got["e", 1])
    got["e", 1] = coarse(section(3))
    fine_of(3)()
    blend(0, got["fine", 0] + got["up", 0], got["beyond"])
    coarsened(section(3), got["e", 1])
    got["q", 1] = lift(high)
    blend(1, got["fine", 1] + got["up", 1], got["beyond"])
    up = spread(got["q", 1], table_ref[:, 0:256])
    got["up", 2], got["up", 3] = up[0:48], up[48:96]
    blend(2, got["fine", 2] + got["up", 2], got["beyond"])
    blend(3, got["fine", 3] + got["up", 3], got["beyond"])


def network(*made, **options):
    vmem = pl.BlockSpec(memory_space=pltpu.VMEM)
    return pl.pallas_call(
        network_kernel,
        out_shape=jax.ShapeDtypeStruct((3, 8, 8, 128), F32),
        in_specs=[vmem] * 9,
        out_specs=vmem,
        scratch_shapes=[
            pltpu.VMEM((5, 256, 1152), BF16),
            pltpu.VMEM((14, 32, 1152), BF16),
            pltpu.VMEM((8, 3, 32, 640), BF16),
            pltpu.VMEM((320, 640), BF16),
        ],
        compiler_params=pltpu.CompilerParams(vmem_limit_bytes=32 * 1024 * 1024),
        **options,
    )(*made)


def per_device(*arrays):
    return network(*exchange(*arrays))


def solution(mesh):
    placed = (P("gy", None, "gx"), P(), P(), P(), P(), P(), P(), P(), P(), P(), P(), P())
    return jax.shard_map(
        per_device, mesh=mesh, in_specs=placed, out_specs=P(None, None, "gx", "gy"), check_vma=False
    )
```

```python
import functools

import jax
import jax.numpy as jnp
import ml_dtypes
import numpy as np
from jax import lax
from jax.experimental import pallas as pl
from jax.experimental.pallas import tpu as pltpu
from jax.sharding import PartitionSpec as P

MESH = pl.DeviceIdType.MESH
F32 = jnp.float32
BF16 = jnp.bfloat16
BIG = -1e30


def iota(shape, dim):
    return lax.broadcasted_iota(jnp.int32, shape, dim)


def within(x, low, high):
    return (x >= low) & (x <= high)


def dot(a, b):
    return jnp.dot(a, b, preferred_element_type=F32)


def neighbours(gi):
    odd = lax.rem(gi, 2)
    column = lax.div(gi, 2)
    beside = lax.rem(column + 7 + 2 * odd, 8)
    return odd, column, beside


def unit_row(dx, block, channel):
    if dx == 1:
        return 32 * block + channel
    unit = 3 * (dx // 2) + block
    if unit < 5:
        return 96 + 28 * unit + channel
    return 236 + channel if channel < 20 else 8 + channel if channel < 24 else 36 + channel


def units_table():
    table = np.zeros((3, 3, 32, 256), np.float32)
    for block in range(3):
        for dx in range(3):
            for channel in range(28):
                table[block, dx, channel, unit_row(dx, block, channel)] = 1
    return table.reshape(288, 256).astype(ml_dtypes.bfloat16)


def level_table():
    spread = np.zeros((256, 256), np.float32)
    core = np.zeros((2, 128, 256), np.float32)
    side = np.zeros((2, 128, 512), np.float32)
    spread_side = np.zeros((2, 128, 128), np.float32)
    for lane in range(256):
        spread[lane // 2, lane] = spread[128 + lane // 2, lane] = 1
    for m in range(64):
        for fine in (0, 1):
            if m >= 1:
                core[:, 2 * m - 2 + fine, m] = 0.25
            if m <= 62:
                core[:, 2 * m + 2 + fine, 64 + m] = 0.25
            core[:, 2 * m + fine, 128 + m] = 0.25
    for section in range(8):
        for fine in (0, 1):
            for dx in range(3):
                for m in (0, 1):
                    left, right = m + dx - 1, 62 + m + dx - 1
                    if left <= 1:
                        side[:, 16 * section + 2 + 2 * left + fine, 128 * dx + 8 * section + 1 + m] = 0.25
                    if right >= 62:
                        side[:, 16 * section + 2 * right - 114 + fine, 128 * dx + 8 * section + 4 + m] = 0.25
            at = 384 + 64 * (section % 2) + section // 2
            side[:, 16 * section + fine, at] = 0.25
            side[:, 16 * section + 14 + fine, at + 60] = 0.25
        for x in range(4):
            spread_side[:, 8 * section + 1 + x // 2, 16 * section + 2 + x] = 1
            spread_side[:, 8 * section + 4 + x // 2, 16 * section + 10 + x] = 1
    parts = [spread, core.reshape(256, 256), side.reshape(256, 512), spread_side.reshape(256, 128)]
    return np.concatenate(parts, axis=1).astype(ml_dtypes.bfloat16)


def as_column(row, size):
    shape = (size, row.shape[1])
    return jnp.sum(jnp.where(iota(shape, 0) == iota(shape, 1), row, 0.0), axis=1, keepdims=True)


def tiled_taps(pad_ref, first, taps):
    tiles = []
    for start in range(0, taps, 4):
        tile = None
        for q in range(min(4, taps - start)):
            part = pad_ref[first + start + q].astype(F32)
            part = part if q == 0 else pltpu.roll(part, 32 * q, 1)
            tile = part if tile is None else tile + part
        tiles.append(tile)
    return jnp.concatenate(tiles, axis=1)


def lay_out_weights(
    units_ref,
    w_in_ref,
    b_in_ref,
    w_a_ref,
    b_a_ref,
    w_d_ref,
    b_d_ref,
    w_u_ref,
    w_o_ref,
    b_o_ref,
    pad_ref,
    conv_in_ref,
    conv_a_ref,
    conv_d_ref,
    w_q_ref,
    w_s_ref,
    bias_ref,
):
    pad_ref[...] = jnp.zeros_like(pad_ref)
    pad_ref[0, 0:9, 0:28] = w_in_ref[...]
    tap = iota((32, 128), 0)
    lane = iota((32, 128), 1)
    put = (lane == 16 * (tap % 3) + tap // 3) & (tap < 9)
    base = lax.dot_general(
        pad_ref[0],
        put.astype(F32).astype(BF16),
        (((0,), (0,)), ((), ())),
        preferred_element_type=F32,
    )[0:32]
    rest = as_column(b_in_ref[...], 32)
    flagged = jnp.zeros((32, 128), F32)
    for n in range(3):
        part = rest.astype(BF16).astype(F32)
        flagged = flagged + jnp.where(lane == 80 + n, part, 0.0)
        rest = rest - part
    stack = []
    for block in range(3):
        for dx in range(3):
            row = []
            for tile in range(5):
                y = 3 * tile + block
                if y > 13:
                    row.append(jnp.zeros((32, 128), F32))
                    continue
                moved = base if dx == y == 0 else pltpu.roll(base, 16 * dx + y, 1)
                off = (lane == 83 + dx) | ((lane == 86) & (y < 3)) | ((lane == 87) & (y >= 11))
                row.append(moved + flagged + jnp.where(off, BIG, 0.0))
            stack.append(jnp.concatenate(row, axis=1))
    made = lax.dot_general(
        units_ref[...],
        jnp.concatenate(stack, axis=0).astype(BF16),
        (((0,), (0,)), ((), ())),
        preferred_element_type=F32,
    )
    ones = within(iota((256, 640), 0), 92, 94) & (iota((256, 640), 1) % 128 == 80)
    made = jnp.where(ones, 1.0, made).astype(BF16)
    for tile in range(5):
        conv_in_ref[256 * tile : 256 * tile + 256] = made[:, 128 * tile : 128 * tile + 128]

    pad_ref[0] = jnp.zeros((32, 128), BF16)
    pad_ref[0:27, 0:28, 0:28] = w_a_ref[...]
    lane = iota((32, 384), 1)
    parts = [[] for _ in range(7)]
    for dz in range(3):
        taps = tiled_taps(pad_ref, 9 * dz, 9)
        for n, shift in enumerate((-1, -2, -1, 0, 1, 2, 0)):
            moved = taps if shift == 0 else pltpu.roll(taps, 96 * shift % 384, 1)
            low, high = 96 * max(shift, 0), 96 * min(3 + shift, 3)
            if n == 0:
                high = 96
            if n == 6:
                low = 96
            parts[n].append(jnp.where((lane >= low) & (lane < high), moved, 0.0))
    taps = jnp.concatenate([part for shift in parts for part in shift], axis=0).astype(BF16)
    made = dot(taps[:, 0:288], units_ref[...])
    rest = as_column(b_a_ref[...], 32)
    lane = iota((32, 256), 1)
    bias = jnp.zeros((32, 256), F32)
    for n in range(3):
        part = rest.astype(BF16).astype(F32)
        bias = bias + jnp.where(lane == 92 + n, part, 0.0)
        rest = rest - part
    none = jnp.zeros((32, 256), F32)
    once = jnp.concatenate([none, bias, none], axis=0)
    none = jnp.concatenate([none] * 9, axis=0)
    conv_a_ref[...] = (made + jnp.concatenate([none, once, once, once, once], axis=0)).astype(BF16)

    pad_ref[0:9] = jnp.zeros((9, 32, 128), BF16)
    pad_ref[0:9, 0:28, 0:36] = w_d_ref[...]
    taps = pad_ref[0:12].astype(F32).reshape(384, 128)
    taps = jnp.where(iota((384, 128), 0) < 288, taps, 0.0)
    taps = jnp.concatenate([taps[128 * n : 128 * n + 128].T[0:40] for n in range(3)], axis=1)
    taps = jnp.concatenate([taps, jnp.zeros((40, 384), F32)], axis=1)
    lane = iota((40, 768), 1)

    def spaced(*moves):
        total = None
        for first, dy, count in moves:
            by = 96 * (first - dy) % 768
            moved = taps if by == 0 else pltpu.roll(taps, by, 1)
            moved = jnp.where(within(lane, 96 * first, 96 * (first + count) - 1), moved, 0.0)
            total = moved if total is None else total + moved
        return total

    outs = [
        spaced((0, 0, 2), (6, 2, 1)),
        spaced((1, 0, 1), (6, 1, 1)),
        spaced((0, 0, 3)),
        spaced((1, 0, 3)),
        spaced((2, 0, 3)),
        spaced((3, 0, 3)),
        spaced((4, 2, 1), (7, 1, 1)),
        spaced((4, 1, 2), (7, 0, 1)),
    ]
    none = [jnp.zeros((8, 256), F32)]
    for at, tile, which in (
        (0, 0, (0, 1, 2, 3, 4)),
        (208, 1, (2, 3, 4, 5, 6, 7)),
        (448, 2, (0, 1, 5, 6, 7)),
    ):
        part = [outs[n][:, 256 * tile : 256 * tile + 256] for n in which]
        part = jnp.concatenate(part if tile == 1 else part + none, axis=0)
        conv_d_ref[at : at + part.shape[0]] = part.astype(BF16)

    w_o = w_o_ref[...].astype(F32)
    w_o = jnp.concatenate([jnp.broadcast_to(w_o[o : o + 1], (8, 28)) for o in range(3)], axis=0)
    w_o = jnp.concatenate([w_o, jnp.zeros((24, 4), F32)], axis=1)
    pad_ref[0] = jnp.zeros((32, 128), BF16)
    pad_ref[0, 0:28, 0:36] = w_u_ref[...]
    w_u = pad_ref[0].astype(F32)
    w_u = jnp.concatenate([w_u, jnp.zeros_like(w_u)], axis=1)
    w_u = w_u + pltpu.roll(w_u, 40, 1)
    w_u = w_u + pltpu.roll(w_u, 80, 1)
    w_q = dot(w_o.astype(BF16), w_u.astype(BF16))
    lane = iota((24, 256), 1)
    w_q = jnp.where(lane // 40 == (iota((24, 256), 0) % 8) // 2, w_q, 0.0)
    high = w_q.astype(BF16).astype(F32)
    w_q_ref[...] = jnp.concatenate([high, w_q - high], axis=0).astype(BF16)
    w_o = jnp.concatenate([w_o] * 12, axis=1)
    w_o = jnp.concatenate([w_o, w_o], axis=0)
    lane = iota((48, 384), 1) // 32
    row = iota((48, 384), 0)
    block = jnp.where(row < 24, row % 8, jnp.where(within(row % 8, 3, 4), row % 8 + 5, row % 8))
    w_s_ref[...] = jnp.where(lane == block, w_o, 0.0).astype(BF16)

    bias_ref[0:32] = jnp.zeros((32, 128), F32)
    bias_ref[32:72] = jnp.broadcast_to(as_column(b_d_ref[...], 40), (40, 128))
    row = iota((48, 3), 0) % 24 // 8
    b_o = jnp.sum(jnp.where(row == iota((48, 3), 1), b_o_ref[...], 0.0), axis=1, keepdims=True)
    bias_ref[72:120] = jnp.broadcast_to(b_o, (48, 128))
    bias_ref[120:128] = jnp.zeros((8, 128), F32)


def fold(core, beyond, z):
    lane = iota((8, 128), 1)
    left = jnp.where(lane < 4, pltpu.roll(beyond, (126 - 16 * z) % 128, 1), 0.0)
    right = jnp.where(lane >= 124, pltpu.roll(beyond, (114 - 16 * z) % 128, 1), 0.0)
    return core + left + right


def blend_weights(gi, gj, margins_ref, blend_ref):
    margins = margins_ref[...].astype(F32)
    places = margins.shape

    def margin(step_y, step_x):
        y, x = gi + step_y, gj + step_x
        here = (iota(places, 0) == x) & (iota(places, 1) == y)
        value = jnp.sum(jnp.where(here, margins, 0.0), keepdims=True)
        return value, (y >= 0) & (y < 16) & (x >= 0) & (x < 8)

    def ramp(distance, pair):
        return jnp.clip(1.0 - distance / (pair[0] + 1.0), 0.0, 1.0) * jnp.where(pair[1], 1.0, 0.0)

    y = iota((8, 128), 0)
    lane = iota((8, 128), 1)
    upper = y < 4
    off_y = jnp.where(upper, y + 1, 8 - y).astype(F32)
    nth = lane % 16
    left = nth < 8
    off_x = jnp.where(
        within(nth, 2, 5), nth - 1, jnp.where(within(nth, 10, 13), 14 - nth, 99)
    ).astype(F32)
    m = {(a, b): margin(a, b) for a in (-1, 0, 1) for b in (-1, 0, 1) if (a, b) != (0, 0)}
    weight_y = jnp.where(upper, ramp(off_y, m[-1, 0]), ramp(off_y, m[1, 0]))
    weight_x = jnp.where(left, ramp(off_x, m[0, -1]), ramp(off_x, m[0, 1]))

    def corner(a, b):
        return ramp(off_y, m[a, b]) * ramp(off_x, m[a, b])

    weight_xy = jnp.where(
        upper,
        jnp.where(left, corner(-1, -1), corner(-1, 1)),
        jnp.where(left, corner(1, -1), corner(1, 1)),
    )
    blend_ref[0:8] = weight_y
    blend_ref[8:16] = weight_x
    blend_ref[16:24] = weight_xy
    blend_ref[24:32] = 1.0 / fold(1.0 + weight_y, weight_x + weight_xy, 0)


def flag_rows(gi, gj, side):
    kind = iota((16, 128), 0)
    lane = iota((16, 128), 1)
    dx = kind - 3
    if side:
        nth = lane % 16
        column = jnp.where(nth < 8, nth - 3 + dx, 113 + nth + dx)
        outside = column == jnp.where(nth < 8, 4, 123)
    else:
        column = lane + dx - 1
        outside = lane < 0
    outside = outside | ((column < 0) & (gj == 0)) | ((column > 127) & (gj == 7))
    value = (kind < 3) | (within(kind, 3, 5) & outside)
    value = value | ((kind == 6) & (gi == 0)) | ((kind == 7) & (gi == 15))
    return jnp.where(value, 1.0, 0.0).astype(BF16)


def shift_raw(slabs, got_ref, got_edge_ref, taps_ref):
    lane = iota((8, 128), 1)
    tile = iota((16, 128), 1)
    sides = [jnp.zeros((16, 128), F32) for _ in range(5)]
    for z in range(8):
        slab = slabs[z]
        near, far = [got_ref[n, slab].astype(F32) for n in range(2)]
        before, after = [jnp.broadcast_to(got_edge_ref[n, slab], (8, 128)) for n in range(2)]
        core = jnp.concatenate(
            [
                jnp.where(lane < 64, near, pltpu.roll(far, 64, 1)),
                jnp.where(lane < 64, pltpu.roll(near, 64, 1), far),
            ],
            axis=0,
        )
        before = jnp.concatenate(
            [pltpu.roll(before, n, 1, stride=16, stride_axis=0) for n in (6, 2)], axis=0
        )
        after = jnp.concatenate(
            [pltpu.roll(after, n, 1, stride=16, stride_axis=0) for n in (14, 10)], axis=0
        )
        low = jnp.where(tile < 6, pltpu.roll(core, 6, 1), after)
        high = jnp.where(tile >= 122, pltpu.roll(core, 122, 1), before)
        beside = jnp.where(tile < 64, low, high)
        for n in range(5):
            s = n - 2
            moved = core if s == 0 else pltpu.roll(core, -s % 128, 1)
            if s > 0:
                moved = jnp.where(tile >= 128 - s, pltpu.roll(beside, 122 - s, 1), moved)
            if s < 0:
                moved = jnp.where(tile < -s, pltpu.roll(beside, 6 - s, 1), moved)
            taps_ref[16 * n : 16 * n + 16, 128 * z : 128 * z + 128] = moved.astype(BF16)
            moved = pltpu.roll(beside, (16 * z + 8 - s) % 128, 1)
            sides[n] = jnp.where(tile // 16 == z, moved, sides[n])
    for n in range(5):
        taps_ref[16 * n : 16 * n + 16, 1024:1152] = sides[n].astype(BF16)


def exchange_kernel(*refs):
    hbm, refs = refs[0:14], refs[14:]
    taps_ref, made, blend_ref, table_ref, refs = refs[0], refs[1:7], refs[7], refs[8], refs[9:]
    loaded, refs = refs[0:13], refs[13:]
    pad_ref, send_ref, send_edge_ref, got_ref, got_edge_ref, load_sem, send_sem, recv_sem, mate_sem = refs
    raw_ref, order_ref, margins_ref, weights = loaded[0], loaded[1], loaded[2], loaded[3:]
    gi = lax.axis_index("gx")
    gj = lax.axis_index("gy")
    odd, column, beside = neighbours(gi)
    inner = (gi > 0) & (gi < 15)
    loads = [
        pltpu.make_async_copy(source, place, load_sem.at[n])
        for n, (source, place) in enumerate(zip(hbm, loaded + (table_ref,)))
    ]
    loads[0].start()
    barrier = pltpu.get_barrier_semaphore()

    core = lax.rem(gj, 2)
    mate = (gi, gj + 1 - 2 * core)
    group = jnp.int32(1)
    for row in SOON:
        group = jnp.where(gi == row, 0, group)

    @pl.when(core == 1)
    def _():
        pl.semaphore_signal(barrier, inc=1, device_id=mate, device_id_type=MESH)

    chips = [lax.rem(lax.div(gj, 2) + n, 4) for n in (2, 1, 3, 0)]
    for chip in chips:
        for strip in (2 * gj, 2 * gj + 1):
            peer = (strip, 2 * chip + group)
            pl.semaphore_signal(barrier, inc=1, device_id=peer, device_id_type=MESH)

    @pl.when(gj > 0)
    def _():
        for chip in chips:
            peer = (2 * gj - 1, 2 * chip + group)
            pl.semaphore_signal(barrier, inc=1, device_id=peer, device_id_type=MESH)

    @pl.when(gj < 7)
    def _():
        for chip in chips:
            peer = (2 * gj + 2, 2 * chip + group)
            pl.semaphore_signal(barrier, inc=1, device_id=peer, device_id_type=MESH)

    for load in loads[1:]:
        load.start()

    lane = iota((128, 256), 1)
    wanted = iota((128, 256), 0) + jnp.where(lane < 128, -4, 4)
    rows = (wanted == lane % 128).astype(F32).astype(BF16)
    lane = iota((128, 128), 1)
    nth = lane % 16 - 8 * (1 - odd)
    cols = jnp.where(within(nth, 0, 3), nth, jnp.where(within(nth, 4, 7), nth + 60, -99)) + 60 * odd
    cols = (iota((128, 128), 0) == cols).astype(F32).astype(BF16)
    own = lane // 16 == 7 - iota((128, 128), 0) % 8
    gather = (iota((16, 128), 0) == iota((16, 128), 1) // 8).astype(F32).astype(BF16)
    loads[0].wait()
    raw = raw_ref[0].astype(F32)
    none = jnp.zeros_like(raw)
    raw = jnp.concatenate(
        [jnp.concatenate([raw, none], axis=1), jnp.concatenate([none, raw], axis=1)], axis=0
    ).astype(BF16)
    message = lax.dot_general(
        rows, raw, (((1,), (1,)), ((), ())), preferred_element_type=F32
    ).astype(BF16)
    send_ref[...] = message.reshape(16, 8, 128)
    edge = dot(gather, jnp.where(own, dot(message, cols), 0.0).astype(BF16))
    for row in range(16):
        send_edge_ref[row] = edge[row : row + 1]

    soon = jnp.where(inner, 2 * len(SOON), len(SOON))
    late = jnp.where(inner, 2 * len(LATE), len(LATE))

    @pl.when(core == 0)
    def _():
        pl.semaphore_wait(barrier, soon + 1)
        pl.semaphore_signal(mate_sem, inc=1, device_id=mate, device_id_type=MESH)

    @pl.when(core == 1)
    def _():
        pl.semaphore_wait(mate_sem, 1)

    def send(row):
        for kind, source, target, place, wanted in (
            (0, send_ref.at[row], got_ref.at[odd, gj], column, True),
            (1, send_edge_ref.at[row], got_edge_ref.at[1 - odd, gj], beside, inner),
        ):
            here = (gi == row) & (gj == place)

            @pl.when(jnp.logical_not(here) & wanted)
            def _():
                pltpu.make_async_remote_copy(
                    src_ref=source,
                    dst_ref=target,
                    send_sem=send_sem.at[kind],
                    recv_sem=recv_sem.at[kind],
                    device_id=(row, place),
                    device_id_type=MESH,
                ).start()

            @pl.when(here & wanted)
            def _():
                pltpu.make_async_copy(source, target, recv_sem.at[kind]).start()

    for row in SOON:
        send(row)

    for load in loads[1:]:
        load.wait()
    lay_out_weights(*weights, pad_ref, *made)
    blend_weights(gi, gj, margins_ref, blend_ref)
    flags = flag_rows(gi, gj, False)
    for z in range(8):
        taps_ref[80:96, 128 * z : 128 * z + 128] = flags
    taps_ref[80:96, 1024:1152] = flag_rows(gi, gj, True)

    @pl.when(core == 0)
    def _():
        pl.semaphore_wait(mate_sem, 1)

    @pl.when(core == 1)
    def _():
        pl.semaphore_wait(barrier, late)
        pl.semaphore_signal(mate_sem, inc=1, device_id=mate, device_id_type=MESH)

    for row in LATE:
        send(row)

    slabs = []
    for z in range(8):
        slab = jnp.int32(0)
        for k in range(8):
            slab = jnp.maximum(slab, jnp.where(order_ref[k] == z, k, 0))
        slabs.append(slab)

    def got(ref, kind):
        pltpu.make_async_copy(ref, ref, recv_sem.at[kind]).wait()

    got(got_ref, 0)

    @pl.when(within(gj, 1, 6))
    def _():
        got(got_edge_ref, 1)

    @pl.when(gj == 0)
    def _():
        got(got_edge_ref.at[1], 1)
        got_edge_ref[0] = jnp.zeros((8, 1, 128), F32)

    @pl.when(gj == 7)
    def _():
        got(got_edge_ref.at[0], 1)
        got_edge_ref[1] = jnp.zeros((8, 1, 128), F32)

    shift_raw(slabs, got_ref, got_edge_ref, taps_ref)

    def sent(ref, count):
        kind = 0 if ref is send_ref else 1
        ref = ref.at[0:count]
        pltpu.make_async_copy(ref, ref, send_sem.at[kind]).wait()

    @pl.when(gj == column)
    def _():
        sent(send_ref, 15)

    @pl.when(gj != column)
    def _():
        sent(send_ref, 16)

    @pl.when(inner & (gj == beside))
    def _():
        sent(send_edge_ref, 15)

    @pl.when(inner & (gj != beside))
    def _():
        sent(send_edge_ref, 16)


ROWS = (0, 1, 4, 8, 12, 2, 3, 5, 9, 13, 6, 7, 10, 14, 11, 15)
SOON = ROWS[:5]
LATE = ROWS[5:]


TAPS = jax.ShapeDtypeStruct((96, 1152), BF16)
MADE = (
    jax.ShapeDtypeStruct((1280, 128), BF16),
    jax.ShapeDtypeStruct((672, 256), BF16),
    jax.ShapeDtypeStruct((656, 256), BF16),
    jax.ShapeDtypeStruct((48, 256), BF16),
    jax.ShapeDtypeStruct((48, 384), BF16),
    jax.ShapeDtypeStruct((128, 128), F32),
)
BLEND = jax.ShapeDtypeStruct((32, 128), F32)
TABLE = jax.ShapeDtypeStruct((256, 1152), BF16)


def as_they_lie(raw, section_order, margins, w_in, b_in, w_a, b_a, w_d, b_d, w_u, w_o, b_o):
    return (
        jnp.transpose(raw, (0, 2, 1)),
        section_order,
        margins.T,
        jnp.asarray(units_table()),
        w_in.T,
        b_in[None],
        w_a,
        b_a[None],
        jnp.transpose(w_d, (0, 2, 1)),
        b_d[None],
        w_u,
        w_o,
        b_o[None],
        jnp.asarray(level_table()),
    )


def exchange(*arrays):
    arrays = [pltpu.with_memory_space_constraint(x, pltpu.HBM) for x in as_they_lie(*arrays)]
    vmem = pl.BlockSpec(memory_space=pltpu.VMEM)
    places = [pltpu.SMEM if n == 1 else pltpu.VMEM for n in range(13)]
    return pl.pallas_call(
        exchange_kernel,
        out_shape=(TAPS,) + MADE + (BLEND, TABLE),
        in_specs=[pl.BlockSpec(memory_space=pltpu.HBM)] * 14,
        out_specs=(vmem,) * 9,
        scratch_shapes=[place(x.shape, x.dtype) for place, x in zip(places, arrays)]
        + [
            pltpu.VMEM((27, 32, 128), BF16),
            pltpu.VMEM((16, 8, 128), BF16),
            pltpu.VMEM((16, 1, 128), F32),
            pltpu.VMEM((2, 8, 8, 128), BF16),
            pltpu.VMEM((2, 8, 1, 128), F32),
            pltpu.SemaphoreType.DMA((14,)),
            pltpu.SemaphoreType.DMA((2,)),
            pltpu.SemaphoreType.DMA((2,)),
            pltpu.SemaphoreType.REGULAR,
        ],
        compiler_params=pltpu.CompilerParams(
            collective_id=0, has_side_effects=True, vmem_limit_bytes=12 * 1024 * 1024
        ),
    )(*arrays)


def network_kernel(
    taps_ref,
    conv_in_ref,
    conv_a_ref,
    conv_d_ref,
    w_q_ref,
    w_s_ref,
    bias_ref,
    blend_ref,
    table_ref,
    out_hbm,
    out_ref,
    out_sem,
    h_ref,
    a_ref,
    d_ref,
    e_ref,
):
    bias_d = jnp.concatenate([bias_ref[32:72]] * 8, axis=0)
    bias_o = bias_ref[72:120]
    weight_y, weight_x, weight_xy, scale = [blend_ref[8 * n : 8 * n + 8] for n in range(4)]
    margins = slice(1024, 1152)

    def pair(q):
        return slice(256 * q, 256 * q + 256)

    def section(z):
        return slice(128 * z, 128 * z + 128)

    def wide(column, at):
        return column if at.stop - at.start == 128 else jnp.concatenate([column, column], axis=1)

    def first_level(at):
        h = dot(conv_in_ref[:, 0:96], taps_ref[:, at]).astype(BF16)
        h_ref[:, :, at] = jnp.maximum(h, 0).reshape(5, 256, at.stop - at.start)

    places = (0, 1, 2, 3, 4, 5, 6, 7, 8, 9, 12, 13, 10, 11)

    tiles = (
        (3, (0, 1, 2), (0,)),
        (1, (1, 2, 3, 4, 5), (1, 2, 3)),
        (0, (12, 4, 5, 6, 7, 8, 13), (4, 5, 6, 12, 13)),
        (1, (7, 8, 9, 10, 11), (7, 8, 9)),
        (1, (10, 11), (10, 11)),
    )

    def products(tile, at, sums):
        first, rows, _ = tiles[tile]
        product = dot(conv_a_ref[96 * first : 96 * (first + len(rows))], h_ref[tile, :, at])
        product = product.reshape(len(rows), 3, 32, at.stop - at.start)
        for n, row in enumerate(rows):
            part = product[n]
            sums[row] = sums[row] + part if row in sums else part
            if tile == 1 and row == 5:
                sums[12] = part

    def finish(row, at, total):
        block = (row + 1 if row < 12 else row - 6) if row != 12 else 6
        tile, nth = block // 3, block % 3
        centre = h_ref[tile, 32 * nth : 32 * nth + 32, at].astype(F32)
        a_ref[places[row], :, at] = (centre + jnp.maximum(total, 0.0)).astype(BF16)

    def pooled_rows(at):
        even = jnp.concatenate([a_ref[n, :, at] for n in (0, 2, 4, 6, 8, 12, 4, 11)], axis=0)
        late = jnp.concatenate([a_ref[n, :, at] for n in (1, 3, 5, 7, 9, 13, 10, 7)], axis=0)
        return jnp.concatenate([even, late], axis=1)

    def keep(dx, at, value):
        d_ref[:, dx, :, at] = value.astype(BF16).reshape(8, 32, 128)

    def pool(q):
        both = jnp.concatenate([pooled_rows(section(2 * q)), pooled_rows(section(2 * q + 1))], axis=0)
        return dot(both, table_ref[:, 256:512])

    def pooled(q, d, ends):
        lane = iota((32, 128), 1)
        low = lane < 64
        for block in range(8):
            rows, more = slice(32 * block, 32 * block + 32), slice(256 + 32 * block, 288 + 32 * block)
            one, two = d[rows, 0:128], pltpu.roll(d[more, 0:128], 64, 1)
            end = ends[rows]
            before = end if q == 0 else pltpu.roll(end, 128 - q, 1)
            after = end if q == 3 else pltpu.roll(end, 3 - q, 1)
            moved = pltpu.roll(jnp.where(low, two, one), 64, 1)
            for dx, value in (
                (0, jnp.where(lane % 64 == 0, before, jnp.where(low, one, two))),
                (1, jnp.where(low, d[rows, 128:256], pltpu.roll(d[more, 128:256], 64, 1))),
                (2, jnp.where(lane % 64 == 63, after, moved)),
            ):
                d_ref[block, dx, :, section(q)] = value.astype(BF16)

    def coarse(at):
        d = d_ref[:, :, :, at].reshape(768, at.stop - at.start)
        one = dot(conv_d_ref[0:208], d[0:256])
        two = dot(conv_d_ref[208:448], d[256:512])
        three = dot(conv_d_ref[448:656], d[512:768])
        return one, two, three

    def coarsened(at, parts):
        one, two, three = parts
        e = jnp.concatenate(
            [
                one[0:80] + three[0:80],
                one[80:200] + two[0:120],
                two[120:240] + three[80:200],
            ],
            axis=0,
        )
        e_ref[:, at] = jnp.maximum(e + wide(bias_d, at), 0.0).astype(BF16)

    def lift(at):
        own = dot(w_q_ref[:, 0:160], e_ref[80:240, at])
        other = dot(w_q_ref[:, 0:160], jnp.concatenate([e_ref[0:80, at], e_ref[240:320, at]], axis=0))
        return own, other

    def spread(parts, table):
        own, other = parts
        q = jnp.concatenate([own[0:24] + own[24:48], other[0:24] + other[24:48]], axis=0)
        high = q.astype(BF16).astype(F32)
        low = q - high
        rows = [
            jnp.concatenate([high[:, at : at + 128], low[:, at : at + 128]], axis=1)
            for at in range(0, q.shape[1], 128)
        ]
        return dot(jnp.concatenate(rows, axis=0).astype(BF16), table)

    def fine(at):
        s = dot(w_s_ref[:, 0:320], a_ref[2:12, :, at].reshape(320, at.stop - at.start))
        return s + wide(bias_o, at)

    def blend(q, s, beyond):
        s = jax.nn.sigmoid(s)
        for half in range(2):
            for o in range(3):
                own = s[8 * o : 8 * o + 8, 128 * half : 128 * half + 128]
                other = s[24 + 8 * o : 32 + 8 * o, 128 * half : 128 * half + 128]
                z = 2 * q + half
                out_ref[o, z] = fold(own + other * weight_y, beyond[o], z) * scale

    first_level(margins)
    first_level(pair(0))
    sums = {}
    along = iota((32, 128), 1)

    def finish_margins(tile):
        for row in tiles[tile][2]:
            before, here, after = sums[row][0], sums[row][1], sums[row][2]
            before = jnp.where(along >= 16, pltpu.roll(before, 16, 1), 0.0)
            after = jnp.where(along < 112, pltpu.roll(after, 112, 1), 0.0)
            finish(row, margins, here + before + after)

    for tile in range(5):
        products(tile, margins, sums)
        if tile > 0:
            finish_margins(tile - 1)
    first_level(pair(1))
    finish_margins(4)

    p = [{}, {}, {}, {}]

    def finish_sections(q, tile):
        for row in tiles[tile][2]:
            here = p[q][row]
            if q > 0:
                last = p[q - 1][row]
                total = last[1, :, 128:256] + last[0, :, 0:128] + here[2, :, 0:128]
                finish(row, section(2 * q - 1), total)
            total = here[1, :, 0:128] + here[2, :, 128:256]
            if q > 0:
                total = total + p[q - 1][row][0, :, 128:256]
            finish(row, section(2 * q), total)
            if q == 3:
                finish(row, section(7), here[1, :, 128:256] + here[0, :, 0:128])

    def residual(q, beside):
        for tile in range(5):
            products(tile, pair(q), p[q])
            if tile > 0:
                finish_sections(q, tile - 1)
            for task in beside[tile : tile + 1]:
                task()

    got = {}

    def margins_pool():
        got["side"] = dot(pooled_rows(margins), table_ref[:, 512:1024])

    def margins_pooled():
        for dx in range(3):
            keep(dx, slice(512, 640), got["side"][:, 128 * dx : 128 * dx + 128])
        got["ends"] = got["side"][:, 384:512]

    def margins_coarse():
        got["e"] = coarse(slice(512, 640))
        got["fine"] = fine(margins)

    def margins_coarsened():
        coarsened(slice(512, 640), got["e"])

    def margins_lift():
        got["q"] = lift(slice(512, 640))

    def margins_spread():
        got["up"] = spread(got["q"], table_ref[:, 1024:1152])

    def margins_done():
        s = jax.nn.sigmoid(got["fine"] + got["up"])
        got["beyond"] = [
            s[8 * o : 8 * o + 8] * weight_x + s[24 + 8 * o : 32 + 8 * o] * weight_xy
            for o in range(3)
        ]

    def pool_of(q):
        def task():
            got["pool", q] = pool(q)

        return task

    def pooled_of(q):
        return lambda: pooled(q, got["pool", q], got["ends"])

    def fine_of(q):
        def task():
            got["fine", q] = fine(pair(q))

        return task

    low, high = slice(0, 256), slice(256, 512)

    def low_coarse():
        got["e", 0] = coarse(low)

    def low_lift():
        coarsened(low, got["e", 0])
        got["q", 0] = lift(low)

    residual(0, [margins_pool, margins_pooled, margins_coarse, margins_coarsened, margins_lift])
    first_level(pair(2))
    finish_sections(0, 4)
    residual(1, [margins_spread, margins_done])
    first_level(pair(3))
    finish_sections(1, 4)
    residual(2, [pool_of(0), pooled_of(0), fine_of(0)])
    finish_sections(2, 4)
    residual(3, [pool_of(1), pooled_of(1), fine_of(1), low_coarse, low_lift])
    finish_sections(3, 4)
    pool_of(2)()
    pool_of(3)()
    up = spread(got["q", 0], table_ref[:, 0:256])
    got["up", 0], got["up", 1] = up[0:48], up[48:96]
    pooled_of(2)()
    got["e", 1] = coarse(section(2))
    fine_of(2)()
    pooled_of(3)()
    coarsened(section(2), got["e", 1])
    got["e", 1] = coarse(section(3))
    fine_of(3)()
    blend(0, got["fine", 0] + got["up", 0], got["beyond"])
    coarsened(section(3), got["e", 1])
    got["q", 1] = lift(high)
    blend(1, got["fine", 1] + got["up", 1], got["beyond"])
    up = spread(got["q", 1], table_ref[:, 0:256])
    got["up", 2], got["up", 3] = up[0:48], up[48:96]
    def out(n):
        part = (slice(None), slice(4 * n, 4 * n + 4))
        return pltpu.make_async_copy(out_ref.at[part], out_hbm.at[part], out_sem.at[n])

    out(0).start()
    blend(2, got["fine", 2] + got["up", 2], got["beyond"])
    blend(3, got["fine", 3] + got["up", 3], got["beyond"])
    out(1).start()
    out(0).wait()
    out(1).wait()


def network(*made, **options):
    vmem = pl.BlockSpec(memory_space=pltpu.VMEM)
    return pl.pallas_call(
        network_kernel,
        out_shape=jax.ShapeDtypeStruct((3, 8, 8, 128), F32),
        in_specs=[vmem] * 9,
        out_specs=pl.BlockSpec(memory_space=pl.ANY),
        scratch_shapes=[
            pltpu.VMEM((3, 8, 8, 128), F32),
            pltpu.SemaphoreType.DMA((2,)),
            pltpu.VMEM((5, 256, 1152), BF16),
            pltpu.VMEM((14, 32, 1152), BF16),
            pltpu.VMEM((8, 3, 32, 640), BF16),
            pltpu.VMEM((320, 640), BF16),
        ],
        compiler_params=pltpu.CompilerParams(vmem_limit_bytes=32 * 1024 * 1024),
        **options,
    )(*made)


def per_device(*arrays):
    return network(*exchange(*arrays))


def solution(mesh):
    placed = (P("gy", None, "gx"), P(), P(), P(), P(), P(), P(), P(), P(), P(), P(), P())
    return jax.shard_map(
        per_device, mesh=mesh, in_specs=placed, out_specs=P(None, None, "gx", "gy"), check_vma=False
    )
```

```python
import functools

import jax
import jax.numpy as jnp
import ml_dtypes
import numpy as np
from jax import lax
from jax.experimental import pallas as pl
from jax.experimental.pallas import tpu as pltpu
from jax.sharding import PartitionSpec as P

MESH = pl.DeviceIdType.MESH
F32 = jnp.float32
BF16 = jnp.bfloat16
BIG = -1e30


def iota(shape, dim):
    return lax.broadcasted_iota(jnp.int32, shape, dim)


def within(x, low, high):
    return (x >= low) & (x <= high)


def dot(a, b):
    return jnp.dot(a, b, preferred_element_type=F32)


def neighbours(gi):
    odd = lax.rem(gi, 2)
    column = lax.div(gi, 2)
    beside = lax.rem(column + 7 + 2 * odd, 8)
    return odd, column, beside


def unit_row(dx, block, channel):
    if dx == 1:
        return 32 * block + channel
    unit = 3 * (dx // 2) + block
    if unit < 5:
        return 96 + 28 * unit + channel
    return 236 + channel if channel < 20 else 8 + channel if channel < 24 else 36 + channel


def units_table():
    table = np.zeros((3, 3, 32, 256), np.float32)
    for block in range(3):
        for dx in range(3):
            for channel in range(28):
                table[block, dx, channel, unit_row(dx, block, channel)] = 1
    return table.reshape(288, 256).astype(ml_dtypes.bfloat16)


def level_table():
    spread = np.zeros((256, 256), np.float32)
    core = np.zeros((2, 128, 256), np.float32)
    side = np.zeros((2, 128, 512), np.float32)
    spread_side = np.zeros((2, 128, 128), np.float32)
    for lane in range(256):
        spread[lane // 2, lane] = spread[128 + lane // 2, lane] = 1
    for m in range(64):
        for fine in (0, 1):
            if m >= 1:
                core[:, 2 * m - 2 + fine, m] = 0.25
            if m <= 62:
                core[:, 2 * m + 2 + fine, 64 + m] = 0.25
            core[:, 2 * m + fine, 128 + m] = 0.25
    for section in range(8):
        for fine in (0, 1):
            for dx in range(3):
                for m in (0, 1):
                    left, right = m + dx - 1, 62 + m + dx - 1
                    if left <= 1:
                        side[:, 16 * section + 2 + 2 * left + fine, 128 * dx + 8 * section + 1 + m] = 0.25
                    if right >= 62:
                        side[:, 16 * section + 2 * right - 114 + fine, 128 * dx + 8 * section + 4 + m] = 0.25
            at = 384 + 64 * (section % 2) + section // 2
            side[:, 16 * section + fine, at] = 0.25
            side[:, 16 * section + 14 + fine, at + 60] = 0.25
        for x in range(4):
            spread_side[:, 8 * section + 1 + x // 2, 16 * section + 2 + x] = 1
            spread_side[:, 8 * section + 4 + x // 2, 16 * section + 10 + x] = 1
    parts = [spread, core.reshape(256, 256), side.reshape(256, 512), spread_side.reshape(256, 128)]
    return np.concatenate(parts, axis=1).astype(ml_dtypes.bfloat16)


def as_column(row, size):
    shape = (size, row.shape[1])
    return jnp.sum(jnp.where(iota(shape, 0) == iota(shape, 1), row, 0.0), axis=1, keepdims=True)


def tiled_taps(pad_ref, first, taps):
    tiles = []
    for start in range(0, taps, 4):
        tile = None
        for q in range(min(4, taps - start)):
            part = pad_ref[first + start + q].astype(F32)
            part = part if q == 0 else pltpu.roll(part, 32 * q, 1)
            tile = part if tile is None else tile + part
        tiles.append(tile)
    return jnp.concatenate(tiles, axis=1)


def lay_out_weights(
    units_ref,
    w_in_ref,
    b_in_ref,
    w_a_ref,
    b_a_ref,
    w_d_ref,
    b_d_ref,
    w_u_ref,
    w_o_ref,
    b_o_ref,
    pad_ref,
    conv_in_ref,
    conv_a_ref,
    conv_d_ref,
    w_q_ref,
    w_s_ref,
    bias_ref,
):
    pad_ref[...] = jnp.zeros_like(pad_ref)
    pad_ref[0, 0:9, 0:28] = w_in_ref[...]
    tap = iota((32, 128), 0)
    lane = iota((32, 128), 1)
    put = (lane == 16 * (tap % 3) + tap // 3) & (tap < 9)
    base = lax.dot_general(
        pad_ref[0],
        put.astype(F32).astype(BF16),
        (((0,), (0,)), ((), ())),
        preferred_element_type=F32,
    )[0:32]
    rest = as_column(b_in_ref[...], 32)
    flagged = jnp.zeros((32, 128), F32)
    for n in range(3):
        part = rest.astype(BF16).astype(F32)
        flagged = flagged + jnp.where(lane == 80 + n, part, 0.0)
        rest = rest - part
    stack = []
    for block in range(3):
        for dx in range(3):
            row = []
            for tile in range(5):
                y = 3 * tile + block
                if y > 13:
                    row.append(jnp.zeros((32, 128), F32))
                    continue
                moved = base if dx == y == 0 else pltpu.roll(base, 16 * dx + y, 1)
                off = (lane == 83 + dx) | ((lane == 86) & (y < 3)) | ((lane == 87) & (y >= 11))
                row.append(moved + flagged + jnp.where(off, BIG, 0.0))
            stack.append(jnp.concatenate(row, axis=1))
    made = lax.dot_general(
        units_ref[...],
        jnp.concatenate(stack, axis=0).astype(BF16),
        (((0,), (0,)), ((), ())),
        preferred_element_type=F32,
    )
    ones = within(iota((256, 640), 0), 92, 94) & (iota((256, 640), 1) % 128 == 80)
    made = jnp.where(ones, 1.0, made).astype(BF16)
    for tile in range(5):
        conv_in_ref[256 * tile : 256 * tile + 256] = made[:, 128 * tile : 128 * tile + 128]

    pad_ref[0] = jnp.zeros((32, 128), BF16)
    pad_ref[0:27, 0:28, 0:28] = w_a_ref[...]
    lane = iota((32, 384), 1)
    parts = [[] for _ in range(7)]
    for dz in range(3):
        taps = tiled_taps(pad_ref, 9 * dz, 9)
        for n, shift in enumerate((-1, -2, -1, 0, 1, 2, 0)):
            moved = taps if shift == 0 else pltpu.roll(taps, 96 * shift % 384, 1)
            low, high = 96 * max(shift, 0), 96 * min(3 + shift, 3)
            if n == 0:
                high = 96
            if n == 6:
                low = 96
            parts[n].append(jnp.where((lane >= low) & (lane < high), moved, 0.0))
    taps = jnp.concatenate([part for shift in parts for part in shift], axis=0).astype(BF16)
    made = dot(taps[:, 0:288], units_ref[...])
    rest = as_column(b_a_ref[...], 32)
    lane = iota((32, 256), 1)
    bias = jnp.zeros((32, 256), F32)
    for n in range(3):
        part = rest.astype(BF16).astype(F32)
        bias = bias + jnp.where(lane == 92 + n, part, 0.0)
        rest = rest - part
    none = jnp.zeros((32, 256), F32)
    once = jnp.concatenate([none, bias, none], axis=0)
    none = jnp.concatenate([none] * 9, axis=0)
    conv_a_ref[...] = (made + jnp.concatenate([none, once, once, once, once], axis=0)).astype(BF16)

    pad_ref[0:9] = jnp.zeros((9, 32, 128), BF16)
    pad_ref[0:9, 0:28, 0:36] = w_d_ref[...]
    taps = pad_ref[0:12].astype(F32).reshape(384, 128)
    taps = jnp.where(iota((384, 128), 0) < 288, taps, 0.0)
    taps = jnp.concatenate([taps[128 * n : 128 * n + 128].T[0:40] for n in range(3)], axis=1)
    taps = jnp.concatenate([taps, jnp.zeros((40, 384), F32)], axis=1)
    lane = iota((40, 768), 1)

    def spaced(*moves):
        total = None
        for first, dy, count in moves:
            by = 96 * (first - dy) % 768
            moved = taps if by == 0 else pltpu.roll(taps, by, 1)
            moved = jnp.where(within(lane, 96 * first, 96 * (first + count) - 1), moved, 0.0)
            total = moved if total is None else total + moved
        return total

    outs = [
        spaced((0, 0, 2), (6, 2, 1)),
        spaced((1, 0, 1), (6, 1, 1)),
        spaced((0, 0, 3)),
        spaced((1, 0, 3)),
        spaced((2, 0, 3)),
        spaced((3, 0, 3)),
        spaced((4, 2, 1), (7, 1, 1)),
        spaced((4, 1, 2), (7, 0, 1)),
    ]
    none = [jnp.zeros((8, 256), F32)]
    for at, tile, which in (
        (0, 0, (0, 1, 2, 3, 4)),
        (208, 1, (2, 3, 4, 5, 6, 7)),
        (448, 2, (0, 1, 5, 6, 7)),
    ):
        part = [outs[n][:, 256 * tile : 256 * tile + 256] for n in which]
        part = jnp.concatenate(part if tile == 1 else part + none, axis=0)
        conv_d_ref[at : at + part.shape[0]] = part.astype(BF16)

    w_o = w_o_ref[...].astype(F32)
    w_o = jnp.concatenate([jnp.broadcast_to(w_o[o : o + 1], (8, 28)) for o in range(3)], axis=0)
    w_o = jnp.concatenate([w_o, jnp.zeros((24, 4), F32)], axis=1)
    pad_ref[0] = jnp.zeros((32, 128), BF16)
    pad_ref[0, 0:28, 0:36] = w_u_ref[...]
    w_u = pad_ref[0].astype(F32)
    w_u = jnp.concatenate([w_u, jnp.zeros_like(w_u)], axis=1)
    w_u = w_u + pltpu.roll(w_u, 40, 1)
    w_u = w_u + pltpu.roll(w_u, 80, 1)
    w_q = dot(w_o.astype(BF16), w_u.astype(BF16))
    lane = iota((24, 256), 1)
    w_q = jnp.where(lane // 40 == (iota((24, 256), 0) % 8) // 2, w_q, 0.0)
    high = w_q.astype(BF16).astype(F32)
    w_q_ref[...] = jnp.concatenate([high, w_q - high], axis=0).astype(BF16)
    w_o = jnp.concatenate([w_o] * 12, axis=1)
    w_o = jnp.concatenate([w_o, w_o], axis=0)
    lane = iota((48, 384), 1) // 32
    row = iota((48, 384), 0)
    block = jnp.where(row < 24, row % 8, jnp.where(within(row % 8, 3, 4), row % 8 + 5, row % 8))
    w_s_ref[...] = jnp.where(lane == block, w_o, 0.0).astype(BF16)

    bias_ref[0:32] = jnp.zeros((32, 128), F32)
    bias_ref[32:72] = jnp.broadcast_to(as_column(b_d_ref[...], 40), (40, 128))
    row = iota((48, 3), 0) % 24 // 8
    b_o = jnp.sum(jnp.where(row == iota((48, 3), 1), b_o_ref[...], 0.0), axis=1, keepdims=True)
    bias_ref[72:120] = jnp.broadcast_to(b_o, (48, 128))
    bias_ref[120:128] = jnp.zeros((8, 128), F32)


def fold(core, beyond, z):
    lane = iota((8, 128), 1)
    left = jnp.where(lane < 4, pltpu.roll(beyond, (126 - 16 * z) % 128, 1), 0.0)
    right = jnp.where(lane >= 124, pltpu.roll(beyond, (114 - 16 * z) % 128, 1), 0.0)
    return core + left + right


def blend_weights(gi, gj, margins_ref, blend_ref):
    margins = margins_ref[...].astype(F32)
    places = margins.shape

    def margin(step_y, step_x):
        y, x = gi + step_y, gj + step_x
        here = (iota(places, 0) == x) & (iota(places, 1) == y)
        value = jnp.sum(jnp.where(here, margins, 0.0), keepdims=True)
        return value, (y >= 0) & (y < 16) & (x >= 0) & (x < 8)

    def ramp(distance, pair):
        return jnp.clip(1.0 - distance / (pair[0] + 1.0), 0.0, 1.0) * jnp.where(pair[1], 1.0, 0.0)

    y = iota((8, 128), 0)
    lane = iota((8, 128), 1)
    upper = y < 4
    off_y = jnp.where(upper, y + 1, 8 - y).astype(F32)
    nth = lane % 16
    left = nth < 8
    off_x = jnp.where(
        within(nth, 2, 5), nth - 1, jnp.where(within(nth, 10, 13), 14 - nth, 99)
    ).astype(F32)
    m = {(a, b): margin(a, b) for a in (-1, 0, 1) for b in (-1, 0, 1) if (a, b) != (0, 0)}
    weight_y = jnp.where(upper, ramp(off_y, m[-1, 0]), ramp(off_y, m[1, 0]))
    weight_x = jnp.where(left, ramp(off_x, m[0, -1]), ramp(off_x, m[0, 1]))

    def corner(a, b):
        return ramp(off_y, m[a, b]) * ramp(off_x, m[a, b])

    weight_xy = jnp.where(
        upper,
        jnp.where(left, corner(-1, -1), corner(-1, 1)),
        jnp.where(left, corner(1, -1), corner(1, 1)),
    )
    blend_ref[0:8] = weight_y
    blend_ref[8:16] = weight_x
    blend_ref[16:24] = weight_xy
    blend_ref[24:32] = 1.0 / fold(1.0 + weight_y, weight_x + weight_xy, 0)


def flag_rows(gi, gj, side):
    kind = iota((16, 128), 0)
    lane = iota((16, 128), 1)
    dx = kind - 3
    if side:
        nth = lane % 16
        column = jnp.where(nth < 8, nth - 3 + dx, 113 + nth + dx)
        outside = column == jnp.where(nth < 8, 4, 123)
    else:
        column = lane + dx - 1
        outside = lane < 0
    outside = outside | ((column < 0) & (gj == 0)) | ((column > 127) & (gj == 7))
    value = (kind < 3) | (within(kind, 3, 5) & outside)
    value = value | ((kind == 6) & (gi == 0)) | ((kind == 7) & (gi == 15))
    return jnp.where(value, 1.0, 0.0).astype(BF16)


def shift_raw(slabs, got_ref, got_edge_ref, taps_ref):
    lane = iota((8, 128), 1)
    tile = iota((16, 128), 1)
    sides = [jnp.zeros((16, 128), F32) for _ in range(5)]
    for z in range(8):
        slab = slabs[z]
        near, far = [got_ref[n, slab].astype(F32) for n in range(2)]
        before, after = [jnp.broadcast_to(got_edge_ref[n, slab], (8, 128)) for n in range(2)]
        core = jnp.concatenate(
            [
                jnp.where(lane < 64, near, pltpu.roll(far, 64, 1)),
                jnp.where(lane < 64, pltpu.roll(near, 64, 1), far),
            ],
            axis=0,
        )
        before = jnp.concatenate(
            [pltpu.roll(before, n, 1, stride=16, stride_axis=0) for n in (6, 2)], axis=0
        )
        after = jnp.concatenate(
            [pltpu.roll(after, n, 1, stride=16, stride_axis=0) for n in (14, 10)], axis=0
        )
        low = jnp.where(tile < 6, pltpu.roll(core, 6, 1), after)
        high = jnp.where(tile >= 122, pltpu.roll(core, 122, 1), before)
        beside = jnp.where(tile < 64, low, high)
        for n in range(5):
            s = n - 2
            moved = core if s == 0 else pltpu.roll(core, -s % 128, 1)
            if s > 0:
                moved = jnp.where(tile >= 128 - s, pltpu.roll(beside, 122 - s, 1), moved)
            if s < 0:
                moved = jnp.where(tile < -s, pltpu.roll(beside, 6 - s, 1), moved)
            taps_ref[16 * n : 16 * n + 16, 128 * z : 128 * z + 128] = moved.astype(BF16)
            moved = pltpu.roll(beside, (16 * z + 8 - s) % 128, 1)
            sides[n] = jnp.where(tile // 16 == z, moved, sides[n])
    for n in range(5):
        taps_ref[16 * n : 16 * n + 16, 1024:1152] = sides[n].astype(BF16)


def exchange_kernel(*refs):
    hbm, refs = refs[0:14], refs[14:]
    taps_ref, made, blend_ref, table_ref, refs = refs[0], refs[1:7], refs[7], refs[8], refs[9:]
    loaded, refs = refs[0:13], refs[13:]
    pad_ref, send_ref, send_edge_ref, got_ref, got_edge_ref, load_sem, send_sem, recv_sem, mate_sem = refs
    raw_ref, order_ref, margins_ref, weights = loaded[0], loaded[1], loaded[2], loaded[3:]
    gi = lax.axis_index("gx")
    gj = lax.axis_index("gy")
    odd, column, beside = neighbours(gi)
    inner = (gi > 0) & (gi < 15)
    loads = [
        pltpu.make_async_copy(source, place, load_sem.at[n])
        for n, (source, place) in enumerate(zip(hbm, loaded + (table_ref,)))
    ]
    loads[0].start()
    barrier = pltpu.get_barrier_semaphore()

    core = lax.rem(gj, 2)
    mate = (gi, gj + 1 - 2 * core)
    group = jnp.int32(1)
    for row in SOON:
        group = jnp.where(gi == row, 0, group)

    @pl.when(core == 1)
    def _():
        pl.semaphore_signal(barrier, inc=1, device_id=mate, device_id_type=MESH)

    chips = [lax.rem(lax.div(gj, 2) + n, 4) for n in (2, 1, 3, 0)]
    for chip in chips:
        for strip in (2 * gj, 2 * gj + 1):
            peer = (strip, 2 * chip + group)
            pl.semaphore_signal(barrier, inc=1, device_id=peer, device_id_type=MESH)

    @pl.when(gj > 0)
    def _():
        for chip in chips:
            peer = (2 * gj - 1, 2 * chip + group)
            pl.semaphore_signal(barrier, inc=1, device_id=peer, device_id_type=MESH)

    @pl.when(gj < 7)
    def _():
        for chip in chips:
            peer = (2 * gj + 2, 2 * chip + group)
            pl.semaphore_signal(barrier, inc=1, device_id=peer, device_id_type=MESH)

    for load in loads[1:]:
        load.start()

    lane = iota((128, 256), 1)
    wanted = iota((128, 256), 0) + jnp.where(lane < 128, -4, 4)
    rows = (wanted == lane % 128).astype(F32).astype(BF16)
    lane = iota((128, 128), 1)
    nth = lane % 16 - 8 * (1 - odd)
    cols = jnp.where(within(nth, 0, 3), nth, jnp.where(within(nth, 4, 7), nth + 60, -99)) + 60 * odd
    cols = (iota((128, 128), 0) == cols).astype(F32).astype(BF16)
    own = lane // 16 == 7 - iota((128, 128), 0) % 8
    gather = (iota((16, 128), 0) == iota((16, 128), 1) // 8).astype(F32).astype(BF16)
    loads[0].wait()
    raw = raw_ref[0].astype(F32)
    none = jnp.zeros_like(raw)
    raw = jnp.concatenate(
        [jnp.concatenate([raw, none], axis=1), jnp.concatenate([none, raw], axis=1)], axis=0
    ).astype(BF16)
    message = lax.dot_general(
        rows, raw, (((1,), (1,)), ((), ())), preferred_element_type=F32
    ).astype(BF16)
    send_ref[...] = message.reshape(16, 8, 128)
    edge = dot(gather, jnp.where(own, dot(message, cols), 0.0).astype(BF16))
    for row in range(16):
        send_edge_ref[row] = edge[row : row + 1]

    soon = jnp.where(inner, 2 * len(SOON), len(SOON))
    late = jnp.where(inner, 2 * len(LATE), len(LATE))

    @pl.when(core == 0)
    def _():
        pl.semaphore_wait(barrier, soon + 1)
        pl.semaphore_signal(mate_sem, inc=1, device_id=mate, device_id_type=MESH)

    @pl.when(core == 1)
    def _():
        pl.semaphore_wait(mate_sem, 1)

    def send(row):
        for kind, source, target, place, wanted in (
            (0, send_ref.at[row], got_ref.at[odd, gj], column, True),
            (1, send_edge_ref.at[row], got_edge_ref.at[1 - odd, gj], beside, inner),
        ):
            here = (gi == row) & (gj == place)

            @pl.when(jnp.logical_not(here) & wanted)
            def _():
                pltpu.make_async_remote_copy(
                    src_ref=source,
                    dst_ref=target,
                    send_sem=send_sem.at[kind],
                    recv_sem=recv_sem.at[kind],
                    device_id=(row, place),
                    device_id_type=MESH,
                ).start()

    for row in SOON:
        send(row)

    @pl.when(gj == column)
    def _():
        pltpu.make_async_copy(send_ref.at[gi], got_ref.at[odd, gj], recv_sem.at[0]).start()

    @pl.when(inner & (gj == beside))
    def _():
        pltpu.make_async_copy(
            send_edge_ref.at[gi], got_edge_ref.at[1 - odd, gj], recv_sem.at[1]
        ).start()

    for load in loads[1:]:
        load.wait()
    lay_out_weights(*weights, pad_ref, *made)
    blend_weights(gi, gj, margins_ref, blend_ref)
    flags = flag_rows(gi, gj, False)
    for z in range(8):
        taps_ref[80:96, 128 * z : 128 * z + 128] = flags
    taps_ref[80:96, 1024:1152] = flag_rows(gi, gj, True)

    @pl.when(core == 0)
    def _():
        pl.semaphore_wait(mate_sem, 1)

    @pl.when(core == 1)
    def _():
        pl.semaphore_wait(barrier, late)
        pl.semaphore_signal(mate_sem, inc=1, device_id=mate, device_id_type=MESH)

    for row in LATE:
        send(row)

    slabs = []
    for z in range(8):
        slab = jnp.int32(0)
        for k in range(8):
            slab = jnp.maximum(slab, jnp.where(order_ref[k] == z, k, 0))
        slabs.append(slab)

    def got(ref, kind):
        pltpu.make_async_copy(ref, ref, recv_sem.at[kind]).wait()

    got(got_ref, 0)

    @pl.when(within(gj, 1, 6))
    def _():
        got(got_edge_ref, 1)

    @pl.when(gj == 0)
    def _():
        got(got_edge_ref.at[1], 1)
        got_edge_ref[0] = jnp.zeros((8, 1, 128), F32)

    @pl.when(gj == 7)
    def _():
        got(got_edge_ref.at[0], 1)
        got_edge_ref[1] = jnp.zeros((8, 1, 128), F32)

    shift_raw(slabs, got_ref, got_edge_ref, taps_ref)

    def sent(ref, count):
        kind = 0 if ref is send_ref else 1
        ref = ref.at[0:count]
        pltpu.make_async_copy(ref, ref, send_sem.at[kind]).wait()

    @pl.when(gj == column)
    def _():
        sent(send_ref, 15)

    @pl.when(gj != column)
    def _():
        sent(send_ref, 16)

    @pl.when(inner & (gj == beside))
    def _():
        sent(send_edge_ref, 15)

    @pl.when(inner & (gj != beside))
    def _():
        sent(send_edge_ref, 16)


ROWS = (0, 1, 4, 8, 12, 2, 3, 5, 9, 13, 6, 7, 10, 14, 11, 15)
SOON = ROWS[:5]
LATE = ROWS[5:]


TAPS = jax.ShapeDtypeStruct((96, 1152), BF16)
MADE = (
    jax.ShapeDtypeStruct((1280, 128), BF16),
    jax.ShapeDtypeStruct((672, 256), BF16),
    jax.ShapeDtypeStruct((656, 256), BF16),
    jax.ShapeDtypeStruct((48, 256), BF16),
    jax.ShapeDtypeStruct((48, 384), BF16),
    jax.ShapeDtypeStruct((128, 128), F32),
)
BLEND = jax.ShapeDtypeStruct((32, 128), F32)
TABLE = jax.ShapeDtypeStruct((256, 1152), BF16)


def as_they_lie(raw, section_order, margins, w_in, b_in, w_a, b_a, w_d, b_d, w_u, w_o, b_o):
    return (
        jnp.transpose(raw, (0, 2, 1)),
        section_order,
        margins.T,
        jnp.asarray(units_table()),
        w_in.T,
        b_in[None],
        w_a,
        b_a[None],
        jnp.transpose(w_d, (0, 2, 1)),
        b_d[None],
        w_u,
        w_o,
        b_o[None],
        jnp.asarray(level_table()),
    )


def exchange(*arrays):
    arrays = [pltpu.with_memory_space_constraint(x, pltpu.HBM) for x in as_they_lie(*arrays)]
    vmem = pl.BlockSpec(memory_space=pltpu.VMEM)
    places = [pltpu.SMEM if n == 1 else pltpu.VMEM for n in range(13)]
    return pl.pallas_call(
        exchange_kernel,
        out_shape=(TAPS,) + MADE + (BLEND, TABLE),
        in_specs=[pl.BlockSpec(memory_space=pltpu.HBM)] * 14,
        out_specs=(vmem,) * 9,
        scratch_shapes=[place(x.shape, x.dtype) for place, x in zip(places, arrays)]
        + [
            pltpu.VMEM((27, 32, 128), BF16),
            pltpu.VMEM((16, 8, 128), BF16),
            pltpu.VMEM((16, 1, 128), F32),
            pltpu.VMEM((2, 8, 8, 128), BF16),
            pltpu.VMEM((2, 8, 1, 128), F32),
            pltpu.SemaphoreType.DMA((14,)),
            pltpu.SemaphoreType.DMA((2,)),
            pltpu.SemaphoreType.DMA((2,)),
            pltpu.SemaphoreType.REGULAR,
        ],
        compiler_params=pltpu.CompilerParams(
            collective_id=0, has_side_effects=True, vmem_limit_bytes=12 * 1024 * 1024
        ),
    )(*arrays)


def network_kernel(
    taps_ref,
    conv_in_ref,
    conv_a_ref,
    conv_d_ref,
    w_q_ref,
    w_s_ref,
    bias_ref,
    blend_ref,
    table_ref,
    out_hbm,
    out_ref,
    out_sem,
    h_ref,
    a_ref,
    d_ref,
    e_ref,
):
    bias_d = jnp.concatenate([bias_ref[32:72]] * 8, axis=0)
    bias_o = bias_ref[72:120]
    weight_y, weight_x, weight_xy, scale = [blend_ref[8 * n : 8 * n + 8] for n in range(4)]
    margins = slice(1024, 1152)

    def pair(q):
        return slice(256 * q, 256 * q + 256)

    def section(z):
        return slice(128 * z, 128 * z + 128)

    def wide(column, at):
        return column if at.stop - at.start == 128 else jnp.concatenate([column, column], axis=1)

    def first_level(at):
        h = dot(conv_in_ref[:, 0:96], taps_ref[:, at]).astype(BF16)
        h_ref[:, :, at] = jnp.maximum(h, 0).reshape(5, 256, at.stop - at.start)

    places = (0, 1, 2, 3, 4, 5, 6, 7, 8, 9, 12, 13, 10, 11)

    tiles = (
        (3, (0, 1, 2), (0,)),
        (1, (1, 2, 3, 4, 5), (1, 2, 3)),
        (0, (12, 4, 5, 6, 7, 8, 13), (4, 5, 6, 12, 13)),
        (1, (7, 8, 9, 10, 11), (7, 8, 9)),
        (1, (10, 11), (10, 11)),
    )

    def products(tile, at, sums):
        first, rows, _ = tiles[tile]
        product = dot(conv_a_ref[96 * first : 96 * (first + len(rows))], h_ref[tile, :, at])
        product = product.reshape(len(rows), 3, 32, at.stop - at.start)
        for n, row in enumerate(rows):
            part = product[n]
            sums[row] = sums[row] + part if row in sums else part
            if tile == 1 and row == 5:
                sums[12] = part

    def finish(row, at, total):
        block = (row + 1 if row < 12 else row - 6) if row != 12 else 6
        tile, nth = block // 3, block % 3
        centre = h_ref[tile, 32 * nth : 32 * nth + 32, at].astype(F32)
        a_ref[places[row], :, at] = (centre + jnp.maximum(total, 0.0)).astype(BF16)

    def pooled_rows(at):
        even = jnp.concatenate([a_ref[n, :, at] for n in (0, 2, 4, 6, 8, 12, 4, 11)], axis=0)
        late = jnp.concatenate([a_ref[n, :, at] for n in (1, 3, 5, 7, 9, 13, 10, 7)], axis=0)
        return jnp.concatenate([even, late], axis=1)

    def keep(dx, at, value):
        d_ref[:, dx, :, at] = value.astype(BF16).reshape(8, 32, 128)

    def pool(q):
        both = jnp.concatenate([pooled_rows(section(2 * q)), pooled_rows(section(2 * q + 1))], axis=0)
        return dot(both, table_ref[:, 256:512])

    def pooled(q, d, ends):
        lane = iota((32, 128), 1)
        low = lane < 64
        for block in range(8):
            rows, more = slice(32 * block, 32 * block + 32), slice(256 + 32 * block, 288 + 32 * block)
            one, two = d[rows, 0:128], pltpu.roll(d[more, 0:128], 64, 1)
            end = ends[rows]
            before = end if q == 0 else pltpu.roll(end, 128 - q, 1)
            after = end if q == 3 else pltpu.roll(end, 3 - q, 1)
            moved = pltpu.roll(jnp.where(low, two, one), 64, 1)
            for dx, value in (
                (0, jnp.where(lane % 64 == 0, before, jnp.where(low, one, two))),
                (1, jnp.where(low, d[rows, 128:256], pltpu.roll(d[more, 128:256], 64, 1))),
                (2, jnp.where(lane % 64 == 63, after, moved)),
            ):
                d_ref[block, dx, :, section(q)] = value.astype(BF16)

    def coarse(at):
        d = d_ref[:, :, :, at].reshape(768, at.stop - at.start)
        one = dot(conv_d_ref[0:208], d[0:256])
        two = dot(conv_d_ref[208:448], d[256:512])
        three = dot(conv_d_ref[448:656], d[512:768])
        return one, two, three

    def coarsened(at, parts):
        one, two, three = parts
        e = jnp.concatenate(
            [
                one[0:80] + three[0:80],
                one[80:200] + two[0:120],
                two[120:240] + three[80:200],
            ],
            axis=0,
        )
        e_ref[:, at] = jnp.maximum(e + wide(bias_d, at), 0.0).astype(BF16)

    def lift(at):
        own = dot(w_q_ref[:, 0:160], e_ref[80:240, at])
        other = dot(w_q_ref[:, 0:160], jnp.concatenate([e_ref[0:80, at], e_ref[240:320, at]], axis=0))
        return own, other

    def spread(parts, table):
        own, other = parts
        q = jnp.concatenate([own[0:24] + own[24:48], other[0:24] + other[24:48]], axis=0)
        high = q.astype(BF16).astype(F32)
        low = q - high
        rows = [
            jnp.concatenate([high[:, at : at + 128], low[:, at : at + 128]], axis=1)
            for at in range(0, q.shape[1], 128)
        ]
        return dot(jnp.concatenate(rows, axis=0).astype(BF16), table)

    def fine(at):
        s = dot(w_s_ref[:, 0:320], a_ref[2:12, :, at].reshape(320, at.stop - at.start))
        return s + wide(bias_o, at)

    def blend(q, s, beyond):
        s = jax.nn.sigmoid(s)
        for half in range(2):
            for o in range(3):
                own = s[8 * o : 8 * o + 8, 128 * half : 128 * half + 128]
                other = s[24 + 8 * o : 32 + 8 * o, 128 * half : 128 * half + 128]
                z = 2 * q + half
                out_ref[o, z] = fold(own + other * weight_y, beyond[o], z) * scale

    first_level(margins)
    first_level(pair(0))
    sums = {}
    along = iota((32, 128), 1)

    def finish_margins(tile):
        for row in tiles[tile][2]:
            before, here, after = sums[row][0], sums[row][1], sums[row][2]
            before = jnp.where(along >= 16, pltpu.roll(before, 16, 1), 0.0)
            after = jnp.where(along < 112, pltpu.roll(after, 112, 1), 0.0)
            finish(row, margins, here + before + after)

    for tile in range(5):
        products(tile, margins, sums)
        if tile > 0:
            finish_margins(tile - 1)
    first_level(pair(1))
    finish_margins(4)

    p = [{}, {}, {}, {}]

    def finish_sections(q, tile):
        for row in tiles[tile][2]:
            here = p[q][row]
            if q > 0:
                last = p[q - 1][row]
                total = last[1, :, 128:256] + last[0, :, 0:128] + here[2, :, 0:128]
                finish(row, section(2 * q - 1), total)
            total = here[1, :, 0:128] + here[2, :, 128:256]
            if q > 0:
                total = total + p[q - 1][row][0, :, 128:256]
            finish(row, section(2 * q), total)
            if q == 3:
                finish(row, section(7), here[1, :, 128:256] + here[0, :, 0:128])

    def residual(q, beside):
        for tile in range(5):
            products(tile, pair(q), p[q])
            if tile > 0:
                finish_sections(q, tile - 1)
            for task in beside[tile : tile + 1]:
                task()

    got = {}

    def margins_pool():
        got["side"] = dot(pooled_rows(margins), table_ref[:, 512:1024])

    def margins_pooled():
        for dx in range(3):
            keep(dx, slice(512, 640), got["side"][:, 128 * dx : 128 * dx + 128])
        got["ends"] = got["side"][:, 384:512]

    def margins_coarse():
        got["e"] = coarse(slice(512, 640))
        got["fine"] = fine(margins)

    def margins_coarsened():
        coarsened(slice(512, 640), got["e"])

    def margins_lift():
        got["q"] = lift(slice(512, 640))

    def margins_spread():
        got["up"] = spread(got["q"], table_ref[:, 1024:1152])

    def margins_done():
        s = jax.nn.sigmoid(got["fine"] + got["up"])
        got["beyond"] = [
            s[8 * o : 8 * o + 8] * weight_x + s[24 + 8 * o : 32 + 8 * o] * weight_xy
            for o in range(3)
        ]

    def pool_of(q):
        def task():
            got["pool", q] = pool(q)

        return task

    def pooled_of(q):
        return lambda: pooled(q, got["pool", q], got["ends"])

    def fine_of(q):
        def task():
            got["fine", q] = fine(pair(q))

        return task

    low, high = slice(0, 256), slice(256, 512)

    def low_coarse():
        got["e", 0] = coarse(low)

    def low_lift():
        coarsened(low, got["e", 0])
        got["q", 0] = lift(low)

    residual(0, [margins_pool, margins_pooled, margins_coarse, margins_coarsened, margins_lift])
    first_level(pair(2))
    finish_sections(0, 4)
    residual(1, [margins_spread, margins_done])
    first_level(pair(3))
    finish_sections(1, 4)
    residual(2, [pool_of(0), pooled_of(0), fine_of(0)])
    finish_sections(2, 4)
    residual(3, [pool_of(1), pooled_of(1), fine_of(1), low_coarse, low_lift])
    finish_sections(3, 4)
    pool_of(2)()
    pool_of(3)()
    up = spread(got["q", 0], table_ref[:, 0:256])
    got["up", 0], got["up", 1] = up[0:48], up[48:96]
    pooled_of(2)()
    got["e", 1] = coarse(section(2))
    fine_of(2)()
    pooled_of(3)()
    coarsened(section(2), got["e", 1])
    got["e", 1] = coarse(section(3))
    fine_of(3)()
    blend(0, got["fine", 0] + got["up", 0], got["beyond"])
    coarsened(section(3), got["e", 1])
    got["q", 1] = lift(high)
    blend(1, got["fine", 1] + got["up", 1], got["beyond"])
    up = spread(got["q", 1], table_ref[:, 0:256])
    got["up", 2], got["up", 3] = up[0:48], up[48:96]
    def out(n):
        part = (slice(None), slice(4 * n, 4 * n + 4))
        return pltpu.make_async_copy(out_ref.at[part], out_hbm.at[part], out_sem.at[n])

    out(0).start()
    blend(2, got["fine", 2] + got["up", 2], got["beyond"])
    blend(3, got["fine", 3] + got["up", 3], got["beyond"])
    out(1).start()
    out(0).wait()
    out(1).wait()


def network(*made, **options):
    vmem = pl.BlockSpec(memory_space=pltpu.VMEM)
    return pl.pallas_call(
        network_kernel,
        out_shape=jax.ShapeDtypeStruct((3, 8, 8, 128), F32),
        in_specs=[vmem] * 9,
        out_specs=pl.BlockSpec(memory_space=pl.ANY),
        scratch_shapes=[
            pltpu.VMEM((3, 8, 8, 128), F32),
            pltpu.SemaphoreType.DMA((2,)),
            pltpu.VMEM((5, 256, 1152), BF16),
            pltpu.VMEM((14, 32, 1152), BF16),
            pltpu.VMEM((8, 3, 32, 640), BF16),
            pltpu.VMEM((320, 640), BF16),
        ],
        compiler_params=pltpu.CompilerParams(vmem_limit_bytes=32 * 1024 * 1024),
        **options,
    )(*made)


def per_device(*arrays):
    return network(*exchange(*arrays))


def solution(mesh):
    placed = (P("gy", None, "gx"), P(), P(), P(), P(), P(), P(), P(), P(), P(), P(), P())
    return jax.shard_map(
        per_device, mesh=mesh, in_specs=placed, out_specs=P(None, None, "gx", "gy"), check_vma=False
    )
```

```python
import functools

import jax
import jax.numpy as jnp
import ml_dtypes
import numpy as np
from jax import lax
from jax.experimental import pallas as pl
from jax.experimental.pallas import tpu as pltpu
from jax.sharding import PartitionSpec as P

MESH = pl.DeviceIdType.MESH
F32 = jnp.float32
BF16 = jnp.bfloat16
BIG = -1e30


def iota(shape, dim):
    return lax.broadcasted_iota(jnp.int32, shape, dim)


def within(x, low, high):
    return (x >= low) & (x <= high)


def dot(a, b):
    return jnp.dot(a, b, preferred_element_type=F32)


def neighbours(gi):
    odd = lax.rem(gi, 2)
    column = lax.div(gi, 2)
    beside = lax.rem(column + 7 + 2 * odd, 8)
    return odd, column, beside


def unit_row(dx, block, channel):
    if dx == 1:
        return 32 * block + channel
    unit = 3 * (dx // 2) + block
    if unit < 5:
        return 96 + 28 * unit + channel
    return 236 + channel if channel < 20 else 8 + channel if channel < 24 else 36 + channel


def units_table():
    table = np.zeros((3, 3, 32, 256), np.float32)
    for block in range(3):
        for dx in range(3):
            for channel in range(28):
                table[block, dx, channel, unit_row(dx, block, channel)] = 1
    return table.reshape(288, 256).astype(ml_dtypes.bfloat16)


def level_table():
    spread = np.zeros((256, 256), np.float32)
    core = np.zeros((2, 128, 256), np.float32)
    side = np.zeros((2, 128, 512), np.float32)
    spread_side = np.zeros((2, 128, 128), np.float32)
    for lane in range(256):
        spread[lane // 2, lane] = spread[128 + lane // 2, lane] = 1
    for m in range(64):
        for fine in (0, 1):
            if m >= 1:
                core[:, 2 * m - 2 + fine, m] = 0.25
            if m <= 62:
                core[:, 2 * m + 2 + fine, 64 + m] = 0.25
            core[:, 2 * m + fine, 128 + m] = 0.25
    for section in range(8):
        for fine in (0, 1):
            for dx in range(3):
                for m in (0, 1):
                    left, right = m + dx - 1, 62 + m + dx - 1
                    if left <= 1:
                        side[:, 16 * section + 2 + 2 * left + fine, 128 * dx + 8 * section + 1 + m] = 0.25
                    if right >= 62:
                        side[:, 16 * section + 2 * right - 114 + fine, 128 * dx + 8 * section + 4 + m] = 0.25
            at = 384 + 64 * (section % 2) + section // 2
            side[:, 16 * section + fine, at] = 0.25
            side[:, 16 * section + 14 + fine, at + 60] = 0.25
        for x in range(4):
            spread_side[:, 8 * section + 1 + x // 2, 16 * section + 2 + x] = 1
            spread_side[:, 8 * section + 4 + x // 2, 16 * section + 10 + x] = 1
    parts = [spread, core.reshape(256, 256), side.reshape(256, 512), spread_side.reshape(256, 128)]
    return np.concatenate(parts, axis=1).astype(ml_dtypes.bfloat16)


def as_column(row, size):
    shape = (size, row.shape[1])
    return jnp.sum(jnp.where(iota(shape, 0) == iota(shape, 1), row, 0.0), axis=1, keepdims=True)


def tiled_taps(pad_ref, first, taps):
    tiles = []
    for start in range(0, taps, 4):
        tile = None
        for q in range(min(4, taps - start)):
            part = pad_ref[first + start + q].astype(F32)
            part = part if q == 0 else pltpu.roll(part, 32 * q, 1)
            tile = part if tile is None else tile + part
        tiles.append(tile)
    return jnp.concatenate(tiles, axis=1)


def lay_out_weights(
    units_ref,
    w_in_ref,
    b_in_ref,
    w_a_ref,
    b_a_ref,
    w_d_ref,
    b_d_ref,
    w_u_ref,
    w_o_ref,
    b_o_ref,
    pad_ref,
    conv_in_ref,
    conv_a_ref,
    conv_d_ref,
    w_q_ref,
    w_s_ref,
    bias_ref,
):
    pad_ref[...] = jnp.zeros_like(pad_ref)
    pad_ref[0, 0:9, 0:28] = w_in_ref[...]
    tap = iota((32, 128), 0)
    lane = iota((32, 128), 1)
    put = (lane == 16 * (tap % 3) + tap // 3) & (tap < 9)
    base = lax.dot_general(
        pad_ref[0],
        put.astype(F32).astype(BF16),
        (((0,), (0,)), ((), ())),
        preferred_element_type=F32,
    )[0:32]
    rest = as_column(b_in_ref[...], 32)
    flagged = jnp.zeros((32, 128), F32)
    for n in range(3):
        part = rest.astype(BF16).astype(F32)
        flagged = flagged + jnp.where(lane == 80 + n, part, 0.0)
        rest = rest - part
    stack = []
    for block in range(3):
        for dx in range(3):
            row = []
            for tile in range(5):
                y = 3 * tile + block
                if y > 13:
                    row.append(jnp.zeros((32, 128), F32))
                    continue
                moved = base if dx == y == 0 else pltpu.roll(base, 16 * dx + y, 1)
                off = (lane == 83 + dx) | ((lane == 86) & (y < 3)) | ((lane == 87) & (y >= 11))
                row.append(moved + flagged + jnp.where(off, BIG, 0.0))
            stack.append(jnp.concatenate(row, axis=1))
    made = lax.dot_general(
        units_ref[...],
        jnp.concatenate(stack, axis=0).astype(BF16),
        (((0,), (0,)), ((), ())),
        preferred_element_type=F32,
    )
    ones = within(iota((256, 640), 0), 92, 94) & (iota((256, 640), 1) % 128 == 80)
    made = jnp.where(ones, 1.0, made).astype(BF16)
    for tile in range(5):
        conv_in_ref[256 * tile : 256 * tile + 256] = made[:, 128 * tile : 128 * tile + 128]

    pad_ref[0] = jnp.zeros((32, 128), BF16)
    pad_ref[0:27, 0:28, 0:28] = w_a_ref[...]
    lane = iota((32, 384), 1)
    parts = [[] for _ in range(7)]
    for dz in range(3):
        taps = tiled_taps(pad_ref, 9 * dz, 9)
        for n, shift in enumerate((-1, -2, -1, 0, 1, 2, 0)):
            moved = taps if shift == 0 else pltpu.roll(taps, 96 * shift % 384, 1)
            low, high = 96 * max(shift, 0), 96 * min(3 + shift, 3)
            if n == 0:
                high = 96
            if n == 6:
                low = 96
            parts[n].append(jnp.where((lane >= low) & (lane < high), moved, 0.0))
    taps = jnp.concatenate([part for shift in parts for part in shift], axis=0).astype(BF16)
    made = dot(taps[:, 0:288], units_ref[...])
    rest = as_column(b_a_ref[...], 32)
    lane = iota((32, 256), 1)
    bias = jnp.zeros((32, 256), F32)
    for n in range(3):
        part = rest.astype(BF16).astype(F32)
        bias = bias + jnp.where(lane == 92 + n, part, 0.0)
        rest = rest - part
    none = jnp.zeros((32, 256), F32)
    once = jnp.concatenate([none, bias, none], axis=0)
    none = jnp.concatenate([none] * 9, axis=0)
    conv_a_ref[...] = (made + jnp.concatenate([none, once, once, once, once], axis=0)).astype(BF16)

    pad_ref[0:9] = jnp.zeros((9, 32, 128), BF16)
    pad_ref[0:9, 0:28, 0:36] = w_d_ref[...]
    taps = pad_ref[0:12].astype(F32).reshape(384, 128)
    taps = jnp.where(iota((384, 128), 0) < 288, taps, 0.0)
    taps = jnp.concatenate([taps[128 * n : 128 * n + 128].T[0:40] for n in range(3)], axis=1)
    taps = jnp.concatenate([taps, jnp.zeros((40, 384), F32)], axis=1)
    lane = iota((40, 768), 1)

    def spaced(*moves):
        total = None
        for first, dy, count in moves:
            by = 96 * (first - dy) % 768
            moved = taps if by == 0 else pltpu.roll(taps, by, 1)
            moved = jnp.where(within(lane, 96 * first, 96 * (first + count) - 1), moved, 0.0)
            total = moved if total is None else total + moved
        return total

    outs = [
        spaced((0, 0, 2), (6, 2, 1)),
        spaced((1, 0, 1), (6, 1, 1)),
        spaced((0, 0, 3)),
        spaced((1, 0, 3)),
        spaced((2, 0, 3)),
        spaced((3, 0, 3)),
        spaced((4, 2, 1), (7, 1, 1)),
        spaced((4, 1, 2), (7, 0, 1)),
    ]
    none = [jnp.zeros((8, 256), F32)]
    for at, tile, which in (
        (0, 0, (0, 1, 2, 3, 4)),
        (208, 1, (2, 3, 4, 5, 6, 7)),
        (448, 2, (0, 1, 5, 6, 7)),
    ):
        part = [outs[n][:, 256 * tile : 256 * tile + 256] for n in which]
        part = jnp.concatenate(part if tile == 1 else part + none, axis=0)
        conv_d_ref[at : at + part.shape[0]] = part.astype(BF16)

    w_o = w_o_ref[...].astype(F32)
    w_o = jnp.concatenate([jnp.broadcast_to(w_o[o : o + 1], (8, 28)) for o in range(3)], axis=0)
    w_o = jnp.concatenate([w_o, jnp.zeros((24, 4), F32)], axis=1)
    pad_ref[0] = jnp.zeros((32, 128), BF16)
    pad_ref[0, 0:28, 0:36] = w_u_ref[...]
    w_u = pad_ref[0].astype(F32)
    w_u = jnp.concatenate([w_u, jnp.zeros_like(w_u)], axis=1)
    w_u = w_u + pltpu.roll(w_u, 40, 1)
    w_u = w_u + pltpu.roll(w_u, 80, 1)
    w_q = dot(w_o.astype(BF16), w_u.astype(BF16))
    lane = iota((24, 256), 1)
    w_q = jnp.where(lane // 40 == (iota((24, 256), 0) % 8) // 2, w_q, 0.0)
    high = w_q.astype(BF16).astype(F32)
    w_q_ref[...] = jnp.concatenate([high, w_q - high], axis=0).astype(BF16)
    w_o = jnp.concatenate([w_o] * 12, axis=1)
    w_o = jnp.concatenate([w_o, w_o], axis=0)
    lane = iota((48, 384), 1) // 32
    row = iota((48, 384), 0)
    block = jnp.where(row < 24, row % 8, jnp.where(within(row % 8, 3, 4), row % 8 + 5, row % 8))
    w_s_ref[...] = jnp.where(lane == block, w_o, 0.0).astype(BF16)

    bias_ref[0:32] = jnp.zeros((32, 128), F32)
    bias_ref[32:72] = jnp.broadcast_to(as_column(b_d_ref[...], 40), (40, 128))
    row = iota((48, 3), 0) % 24 // 8
    b_o = jnp.sum(jnp.where(row == iota((48, 3), 1), b_o_ref[...], 0.0), axis=1, keepdims=True)
    bias_ref[72:120] = jnp.broadcast_to(b_o, (48, 128))
    bias_ref[120:128] = jnp.zeros((8, 128), F32)


def fold(core, beyond, z):
    lane = iota((8, 128), 1)
    left = jnp.where(lane < 4, pltpu.roll(beyond, (126 - 16 * z) % 128, 1), 0.0)
    right = jnp.where(lane >= 124, pltpu.roll(beyond, (114 - 16 * z) % 128, 1), 0.0)
    return core + left + right


def blend_weights(gi, gj, margins_ref, blend_ref):
    margins = margins_ref[...].astype(F32)
    places = margins.shape

    def margin(step_y, step_x):
        y, x = gi + step_y, gj + step_x
        here = (iota(places, 0) == x) & (iota(places, 1) == y)
        value = jnp.sum(jnp.where(here, margins, 0.0), keepdims=True)
        return value, (y >= 0) & (y < 16) & (x >= 0) & (x < 8)

    def ramp(distance, pair):
        return jnp.clip(1.0 - distance / (pair[0] + 1.0), 0.0, 1.0) * jnp.where(pair[1], 1.0, 0.0)

    y = iota((8, 128), 0)
    lane = iota((8, 128), 1)
    upper = y < 4
    off_y = jnp.where(upper, y + 1, 8 - y).astype(F32)
    nth = lane % 16
    left = nth < 8
    off_x = jnp.where(
        within(nth, 2, 5), nth - 1, jnp.where(within(nth, 10, 13), 14 - nth, 99)
    ).astype(F32)
    m = {(a, b): margin(a, b) for a in (-1, 0, 1) for b in (-1, 0, 1) if (a, b) != (0, 0)}
    weight_y = jnp.where(upper, ramp(off_y, m[-1, 0]), ramp(off_y, m[1, 0]))
    weight_x = jnp.where(left, ramp(off_x, m[0, -1]), ramp(off_x, m[0, 1]))

    def corner(a, b):
        return ramp(off_y, m[a, b]) * ramp(off_x, m[a, b])

    weight_xy = jnp.where(
        upper,
        jnp.where(left, corner(-1, -1), corner(-1, 1)),
        jnp.where(left, corner(1, -1), corner(1, 1)),
    )
    blend_ref[0:8] = weight_y
    blend_ref[8:16] = weight_x
    blend_ref[16:24] = weight_xy
    blend_ref[24:32] = 1.0 / fold(1.0 + weight_y, weight_x + weight_xy, 0)


def flag_rows(gi, gj, side):
    kind = iota((16, 128), 0)
    lane = iota((16, 128), 1)
    dx = kind - 3
    if side:
        nth = lane % 16
        column = jnp.where(nth < 8, nth - 3 + dx, 113 + nth + dx)
        outside = column == jnp.where(nth < 8, 4, 123)
    else:
        column = lane + dx - 1
        outside = lane < 0
    outside = outside | ((column < 0) & (gj == 0)) | ((column > 127) & (gj == 7))
    value = (kind < 3) | (within(kind, 3, 5) & outside)
    value = value | ((kind == 6) & (gi == 0)) | ((kind == 7) & (gi == 15))
    return jnp.where(value, 1.0, 0.0).astype(BF16)


def shift_raw(slabs, got_ref, got_edge_ref, taps_ref):
    lane = iota((8, 128), 1)
    tile = iota((16, 128), 1)
    sides = [jnp.zeros((16, 128), F32) for _ in range(5)]
    for z in range(8):
        slab = slabs[z]
        near, far = [got_ref[n, slab].astype(F32) for n in range(2)]
        before, after = [jnp.broadcast_to(got_edge_ref[n, slab], (8, 128)) for n in range(2)]
        core = jnp.concatenate(
            [
                jnp.where(lane < 64, near, pltpu.roll(far, 64, 1)),
                jnp.where(lane < 64, pltpu.roll(near, 64, 1), far),
            ],
            axis=0,
        )
        before = jnp.concatenate(
            [pltpu.roll(before, n, 1, stride=16, stride_axis=0) for n in (6, 2)], axis=0
        )
        after = jnp.concatenate(
            [pltpu.roll(after, n, 1, stride=16, stride_axis=0) for n in (14, 10)], axis=0
        )
        low = jnp.where(tile < 6, pltpu.roll(core, 6, 1), after)
        high = jnp.where(tile >= 122, pltpu.roll(core, 122, 1), before)
        beside = jnp.where(tile < 64, low, high)
        for n in range(5):
            s = n - 2
            moved = core if s == 0 else pltpu.roll(core, -s % 128, 1)
            if s > 0:
                moved = jnp.where(tile >= 128 - s, pltpu.roll(beside, 122 - s, 1), moved)
            if s < 0:
                moved = jnp.where(tile < -s, pltpu.roll(beside, 6 - s, 1), moved)
            taps_ref[16 * n : 16 * n + 16, 128 * z : 128 * z + 128] = moved.astype(BF16)
            moved = pltpu.roll(beside, (16 * z + 8 - s) % 128, 1)
            sides[n] = jnp.where(tile // 16 == z, moved, sides[n])
    for n in range(5):
        taps_ref[16 * n : 16 * n + 16, 1024:1152] = sides[n].astype(BF16)


def exchange_kernel(*refs):
    hbm, refs = refs[0:14], refs[14:]
    taps_ref, made, blend_ref, table_ref, refs = refs[0], refs[1:7], refs[7], refs[8], refs[9:]
    loaded, refs = refs[0:13], refs[13:]
    pad_ref, send_ref, send_edge_ref, got_ref, got_edge_ref, load_sem, send_sem, recv_sem, mate_sem = refs
    raw_ref, order_ref, margins_ref, weights = loaded[0], loaded[1], loaded[2], loaded[3:]
    gi = lax.axis_index("gx")
    gj = lax.axis_index("gy")
    odd, column, beside = neighbours(gi)
    inner = (gi > 0) & (gi < 15)
    loads = [
        pltpu.make_async_copy(source, place, load_sem.at[n])
        for n, (source, place) in enumerate(zip(hbm, loaded + (table_ref,)))
    ]
    loads[0].start()
    barrier = pltpu.get_barrier_semaphore()

    core = lax.rem(gj, 2)
    mate = (gi, gj + 1 - 2 * core)
    group = jnp.int32(1)
    for row in SOON:
        group = jnp.where(gi == row, 0, group)

    @pl.when(core == 1)
    def _():
        pl.semaphore_signal(barrier, inc=1, device_id=mate, device_id_type=MESH)

    chips = [lax.rem(lax.div(gj, 2) + n, 4) for n in (2, 1, 3, 0)]
    for chip in chips:
        for strip in (2 * gj, 2 * gj + 1):
            peer = (strip, 2 * chip + group)
            pl.semaphore_signal(barrier, inc=1, device_id=peer, device_id_type=MESH)

    @pl.when(gj > 0)
    def _():
        for chip in chips:
            peer = (2 * gj - 1, 2 * chip + group)
            pl.semaphore_signal(barrier, inc=1, device_id=peer, device_id_type=MESH)

    @pl.when(gj < 7)
    def _():
        for chip in chips:
            peer = (2 * gj + 2, 2 * chip + group)
            pl.semaphore_signal(barrier, inc=1, device_id=peer, device_id_type=MESH)

    for load in loads[1:]:
        load.start()

    lane = iota((128, 256), 1)
    wanted = iota((128, 256), 0) + jnp.where(lane < 128, -4, 4)
    rows = (wanted == lane % 128).astype(F32).astype(BF16)
    lane = iota((128, 128), 1)
    nth = lane % 16 - 8 * (1 - odd)
    cols = jnp.where(within(nth, 0, 3), nth, jnp.where(within(nth, 4, 7), nth + 60, -99)) + 60 * odd
    cols = (iota((128, 128), 0) == cols).astype(F32).astype(BF16)
    own = lane // 16 == 7 - iota((128, 128), 0) % 8
    gather = (iota((16, 128), 0) == iota((16, 128), 1) // 8).astype(F32).astype(BF16)
    loads[0].wait()
    raw = raw_ref[0].astype(F32)
    none = jnp.zeros_like(raw)
    raw = jnp.concatenate(
        [jnp.concatenate([raw, none], axis=1), jnp.concatenate([none, raw], axis=1)], axis=0
    ).astype(BF16)
    message = lax.dot_general(
        rows, raw, (((1,), (1,)), ((), ())), preferred_element_type=F32
    ).astype(BF16)
    send_ref[...] = message.reshape(16, 8, 128)
    edge = dot(gather, jnp.where(own, dot(message, cols), 0.0).astype(BF16))
    for row in range(16):
        send_edge_ref[row] = edge[row : row + 1]

    soon = jnp.where(inner, 2 * len(SOON), len(SOON))
    late = jnp.where(inner, 2 * len(LATE), len(LATE))

    @pl.when(core == 0)
    def _():
        pl.semaphore_wait(barrier, soon + 1)
        pl.semaphore_signal(mate_sem, inc=1, device_id=mate, device_id_type=MESH)

    @pl.when(core == 1)
    def _():
        pl.semaphore_wait(mate_sem, 1)

    def send(row):
        for kind, source, target, place, wanted in (
            (0, send_ref.at[row], got_ref.at[odd, gj], column, True),
            (1, send_edge_ref.at[row], got_edge_ref.at[1 - odd, gj], beside, inner),
        ):
            here = (gi == row) & (gj == place)

            @pl.when(jnp.logical_not(here) & wanted)
            def _():
                pltpu.make_async_remote_copy(
                    src_ref=source,
                    dst_ref=target,
                    send_sem=send_sem.at[kind],
                    recv_sem=recv_sem.at[kind],
                    device_id=(row, place),
                    device_id_type=MESH,
                ).start()

    for row in SOON:
        send(row)

    @pl.when(gj == column)
    def _():
        pltpu.make_async_copy(send_ref.at[gi], got_ref.at[odd, gj], recv_sem.at[0]).start()

    @pl.when(inner & (gj == beside))
    def _():
        pltpu.make_async_copy(
            send_edge_ref.at[gi], got_edge_ref.at[1 - odd, gj], recv_sem.at[1]
        ).start()

    for load in loads[1:]:
        load.wait()
    lay_out_weights(*weights, pad_ref, *made)
    blend_weights(gi, gj, margins_ref, blend_ref)
    flags = flag_rows(gi, gj, False)
    for z in range(8):
        taps_ref[80:96, 128 * z : 128 * z + 128] = flags
    taps_ref[80:96, 1024:1152] = flag_rows(gi, gj, True)

    @pl.when(core == 0)
    def _():
        pl.semaphore_wait(mate_sem, 1)

    @pl.when(core == 1)
    def _():
        pl.semaphore_wait(barrier, late)
        pl.semaphore_signal(mate_sem, inc=1, device_id=mate, device_id_type=MESH)

    for row in LATE:
        send(row)

    slabs = []
    for z in range(8):
        slab = jnp.int32(0)
        for k in range(8):
            slab = jnp.maximum(slab, jnp.where(order_ref[k] == z, k, 0))
        slabs.append(slab)

    def got(ref, kind):
        pltpu.make_async_copy(ref, ref, recv_sem.at[kind]).wait()

    got(got_ref, 0)

    @pl.when(within(gj, 1, 6))
    def _():
        got(got_edge_ref, 1)

    @pl.when(gj == 0)
    def _():
        got(got_edge_ref.at[1], 1)
        got_edge_ref[0] = jnp.zeros((8, 1, 128), F32)

    @pl.when(gj == 7)
    def _():
        got(got_edge_ref.at[0], 1)
        got_edge_ref[1] = jnp.zeros((8, 1, 128), F32)

    shift_raw(slabs, got_ref, got_edge_ref, taps_ref)

    def sent(ref, count):
        kind = 0 if ref is send_ref else 1
        ref = ref.at[0:count]
        pltpu.make_async_copy(ref, ref, send_sem.at[kind]).wait()

    @pl.when(gj == column)
    def _():
        sent(send_ref, 15)

    @pl.when(gj != column)
    def _():
        sent(send_ref, 16)

    @pl.when(inner & (gj == beside))
    def _():
        sent(send_edge_ref, 15)

    @pl.when(inner & (gj != beside))
    def _():
        sent(send_edge_ref, 16)


ROWS = (0, 1, 4, 8, 12, 2, 3, 5, 9, 13, 6, 7, 10, 14, 11, 15)
SOON = ROWS[:5]
LATE = ROWS[5:]


TAPS = jax.ShapeDtypeStruct((96, 1152), BF16)
MADE = (
    jax.ShapeDtypeStruct((1280, 128), BF16),
    jax.ShapeDtypeStruct((672, 256), BF16),
    jax.ShapeDtypeStruct((656, 256), BF16),
    jax.ShapeDtypeStruct((48, 256), BF16),
    jax.ShapeDtypeStruct((48, 384), BF16),
    jax.ShapeDtypeStruct((128, 128), F32),
)
BLEND = jax.ShapeDtypeStruct((32, 128), F32)
TABLE = jax.ShapeDtypeStruct((256, 1152), BF16)


def as_they_lie(raw, section_order, margins, w_in, b_in, w_a, b_a, w_d, b_d, w_u, w_o, b_o):
    return (
        jnp.transpose(raw, (0, 2, 1)),
        section_order,
        margins.T,
        jnp.asarray(units_table()),
        w_in.T,
        b_in[None],
        w_a,
        b_a[None],
        jnp.transpose(w_d, (0, 2, 1)),
        b_d[None],
        w_u,
        w_o,
        b_o[None],
        jnp.asarray(level_table()),
    )


def exchange(*arrays):
    arrays = [pltpu.with_memory_space_constraint(x, pltpu.HBM) for x in as_they_lie(*arrays)]
    vmem = pl.BlockSpec(memory_space=pltpu.VMEM)
    places = [pltpu.SMEM if n == 1 else pltpu.VMEM for n in range(13)]
    return pl.pallas_call(
        exchange_kernel,
        out_shape=(TAPS,) + MADE + (BLEND, TABLE),
        in_specs=[pl.BlockSpec(memory_space=pltpu.HBM)] * 14,
        out_specs=(vmem,) * 9,
        scratch_shapes=[place(x.shape, x.dtype) for place, x in zip(places, arrays)]
        + [
            pltpu.VMEM((27, 32, 128), BF16),
            pltpu.VMEM((16, 8, 128), BF16),
            pltpu.VMEM((16, 1, 128), F32),
            pltpu.VMEM((2, 8, 8, 128), BF16),
            pltpu.VMEM((2, 8, 1, 128), F32),
            pltpu.SemaphoreType.DMA((14,)),
            pltpu.SemaphoreType.DMA((2,)),
            pltpu.SemaphoreType.DMA((2,)),
            pltpu.SemaphoreType.REGULAR,
        ],
        compiler_params=pltpu.CompilerParams(
            collective_id=0, has_side_effects=True, vmem_limit_bytes=12 * 1024 * 1024
        ),
    )(*arrays)


def network_kernel(
    taps_ref,
    conv_in_ref,
    conv_a_ref,
    conv_d_ref,
    w_q_ref,
    w_s_ref,
    bias_ref,
    blend_ref,
    table_ref,
    out_hbm,
    out_ref,
    out_sem,
    h_ref,
    a_ref,
    d_ref,
    e_ref,
):
    bias_d = jnp.concatenate([bias_ref[32:72]] * 8, axis=0)
    bias_o = bias_ref[72:120]
    weight_y, weight_x, weight_xy, scale = [blend_ref[8 * n : 8 * n + 8] for n in range(4)]
    margins = slice(1024, 1152)

    def pair(q):
        return slice(256 * q, 256 * q + 256)

    def section(z):
        return slice(128 * z, 128 * z + 128)

    def wide(column, at):
        return column if at.stop - at.start == 128 else jnp.concatenate([column, column], axis=1)

    def first_level(at):
        h = dot(conv_in_ref[:, 0:96], taps_ref[:, at]).astype(BF16)
        h_ref[:, :, at] = jnp.maximum(h, 0).reshape(5, 256, at.stop - at.start)

    places = (0, 1, 2, 3, 4, 5, 6, 7, 8, 9, 12, 13, 10, 11)

    tiles = (
        (3, (0, 1, 2), (0,)),
        (1, (1, 2, 3, 4, 5), (1, 2, 3)),
        (0, (12, 4, 5, 6, 7, 8, 13), (4, 5, 6, 12, 13)),
        (1, (7, 8, 9, 10, 11), (7, 8, 9)),
        (1, (10, 11), (10, 11)),
    )

    def products(tile, at, sums):
        first, rows, _ = tiles[tile]
        product = dot(conv_a_ref[96 * first : 96 * (first + len(rows))], h_ref[tile, :, at])
        product = product.reshape(len(rows), 3, 32, at.stop - at.start)
        for n, row in enumerate(rows):
            part = product[n]
            sums[row] = sums[row] + part if row in sums else part
            if tile == 1 and row == 5:
                sums[12] = part

    def finish(row, at, total):
        block = (row + 1 if row < 12 else row - 6) if row != 12 else 6
        tile, nth = block // 3, block % 3
        centre = h_ref[tile, 32 * nth : 32 * nth + 32, at].astype(F32)
        a_ref[places[row], :, at] = (centre + jnp.maximum(total, 0.0)).astype(BF16)

    def pooled_rows(at):
        even = jnp.concatenate([a_ref[n, :, at] for n in (0, 2, 4, 6, 8, 12, 4, 11)], axis=0)
        late = jnp.concatenate([a_ref[n, :, at] for n in (1, 3, 5, 7, 9, 13, 10, 7)], axis=0)
        return jnp.concatenate([even, late], axis=1)

    def keep(dx, at, value):
        d_ref[:, dx, :, at] = value.astype(BF16).reshape(8, 32, 128)

    def pool(q):
        both = jnp.concatenate([pooled_rows(section(2 * q)), pooled_rows(section(2 * q + 1))], axis=0)
        return dot(both, table_ref[:, 256:512])

    def pooled(q, d, ends):
        lane = iota((32, 128), 1)
        low = lane < 64
        for block in range(8):
            rows, more = slice(32 * block, 32 * block + 32), slice(256 + 32 * block, 288 + 32 * block)
            one, two = d[rows, 0:128], pltpu.roll(d[more, 0:128], 64, 1)
            end = ends[rows]
            before = end if q == 0 else pltpu.roll(end, 128 - q, 1)
            after = end if q == 3 else pltpu.roll(end, 3 - q, 1)
            moved = pltpu.roll(jnp.where(low, two, one), 64, 1)
            for dx, value in (
                (0, jnp.where(lane % 64 == 0, before, jnp.where(low, one, two))),
                (1, jnp.where(low, d[rows, 128:256], pltpu.roll(d[more, 128:256], 64, 1))),
                (2, jnp.where(lane % 64 == 63, after, moved)),
            ):
                d_ref[block, dx, :, section(q)] = value.astype(BF16)

    def coarse(at):
        d = d_ref[:, :, :, at].reshape(768, at.stop - at.start)
        one = dot(conv_d_ref[0:208], d[0:256])
        two = dot(conv_d_ref[208:448], d[256:512])
        three = dot(conv_d_ref[448:656], d[512:768])
        return one, two, three

    def coarsened(at, parts):
        one, two, three = parts
        e = jnp.concatenate(
            [
                one[0:80] + three[0:80],
                one[80:200] + two[0:120],
                two[120:240] + three[80:200],
            ],
            axis=0,
        )
        e_ref[:, at] = jnp.maximum(e + wide(bias_d, at), 0.0).astype(BF16)

    def lift(at):
        own = dot(w_q_ref[:, 0:160], e_ref[80:240, at])
        other = dot(w_q_ref[:, 0:160], jnp.concatenate([e_ref[0:80, at], e_ref[240:320, at]], axis=0))
        return own, other

    def spread(parts, table):
        own, other = parts
        q = jnp.concatenate([own[0:24] + own[24:48], other[0:24] + other[24:48]], axis=0)
        high = q.astype(BF16).astype(F32)
        low = q - high
        rows = [
            jnp.concatenate([high[:, at : at + 128], low[:, at : at + 128]], axis=1)
            for at in range(0, q.shape[1], 128)
        ]
        return dot(jnp.concatenate(rows, axis=0).astype(BF16), table)

    def fine(at):
        s = dot(w_s_ref[:, 0:320], a_ref[2:12, :, at].reshape(320, at.stop - at.start))
        return s + wide(bias_o, at)

    def blend(q, s, beyond):
        s = jax.nn.sigmoid(s)
        for half in range(2):
            for o in range(3):
                own = s[8 * o : 8 * o + 8, 128 * half : 128 * half + 128]
                other = s[24 + 8 * o : 32 + 8 * o, 128 * half : 128 * half + 128]
                z = 2 * q + half
                out_ref[o, z] = fold(own + other * weight_y, beyond[o], z) * scale

    first_level(margins)
    first_level(pair(0))
    sums = {}
    along = iota((32, 128), 1)

    def add(row, part):
        sums[row] = sums[row] + part if row in sums else part

    def margin_products(first, count, *places):
        h = jnp.concatenate([h_ref[tile, :, margins] for tile, _, _ in places], axis=1)
        product = dot(conv_a_ref[96 * first : 96 * (first + count)], h)
        product = product.reshape(count, 3, 32, h.shape[1])
        for half, (tile, skip, rows) in enumerate(places):
            for n, row in enumerate(rows):
                part = product[skip + n, :, :, 128 * half : 128 * half + 128]
                add(row, part)
                if tile == 1 and row == 5:
                    add(12, part)

    def finish_margins(rows):
        for row in rows:
            before, here, after = sums[row][0], sums[row][1], sums[row][2]
            before = jnp.where(along >= 16, pltpu.roll(before, 16, 1), 0.0)
            after = jnp.where(along < 112, pltpu.roll(after, 112, 1), 0.0)
            finish(row, margins, here + before + after)

    margin_products(1, 5, (1, 0, tiles[1][1]), (3, 0, tiles[3][1]))
    finish_margins((3, 9))
    margin_products(0, 7, (2, 0, tiles[2][1]), (0, 3, tiles[0][1]))
    finish_margins((0, 1, 2, 4, 5, 6, 7, 8, 12, 13))
    margin_products(1, 2, (4, 0, tiles[4][1]))
    first_level(pair(1))
    finish_margins((10, 11))

    p = [{}, {}, {}, {}]

    def finish_sections(q, tile):
        for row in tiles[tile][2]:
            here = p[q][row]
            if q > 0:
                last = p[q - 1][row]
                total = last[1, :, 128:256] + last[0, :, 0:128] + here[2, :, 0:128]
                finish(row, section(2 * q - 1), total)
            total = here[1, :, 0:128] + here[2, :, 128:256]
            if q > 0:
                total = total + p[q - 1][row][0, :, 128:256]
            finish(row, section(2 * q), total)
            if q == 3:
                finish(row, section(7), here[1, :, 128:256] + here[0, :, 0:128])

    def residual(q, beside):
        for tile in range(5):
            products(tile, pair(q), p[q])
            if tile > 0:
                finish_sections(q, tile - 1)
            for task in beside[tile : tile + 1]:
                task()

    got = {}

    def margins_pool():
        got["side"] = dot(pooled_rows(margins), table_ref[:, 512:1024])

    def margins_pooled():
        for dx in range(3):
            keep(dx, slice(512, 640), got["side"][:, 128 * dx : 128 * dx + 128])
        got["ends"] = got["side"][:, 384:512]

    def margins_coarse():
        got["e"] = coarse(slice(512, 640))
        got["fine"] = fine(margins)

    def margins_coarsened():
        coarsened(slice(512, 640), got["e"])

    def margins_lift():
        got["q"] = lift(slice(512, 640))

    def margins_spread():
        got["up"] = spread(got["q"], table_ref[:, 1024:1152])

    def margins_done():
        s = jax.nn.sigmoid(got["fine"] + got["up"])
        got["beyond"] = [
            s[8 * o : 8 * o + 8] * weight_x + s[24 + 8 * o : 32 + 8 * o] * weight_xy
            for o in range(3)
        ]

    def pool_of(q):
        def task():
            got["pool", q] = pool(q)

        return task

    def pooled_of(q):
        return lambda: pooled(q, got["pool", q], got["ends"])

    def fine_of(q):
        def task():
            got["fine", q] = fine(pair(q))

        return task

    low, high = slice(0, 256), slice(256, 512)

    def low_coarse():
        got["e", 0] = coarse(low)

    def low_lift():
        coarsened(low, got["e", 0])
        got["q", 0] = lift(low)

    residual(0, [margins_pool, margins_pooled, margins_coarse, margins_coarsened, margins_lift])
    first_level(pair(2))
    finish_sections(0, 4)
    residual(1, [margins_spread, margins_done])
    first_level(pair(3))
    finish_sections(1, 4)
    residual(2, [pool_of(0), pooled_of(0), fine_of(0)])
    finish_sections(2, 4)
    residual(3, [pool_of(1), pooled_of(1), fine_of(1), low_coarse, low_lift])
    finish_sections(3, 4)
    pool_of(2)()
    pool_of(3)()
    up = spread(got["q", 0], table_ref[:, 0:256])
    got["up", 0], got["up", 1] = up[0:48], up[48:96]
    pooled_of(2)()
    got["e", 1] = coarse(section(2))
    fine_of(2)()
    pooled_of(3)()
    coarsened(section(2), got["e", 1])
    got["e", 1] = coarse(section(3))
    fine_of(3)()
    blend(0, got["fine", 0] + got["up", 0], got["beyond"])
    coarsened(section(3), got["e", 1])
    got["q", 1] = lift(high)
    blend(1, got["fine", 1] + got["up", 1], got["beyond"])
    up = spread(got["q", 1], table_ref[:, 0:256])
    got["up", 2], got["up", 3] = up[0:48], up[48:96]
    def out(n):
        part = (slice(None), slice(4 * n, 4 * n + 4))
        return pltpu.make_async_copy(out_ref.at[part], out_hbm.at[part], out_sem.at[n])

    out(0).start()
    blend(2, got["fine", 2] + got["up", 2], got["beyond"])
    blend(3, got["fine", 3] + got["up", 3], got["beyond"])
    out(1).start()
    out(0).wait()
    out(1).wait()


def network(*made, **options):
    vmem = pl.BlockSpec(memory_space=pltpu.VMEM)
    return pl.pallas_call(
        network_kernel,
        out_shape=jax.ShapeDtypeStruct((3, 8, 8, 128), F32),
        in_specs=[vmem] * 9,
        out_specs=pl.BlockSpec(memory_space=pl.ANY),
        scratch_shapes=[
            pltpu.VMEM((3, 8, 8, 128), F32),
            pltpu.SemaphoreType.DMA((2,)),
            pltpu.VMEM((5, 256, 1152), BF16),
            pltpu.VMEM((14, 32, 1152), BF16),
            pltpu.VMEM((8, 3, 32, 640), BF16),
            pltpu.VMEM((320, 640), BF16),
        ],
        compiler_params=pltpu.CompilerParams(vmem_limit_bytes=32 * 1024 * 1024),
        **options,
    )(*made)


def per_device(*arrays):
    return network(*exchange(*arrays))


def solution(mesh):
    placed = (P("gy", None, "gx"), P(), P(), P(), P(), P(), P(), P(), P(), P(), P(), P())
    return jax.shard_map(
        per_device, mesh=mesh, in_specs=placed, out_specs=P(None, None, "gx", "gy"), check_vma=False
    )
```
